32 devices in a mesh: dp: 8 (over z, core), seq: 4 (over y, x).
Axes of the slice: x: 2, y: 2, z: 4, core: 2. Of those that a mesh axis runs over, the one named last changes fastest.
Arguments:
- latents: bfloat16 [2, 16, 1024, 1152], P(None, 'dp', 'seq'), may hold values from -6 to 6
- condition: bfloat16 [2, 16, 1152], P(None, 'dp'), may hold values from -6 to 6
- cotangent: bfloat16 [2, 16, 1024, 1152], P(None, 'dp', 'seq'), may hold values from -6 to 6
- modulate_weight: bfloat16 [1152, 6912], P(('dp', 'seq')), may hold values from -0.1875 to 0.1875
- modulate_bias: bfloat16 [6912], P(('dp', 'seq')), may hold values from -1.796875 to 1.796875
- triple_weight: bfloat16 [1152, 3456], P(('dp', 'seq')), may hold values from -0.1875 to 0.1875
- triple_bias: bfloat16 [2304], P(('dp', 'seq')), may hold values from -1.796875 to 1.796875
- output_weight: bfloat16 [1152, 1152], P(('dp', 'seq')), may hold values from -3 to 3
- output_bias: bfloat16 [1152], P(('dp', 'seq')), may hold values from -1.796875 to 1.796875
- expand_weight: bfloat16 [1152, 4608], P(('dp', 'seq')), may hold values from -0.1875 to 0.1875
- expand_bias: bfloat16 [4608], P(('dp', 'seq')), may hold values from -3 to 3
- shrink_weight: bfloat16 [4608, 1152], P(('dp', 'seq')), may hold values from -0.09375 to 0.09375
- shrink_bias: bfloat16 [1152], P(('dp', 'seq')), may hold values from -1.796875 to 1.796875
Outputs:
- output: bfloat16 [2, 16, 1024, 1152], P(None, 'dp', 'seq')
- latents_gradient: float32 [2, 16, 1024, 1152], P(None, 'dp', 'seq')
- condition_gradient: float32 [2, 16, 1152], P(None, 'dp')
- modulate_weight_gradient: float32 [1152, 6912], P(('dp', 'seq'))
- modulate_bias_gradient: float32 [6912], P(('dp', 'seq'))
- triple_weight_gradient: float32 [1152, 3456], P(('dp', 'seq'))
- triple_bias_gradient: float32 [2304], P(('dp', 'seq'))
- output_weight_gradient: float32 [1152, 1152], P(('dp', 'seq'))
- output_bias_gradient: float32 [1152], P(('dp', 'seq'))
- expand_weight_gradient: float32 [1152, 4608], P(('dp', 'seq'))
- expand_bias_gradient: float32 [4608], P(('dp', 'seq'))
- shrink_weight_gradient: float32 [4608, 1152], P(('dp', 'seq'))
- shrink_bias_gradient: float32 [1152], P(('dp', 'seq'))
The draws below stay inside these ranges and needn't reach their ends.
All inputs are finite; a program needn't handle non-finite values.
Results may differ from the reference program's by a relative error of at most 0.013.
The reference program's roundings to bfloat16 on the way count: a program that leaves them out, or rounds other values in their place, can miss the bound.
Values may be sent and summed in bfloat16 or wider, within the bound.
A program may use at most 384 MiB of HBM per device.

```python
import jax
import jax.numpy as jnp
from jax import lax

D = 1152
HEADS = 16
HD = 72
FF = 4608
SEQ = 1024
MB = 2
LATENTS = 16


def block_scale(key, extent, cuts, low, largest):
    def one(position, shards_of):
        steps = jax.random.uniform(jax.random.fold_in(jax.random.fold_in(key, 6), position), (shards_of,), jnp.float32, low / len(cuts), largest / len(cuts))
        return jnp.repeat(jnp.exp(steps), extent[position] // shards_of).reshape((-1,) + (1,) * (len(extent) - position - 1))

    gain = one(*cuts[0])
    for cut in cuts[1:]:
        gain = gain * one(*cut)
    return gain


def noise(stream_key, shape, scale, bound, cuts=(), kind=jnp.bfloat16):
    level = block_scale(stream_key, shape, cuts, -0.22, 0.18) if cuts else 1.0
    values = jax.random.normal(stream_key, shape, jnp.float32) * scale * level
    return jnp.minimum(jnp.maximum(values, -bound), bound).astype(kind)


def setup_inputs(seed: int = 0) -> dict:
    key_of = jax.random.split(jax.random.key(seed), 14)
    latents = noise(key_of[0], (MB, LATENTS, SEQ, D), 1.0, 6.0, ((1, 8), (2, 4)))
    condition = noise(key_of[1], (MB, LATENTS, D), 1.0, 6.0, ((1, 8),))
    cotangent = noise(key_of[2], (MB, LATENTS, SEQ, D), 1.0, 6.0, ((1, 8), (2, 4)))
    modulate_weight = noise(key_of[3], (D, 6 * D), D ** -0.5, 0.1875, ((0, 32),))
    modulate_bias = noise(key_of[4], (6 * D,), 0.3, 1.796875, ((0, 32),))
    triple_weight = noise(key_of[5], (D, 3 * D), D ** -0.5, 0.1875, ((0, 32),))
    triple_bias = noise(key_of[6], (2 * D,), 0.3, 1.796875, ((0, 32),))
    output_weight = noise(key_of[7], (D, D), (max(D // 256, 1)) ** -0.5, 3.0, ((0, 32),))
    output_bias = noise(key_of[8], (D,), 0.3, 1.796875, ((0, 32),))
    expand_weight = noise(key_of[9], (D, FF), D ** -0.5, 0.1875, ((0, 32),))
    expand_bias = noise(key_of[10], (FF,), 0.5, 3.0, ((0, 32),))
    shrink_weight = noise(key_of[11], (FF, D), FF ** -0.5, 0.09375, ((0, 32),))
    shrink_bias = noise(key_of[12], (D,), 0.3, 1.796875, ((0, 32),))
    return dict(latents=latents, condition=condition, cotangent=cotangent, modulate_weight=modulate_weight, modulate_bias=modulate_bias, triple_weight=triple_weight, triple_bias=triple_bias, output_weight=output_weight, output_bias=output_bias, expand_weight=expand_weight, expand_bias=expand_bias, shrink_weight=shrink_weight, shrink_bias=shrink_bias)


@jax.custom_vjp
def low(v):
    return lax.optimization_barrier(v.astype(jnp.bfloat16)).astype(jnp.float32)

@jax.custom_vjp
def low_back(v):
    return v

def low_keep(v):
    return (low(v), None)

def low_pass(kept, grad):
    return (grad,)

def back_keep(v):
    return (v, None)

def back_low(kept, grad):
    return (low(grad),)
low.defvjp(low_keep, low_pass)
low_back.defvjp(back_keep, back_low)
EPSILON = 1e-06
GELU_COEF = 0.7978845608028654
CUBIC = 0.044715

def matmul(left, right):
    return jnp.dot(left, right, precision=lax.Precision.HIGHEST, preferred_element_type=jnp.float32)

def gelu_tanh(values):
    return 0.5 * values * (1.0 + jnp.tanh(GELU_COEF * (values + CUBIC * values * values * values)))

def normalized(values):
    centered = values - lax.optimization_barrier(jnp.mean(values, axis=-1, keepdims=True))
    variance = lax.optimization_barrier(jnp.mean(centered * centered, axis=-1, keepdims=True))
    return centered * lax.rsqrt(variance + EPSILON)

def one_head(queries, key_rows, value_rows):
    product = low_back(matmul(queries, key_rows.T))
    scores = product * HD ** (-0.5)
    row_peak = lax.optimization_barrier(jnp.max(scores, axis=-1, keepdims=True))
    exp_scores = jnp.exp(scores - row_peak)
    soft_weights = exp_scores / lax.optimization_barrier(jnp.sum(exp_scores, axis=-1, keepdims=True))
    return matmul(low(soft_weights), value_rows)

def block(latent, condition, modulate_weight, modulate_bias, triple_weight, triple_bias, output_weight, output_bias, expand_weight, expand_bias, shrink_weight, shrink_bias):
    cond_act = low(jax.nn.silu(condition))
    modulation = low_back(matmul(cond_act[None, :], modulate_weight)[0] + modulate_bias)
    shift_one, scale_one, gate_one, shift_two, scale_two, gate_two = jnp.split(modulation, 6)
    hidden_one = low(normalized(latent) * (1.0 + scale_one) + shift_one)
    full_bias = jnp.concatenate([triple_bias[:D], jnp.zeros((D,), jnp.float32), triple_bias[D:]])
    projected = matmul(hidden_one, triple_weight) + full_bias
    queries = low(low_back(projected[:, :D]))
    key_rows = low(low_back(projected[:, D:2 * D]))
    value_rows = low(low_back(projected[:, 2 * D:]))
    query_heads = queries.reshape(SEQ, HEADS, HD).transpose(1, 0, 2)
    per_head_keys = key_rows.reshape(SEQ, HEADS, HD).transpose(1, 0, 2)
    value_heads = value_rows.reshape(SEQ, HEADS, HD).transpose(1, 0, 2)
    head_fn = jax.checkpoint(one_head)
    attended = lax.map(lambda operands: head_fn(operands[0], operands[1], operands[2]), (query_heads, per_head_keys, value_heads))
    attended = attended.transpose(1, 0, 2).reshape(SEQ, D)
    mixed = low(low_back(attended))
    branch_one = low_back(matmul(mixed, output_weight) + output_bias)
    middle = latent + gate_one * branch_one
    second_hidden = low(normalized(middle) * (1.0 + scale_two) + shift_two)
    pre_act = low_back(matmul(second_hidden, expand_weight) + expand_bias)
    activated_hidden = low(gelu_tanh(pre_act))
    branch_two = low_back(matmul(activated_hidden, shrink_weight) + shrink_bias)
    return middle + gate_two * branch_two

def reference(latents, condition, cotangent, modulate_weight, modulate_bias, triple_weight, triple_bias, output_weight, output_bias, expand_weight, expand_bias, shrink_weight, shrink_bias):
    params = tuple((weight_arg.astype(jnp.float32) for weight_arg in (modulate_weight, modulate_bias, triple_weight, triple_bias, output_weight, output_bias, expand_weight, expand_bias, shrink_weight, shrink_bias)))
    flat_tokens = latents.reshape(MB * LATENTS, SEQ, D).astype(jnp.float32)
    flat_cond = condition.reshape(MB * LATENTS, D).astype(jnp.float32)
    flat_cotangent = cotangent.reshape(MB * LATENTS, SEQ, D).astype(jnp.float32)

    def advance(totals, operands):
        latent, cond_row, cotangent_row = operands
        result, pullback = jax.vjp(block, latent, cond_row, *params)
        gradients = pullback(cotangent_row)
        totals = tuple((total_term + new_term for total_term, new_term in zip(totals, gradients[2:])))
        return (totals, (result, gradients[0], gradients[1]))
    zero_totals = tuple((jnp.zeros_like(weight_arg) for weight_arg in params))
    totals, (results, token_grads, cond_grads) = lax.scan(advance, zero_totals, (flat_tokens, flat_cond, flat_cotangent))
    return (results.reshape(latents.shape).astype(jnp.bfloat16), token_grads.reshape(latents.shape), cond_grads.reshape(condition.shape), totals[0], totals[1], totals[2], totals[3], totals[4], totals[5], totals[6], totals[7], totals[8], totals[9])
```

```python
import functools

import jax
import jax.numpy as jnp
from jax import lax
from jax.experimental import pallas as pl
from jax.experimental.pallas import tpu as pltpu
from jax.sharding import PartitionSpec as P

HEADS = 16
HD = 72
LANES = 128
WINDOW = 256
QUERY_BLOCK = 256

EPSILON = 1e-06
GELU_COEF = 0.7978845608028654
CUBIC = 0.044715
LOG2E = 1.4426950408889634
AXES = ("dp", "seq")
F32 = jnp.float32
BF16 = jnp.bfloat16


def gelu_parts(values):
    square = values * values
    tangent = jnp.tanh(GELU_COEF * values * (1.0 + CUBIC * square))
    half = 0.5 * (1.0 + tangent)
    slope = half + (0.5 * GELU_COEF) * values * (1.0 - tangent * tangent) * (1.0 + 3.0 * CUBIC * square)
    return (values * half, slope)


def norm_parts(values):
    centered = values - jnp.mean(values, axis=-1, keepdims=True)
    variance = jnp.mean(centered * centered, axis=-1, keepdims=True)
    inverse = lax.rsqrt(variance + EPSILON)
    return (centered * inverse, inverse)


def norm_back(incoming, normed, inverse, scaling):
    shift_grad = jnp.sum(incoming, axis=1)
    scale_grad = jnp.sum(incoming * normed, axis=1)
    normed_grad = incoming * (1.0 + scaling)
    mean_first = jnp.mean(normed_grad, axis=-1, keepdims=True)
    mean_second = jnp.mean(normed_grad * normed, axis=-1, keepdims=True)
    return (inverse * (normed_grad - mean_first - normed * mean_second), shift_grad, scale_grad)


def dot_nt(left, right):
    return lax.dot_general(left, right, (((1,), (1,)), ((), ())), preferred_element_type=F32)


def dot_tn(left, right):
    return lax.dot_general(left, right, (((0,), (0,)), ((), ())), preferred_element_type=F32)


def dot_nn(left, right):
    return jnp.dot(left, right, preferred_element_type=F32)


def head_window(features):
    head = pl.program_id(0)
    last = features // LANES - WINDOW // LANES
    tile = jnp.minimum(head * HD // LANES, last)
    start = pl.multiple_of(tile * LANES, LANES)
    first = head * HD - start
    lane = lax.broadcasted_iota(jnp.int32, (1, WINDOW), 1)
    return start, (lane >= first) & (lane < first + HD)


def attend_forward_kernel(query_ref, key_ref, value_ref, mixed_ref, log_ref):
    features = query_ref.shape[1]
    start, inside = head_window(features)
    window = pl.ds(start, WINDOW)
    keys = jnp.where(inside, key_ref[:, window], 0)
    values = jnp.where(inside, value_ref[:, window], 0)
    factor = HD**-0.5 * LOG2E
    for block in range(query_ref.shape[0] // QUERY_BLOCK):
        rows = pl.ds(block * QUERY_BLOCK, QUERY_BLOCK)
        scores = dot_nt(keys, query_ref[rows, window])
        peak = jnp.max(scores, axis=0, keepdims=True)
        powers = jnp.exp2((scores - peak) * factor)
        total = jnp.sum(powers, axis=0, keepdims=True)
        log_ref[0, :, rows] = peak * factor + jnp.log2(total)
        weights = (powers * (1.0 / total)).astype(BF16)
        mixed = dot_tn(values, weights).T.astype(BF16)
        mixed_ref[rows, window] = jnp.where(inside, mixed, mixed_ref[rows, window])


def attend_backward_kernel(
    query_ref, key_ref, value_ref, incoming_ref, log_ref, grad_ref, key_total, value_total
):
    features = query_ref.shape[1]
    start, inside = head_window(features)
    window = pl.ds(start, WINDOW)
    keys = jnp.where(inside, key_ref[:, window], 0)
    values = jnp.where(inside, value_ref[:, window], 0)
    scale = HD**-0.5
    factor = scale * LOG2E
    for block in range(query_ref.shape[0] // QUERY_BLOCK):
        rows = pl.ds(block * QUERY_BLOCK, QUERY_BLOCK)
        queries = query_ref[rows, window]
        incoming = incoming_ref[rows, window]
        probs = jnp.exp2(dot_nt(keys, queries) * factor - log_ref[0, :, rows])
        prob_grad = dot_nt(values, incoming)
        centre = jnp.sum(probs * prob_grad, axis=0, keepdims=True)
        score_grad = (probs * (prob_grad - centre) * scale).astype(BF16)
        key_part = dot_nn(score_grad, queries)
        value_part = dot_nn(probs.astype(BF16), incoming)
        if block == 0:
            key_total[...] = key_part
            value_total[...] = value_part
        else:
            key_total[...] += key_part
            value_total[...] += value_part
        query_grad = dot_tn(keys, score_grad).T.astype(grad_ref.dtype)
        grad_ref[rows, window] = jnp.where(inside, query_grad, grad_ref[rows, window])
    for part, total in ((1, key_total), (2, value_total)):
        place = pl.ds(pl.multiple_of(start + part * features, LANES), WINDOW)
        grad_ref[:, place] = jnp.where(inside, total[...].astype(grad_ref.dtype), grad_ref[:, place])


def whole_block(shape, column):
    return pl.BlockSpec(shape, lambda head: (0, column), pipeline_mode=pl.Buffered(1))


def attend_forward(projected, everyone):
    rows = projected.shape[0]
    features = projected.shape[1] // 3
    tokens = everyone.shape[0]
    return pl.pallas_call(
        attend_forward_kernel,
        grid=(HEADS,),
        in_specs=[
            whole_block((rows, features), 0),
            whole_block((tokens, features), 1),
            whole_block((tokens, features), 2),
        ],
        out_specs=[
            whole_block((rows, features), 0),
            pl.BlockSpec((1, 1, rows), lambda head: (head, 0, 0)),
        ],
        out_shape=[
            jax.ShapeDtypeStruct((rows, features), BF16),
            jax.ShapeDtypeStruct((HEADS, 1, rows), F32),
        ],
        compiler_params=pltpu.CompilerParams(vmem_limit_bytes=56 * 1024 * 1024),
        cost_estimate=pl.CostEstimate(
            flops=4 * rows * tokens * HEADS * WINDOW,
            bytes_accessed=2 * (rows * 2 + tokens * 2) * features,
            transcendentals=rows * tokens * HEADS,
        ),
    )(projected, everyone, everyone)


def attend_backward(projected, everyone, incoming, log_total):
    rows = projected.shape[0]
    features = projected.shape[1] // 3
    tokens = everyone.shape[0]
    kind = BF16 if rows == tokens else F32
    return pl.pallas_call(
        attend_backward_kernel,
        grid=(HEADS,),
        in_specs=[
            whole_block((rows, features), 0),
            whole_block((tokens, features), 1),
            whole_block((tokens, features), 2),
            whole_block((rows, features), 0),
            pl.BlockSpec((1, 1, rows), lambda head: (head, 0, 0)),
        ],
        out_specs=whole_block((tokens, 3 * features), 0),
        out_shape=jax.ShapeDtypeStruct((tokens, 3 * features), kind),
        scratch_shapes=[pltpu.VMEM((tokens, WINDOW), F32), pltpu.VMEM((tokens, WINDOW), F32)],
        compiler_params=pltpu.CompilerParams(vmem_limit_bytes=56 * 1024 * 1024),
        cost_estimate=pl.CostEstimate(
            flops=10 * rows * tokens * HEADS * WINDOW,
            bytes_accessed=2 * (rows * 2 + tokens * 5) * features,
            transcendentals=rows * tokens * HEADS,
        ),
    )(projected, everyone, everyone, incoming, log_total)


class Layout:
    def __init__(self, micro, local, tokens, seq):
        self.micro, self.local, self.tokens, self.seq = micro, local, tokens, seq
        self.latents = micro * local
        self.sharers = max(1, seq // self.latents)
        self.held = max(1, self.latents // seq)
        self.span = seq // self.sharers

    def gather(self, values):
        values = values.reshape(self.latents, self.tokens, values.shape[-1])
        if self.sharers > 1:
            values = jnp.repeat(values, self.sharers, axis=0)
        moved = lax.all_to_all(values, "seq", split_axis=0, concat_axis=1, tiled=True)
        if self.sharers > 1:
            part = lax.axis_index("seq") % self.sharers
            count = self.span * self.tokens
            moved = lax.dynamic_slice_in_dim(moved, part * count, count, axis=1)
        return moved

    def scatter(self, values):
        if self.sharers > 1:
            values = jnp.concatenate([values] * self.sharers, axis=1)
        moved = lax.all_to_all(values, "seq", split_axis=1, concat_axis=0, tiled=True)
        if self.sharers > 1:
            part = lax.axis_index("seq") // self.span
            moved = moved.reshape(self.latents, self.sharers, self.tokens, values.shape[-1])
            moved = lax.dynamic_index_in_dim(moved, part, axis=1, keepdims=False)
        return moved.reshape(self.micro, self.local, self.tokens, values.shape[-1])

    def own_group(self, values, axis):
        if self.sharers == self.seq:
            return values
        count = values.shape[axis] // self.seq * self.sharers
        return lax.dynamic_slice_in_dim(
            values, lax.axis_index("seq") // self.sharers * count, count, axis=axis
        )


def on_device(
    latents,
    condition,
    cotangent,
    modulate_weight,
    modulate_bias,
    triple_weight,
    triple_bias,
    output_weight,
    output_bias,
    expand_weight,
    expand_bias,
    shrink_weight,
    shrink_bias,
):
    micro, local, tokens, features = latents.shape
    hidden = expand_weight.shape[1]
    groups = lax.axis_size("dp")
    seq = lax.axis_size("seq")
    devices = groups * seq
    place = Layout(micro, local, tokens, seq)
    held = place.held
    me = lax.axis_index("dp") * seq + lax.axis_index("seq")

    everyone_cond = lax.all_gather(condition.reshape(micro * local, features), "dp", axis=0, tiled=True)
    bias_shard = jnp.concatenate([modulate_bias, triple_bias, output_bias, expand_bias, shrink_bias])
    biases = lax.all_gather(bias_shard, AXES, axis=0, tiled=False).astype(F32)
    cuts = []
    offset = 0
    for shard in (modulate_bias, triple_bias, output_bias, expand_bias, shrink_bias):
        cuts.append(biases[:, offset : offset + shard.shape[0]].reshape(-1))
        offset += shard.shape[0]
    modulate_offset, triple_offset, output_offset, expand_offset, shrink_offset = cuts

    latent_rows = place.gather(latents)
    first_shard = jnp.concatenate([triple_weight, output_weight], axis=1)
    first_full = lax.all_gather(first_shard, AXES, axis=0, tiled=True)
    triple_full = first_full[:, : 3 * features]
    output_full = first_full[:, 3 * features :]
    expand_full = lax.all_gather(expand_weight, AXES, axis=0, tiled=True)
    shrink_full = lax.all_gather(shrink_weight, AXES, axis=0, tiled=True)

    owned = modulate_weight.shape[0]
    cond_act = jax.nn.silu(everyone_cond.astype(F32)).astype(BF16)
    act_owned = lax.dynamic_slice_in_dim(cond_act, me * owned, owned, axis=1)
    modulation_part = dot_nn(act_owned, modulate_weight)
    if place.sharers > 1:
        modulation_part = jnp.repeat(modulation_part, place.sharers, axis=0)
    modulation_parts = lax.all_to_all(modulation_part, AXES, split_axis=0, concat_axis=0, tiled=True)
    modulation = jnp.sum(modulation_parts.reshape(devices, held, -1), axis=0) + modulate_offset
    shift_one, scale_one, gate_one, shift_two, scale_two, gate_two = jnp.split(
        modulation[:, None, :], 6, axis=-1
    )

    latent_float = latent_rows.astype(F32)
    normed_one, inverse_one = norm_parts(latent_float)
    hidden_one = (normed_one * (1.0 + scale_one) + shift_one).astype(BF16)
    rows = held * latent_rows.shape[1]

    def flat(values):
        return values.reshape(rows, values.shape[-1])

    def unflat(values):
        return values.reshape(held, rows // held, values.shape[-1])

    zero = jnp.zeros((features,), F32)
    full_bias = jnp.concatenate([triple_offset[:features], zero, triple_offset[features:]])
    projected = unflat((dot_nn(flat(hidden_one), triple_full) + full_bias).astype(BF16))
    if place.sharers > 1:
        everyone = place.own_group(lax.all_gather(projected, "seq", axis=1, tiled=True), 1)
    else:
        everyone = projected
    mixed_parts, log_parts = zip(
        *(attend_forward(projected[index], everyone[index]) for index in range(held))
    )
    mixed = jnp.stack(mixed_parts) if held > 1 else mixed_parts[0][None]
    branch_one = unflat(dot_nn(flat(mixed), output_full)) + output_offset
    middle = latent_float + gate_one * branch_one
    normed_two, inverse_two = norm_parts(middle)
    hidden_two = (normed_two * (1.0 + scale_two) + shift_two).astype(BF16)
    pre_act = dot_nn(flat(hidden_two), expand_full) + expand_offset
    activated = gelu_parts(pre_act)[0].astype(BF16)
    branch_two = unflat(dot_nn(activated, shrink_full)) + shrink_offset
    output = place.scatter((middle + gate_two * branch_two).astype(BF16))

    incoming = place.gather(cotangent).astype(F32)
    branch_two_grad = (gate_two * incoming).astype(BF16)
    gate_two_grad = jnp.sum(incoming * branch_two, axis=1)
    shrink_offset_grad = jnp.sum(branch_two_grad.astype(F32), axis=(0, 1))
    shrink_grad = dot_tn(activated, flat(branch_two_grad)).astype(BF16)
    shrink_total = lax.psum_scatter(shrink_grad, AXES, scatter_dimension=0, tiled=True).astype(F32)
    act_grad = dot_nt(flat(branch_two_grad), shrink_full)
    pre_grad = (act_grad * gelu_parts(pre_act)[1]).astype(BF16)
    expand_offset_grad = jnp.sum(pre_grad.astype(F32), axis=0)
    expand_grad = dot_tn(flat(hidden_two), pre_grad).astype(BF16)
    expand_total = scatter_rows(expand_grad, devices)
    hidden_two_grad = unflat(dot_nt(pre_grad, expand_full))
    norm_grad_two, shift_two_grad, scale_two_grad = norm_back(
        hidden_two_grad, normed_two, inverse_two, scale_two
    )
    middle_grad = incoming + norm_grad_two
    branch_one_grad = (gate_one * middle_grad).astype(BF16)
    gate_one_grad = jnp.sum(middle_grad * branch_one, axis=1)
    output_offset_grad = jnp.sum(branch_one_grad.astype(F32), axis=(0, 1))
    output_grad = dot_tn(flat(mixed), flat(branch_one_grad)).astype(BF16)
    mixed_grad = unflat(dot_nt(flat(branch_one_grad), output_full).astype(BF16))
    grads = []
    for index in range(held):
        grad = attend_backward(projected[index], everyone[index], mixed_grad[index], log_parts[index])
        if place.sharers > 1:
            key_value = grad[:, features:]
            key_value = lax.psum_scatter(
                own_slots(key_value, place), "seq", scatter_dimension=0, tiled=True
            ).astype(BF16)
            grad = jnp.concatenate([grad[: rows // held, :features].astype(BF16), key_value], axis=1)
        grads.append(grad)
    triple_rows = jnp.concatenate(grads) if held > 1 else grads[0]
    column_sums = jnp.sum(triple_rows.astype(F32), axis=0)
    triple_offset_grad = jnp.concatenate([column_sums[:features], column_sums[2 * features :]])
    triple_grad = dot_tn(flat(hidden_one), triple_rows).astype(BF16)
    first_grad = jnp.concatenate([triple_grad, output_grad], axis=1)
    first_total = scatter_rows(first_grad, devices)
    hidden_one_grad = unflat(dot_nt(triple_rows, triple_full))
    norm_grad_one, shift_one_grad, scale_one_grad = norm_back(
        hidden_one_grad, normed_one, inverse_one, scale_one
    )
    latents_gradient = place.scatter((middle_grad + norm_grad_one).astype(BF16)).astype(F32)

    modulation_grad = jnp.concatenate(
        [shift_one_grad, scale_one_grad, gate_one_grad, shift_two_grad, scale_two_grad, gate_two_grad],
        axis=-1,
    )
    if place.sharers > 1:
        parts = lax.all_gather(modulation_grad, "seq", axis=0, tiled=True)
        modulation_grad = jnp.sum(place.own_group(parts, 0), axis=0, keepdims=True)
    all_grads = lax.all_gather(modulation_grad.astype(BF16), AXES, axis=0, tiled=True)
    if place.sharers > 1:
        all_grads = all_grads[:: place.sharers]
    modulate_total = dot_tn(act_owned, all_grads)
    shard = modulate_bias.shape[0]
    modulate_offset_total = jnp.sum(
        lax.dynamic_slice_in_dim(all_grads, me * shard, shard, axis=1).astype(F32), axis=0
    )
    cond_back = dot_nt(all_grads, modulate_weight)
    everyone_back = lax.all_gather(cond_back, AXES, axis=1, tiled=True)
    group_back = lax.dynamic_slice_in_dim(
        everyone_back, lax.axis_index("dp") * micro * local, micro * local, axis=0
    ).reshape(condition.shape)
    cond_float = condition.astype(F32)
    sigmoid_cond = jax.nn.sigmoid(cond_float)
    condition_gradient = group_back * (sigmoid_cond * (1.0 + cond_float * (1.0 - sigmoid_cond)))

    bias_grads = jnp.concatenate(
        [
            values.reshape(devices, -1)
            for values in (triple_offset_grad, output_offset_grad, expand_offset_grad, shrink_offset_grad)
        ],
        axis=1,
    )
    bias_total = jnp.sum(
        lax.all_to_all(bias_grads, AXES, split_axis=0, concat_axis=0, tiled=True), axis=0
    )
    bias_cuts = []
    offset = 0
    for part in (triple_bias, output_bias, expand_bias, shrink_bias):
        bias_cuts.append(bias_total[offset : offset + part.shape[0]])
        offset += part.shape[0]
    return (
        output,
        latents_gradient,
        condition_gradient,
        modulate_total,
        modulate_offset_total,
        first_total[:, : 3 * features],
        bias_cuts[0],
        first_total[:, 3 * features :],
        bias_cuts[1],
        expand_total,
        bias_cuts[2],
        shrink_total,
        bias_cuts[3],
    )


def scatter_rows(values, devices):
    rows, columns = values.shape
    slots = values.reshape(rows * columns // 1152, 1152)
    total = lax.psum_scatter(slots, AXES, scatter_dimension=0, tiled=True)
    return total.reshape(rows // devices, columns).astype(F32)


def own_slots(values, place):
    group = lax.axis_index("seq") // place.sharers
    slots = jnp.zeros((place.seq // place.sharers,) + values.shape, values.dtype)
    slots = lax.dynamic_update_index_in_dim(slots, values, group, axis=0)
    return slots.reshape(-1, values.shape[-1])


def solution(mesh):
    tokens = P(None, "dp", "seq", None)
    conditions = P(None, "dp", None)
    weight = P(AXES, None)
    bias = P(AXES)
    parameters = (weight, bias) * 5
    return jax.shard_map(
        on_device,
        mesh=mesh,
        in_specs=(tokens, conditions, tokens) + parameters,
        out_specs=(tokens, tokens, conditions) + parameters,
        check_vma=False,
    )
```

```python
import functools

import jax
import jax.numpy as jnp
from jax import lax
from jax.experimental import pallas as pl
from jax.experimental.pallas import tpu as pltpu
from jax.sharding import PartitionSpec as P

HEADS = 16
HD = 72
LANES = 128
WINDOW = 256
QUERY_BLOCK = 256

EPSILON = 1e-06
GELU_COEF = 0.7978845608028654
CUBIC = 0.044715
LOG2E = 1.4426950408889634
AXES = ("dp", "seq")
F32 = jnp.float32
BF16 = jnp.bfloat16


def gelu_parts(values):
    square = values * values
    tangent = jnp.tanh(GELU_COEF * values * (1.0 + CUBIC * square))
    half = 0.5 * (1.0 + tangent)
    slope = half + (0.5 * GELU_COEF) * values * (1.0 - tangent * tangent) * (1.0 + 3.0 * CUBIC * square)
    return (values * half, slope)


def norm_parts(values):
    centered = values - jnp.mean(values, axis=-1, keepdims=True)
    variance = jnp.mean(centered * centered, axis=-1, keepdims=True)
    inverse = lax.rsqrt(variance + EPSILON)
    return (centered * inverse, inverse)


def norm_back(incoming, normed, inverse, scaling):
    shift_grad = jnp.sum(incoming, axis=1)
    scale_grad = jnp.sum(incoming * normed, axis=1)
    normed_grad = incoming * (1.0 + scaling)
    mean_first = jnp.mean(normed_grad, axis=-1, keepdims=True)
    mean_second = jnp.mean(normed_grad * normed, axis=-1, keepdims=True)
    return (inverse * (normed_grad - mean_first - normed * mean_second), shift_grad, scale_grad)


def dot_nt(left, right):
    return lax.dot_general(left, right, (((1,), (1,)), ((), ())), preferred_element_type=F32)


def dot_tn(left, right):
    return lax.dot_general(left, right, (((0,), (0,)), ((), ())), preferred_element_type=F32)


def dot_nn(left, right):
    return jnp.dot(left, right, preferred_element_type=F32)


def head_window(features):
    head = pl.program_id(0)
    last = features // LANES - WINDOW // LANES
    tile = jnp.minimum(head * HD // LANES, last)
    start = pl.multiple_of(tile * LANES, LANES)
    first = head * HD - start
    lane = lax.broadcasted_iota(jnp.int32, (1, WINDOW), 1)
    return start, (lane >= first) & (lane < first + HD)


def attend_forward_kernel(query_ref, key_ref, value_ref, mixed_ref, log_ref):
    features = query_ref.shape[1]
    start, inside = head_window(features)
    window = pl.ds(start, WINDOW)
    keys = jnp.where(inside, key_ref[:, window], 0)
    values = jnp.where(inside, value_ref[:, window], 0)
    factor = HD**-0.5 * LOG2E
    for block in range(query_ref.shape[0] // QUERY_BLOCK):
        rows = pl.ds(block * QUERY_BLOCK, QUERY_BLOCK)
        scores = dot_nt(keys, query_ref[rows, window])
        peak = jnp.max(scores, axis=0, keepdims=True)
        powers = jnp.exp2((scores - peak) * factor)
        total = jnp.sum(powers, axis=0, keepdims=True)
        log_ref[0, :, rows] = peak * factor + jnp.log2(total)
        weights = (powers * (1.0 / total)).astype(BF16)
        mixed = dot_tn(values, weights).T.astype(BF16)
        mixed_ref[rows, window] = jnp.where(inside, mixed, mixed_ref[rows, window])


def attend_backward_kernel(
    query_ref, key_ref, value_ref, incoming_ref, log_ref, grad_ref, key_total, value_total
):
    features = query_ref.shape[1]
    start, inside = head_window(features)
    window = pl.ds(start, WINDOW)
    keys = jnp.where(inside, key_ref[:, window], 0)
    values = jnp.where(inside, value_ref[:, window], 0)
    scale = HD**-0.5
    factor = scale * LOG2E
    for block in range(query_ref.shape[0] // QUERY_BLOCK):
        rows = pl.ds(block * QUERY_BLOCK, QUERY_BLOCK)
        queries = query_ref[rows, window]
        incoming = incoming_ref[rows, window]
        probs = jnp.exp2(dot_nt(keys, queries) * factor - log_ref[0, :, rows])
        prob_grad = dot_nt(values, incoming)
        centre = jnp.sum(probs * prob_grad, axis=0, keepdims=True)
        score_grad = (probs * (prob_grad - centre) * scale).astype(BF16)
        key_part = dot_nn(score_grad, queries)
        value_part = dot_nn(probs.astype(BF16), incoming)
        if block == 0:
            key_total[...] = key_part
            value_total[...] = value_part
        else:
            key_total[...] += key_part
            value_total[...] += value_part
        query_grad = dot_tn(keys, score_grad).T.astype(grad_ref.dtype)
        grad_ref[rows, window] = jnp.where(inside, query_grad, grad_ref[rows, window])
    for part, total in ((1, key_total), (2, value_total)):
        place = pl.ds(pl.multiple_of(start + part * features, LANES), WINDOW)
        grad_ref[:, place] = jnp.where(inside, total[...].astype(grad_ref.dtype), grad_ref[:, place])


def whole_block(shape, column):
    return pl.BlockSpec(shape, lambda head: (0, column), pipeline_mode=pl.Buffered(1))


def attend_forward(projected, everyone):
    rows = projected.shape[0]
    features = projected.shape[1] // 3
    tokens = everyone.shape[0]
    return pl.pallas_call(
        attend_forward_kernel,
        grid=(HEADS,),
        in_specs=[
            whole_block((rows, features), 0),
            whole_block((tokens, features), 1),
            whole_block((tokens, features), 2),
        ],
        out_specs=[
            whole_block((rows, features), 0),
            pl.BlockSpec((1, 1, rows), lambda head: (head, 0, 0)),
        ],
        out_shape=[
            jax.ShapeDtypeStruct((rows, features), BF16),
            jax.ShapeDtypeStruct((HEADS, 1, rows), F32),
        ],
        compiler_params=pltpu.CompilerParams(vmem_limit_bytes=56 * 1024 * 1024),
        cost_estimate=pl.CostEstimate(
            flops=4 * rows * tokens * HEADS * WINDOW,
            bytes_accessed=2 * (rows * 2 + tokens * 2) * features,
            transcendentals=rows * tokens * HEADS,
        ),
    )(projected, everyone, everyone)


def attend_backward(projected, everyone, incoming, log_total):
    rows = projected.shape[0]
    features = projected.shape[1] // 3
    tokens = everyone.shape[0]
    kind = BF16 if rows == tokens else F32
    return pl.pallas_call(
        attend_backward_kernel,
        grid=(HEADS,),
        in_specs=[
            whole_block((rows, features), 0),
            whole_block((tokens, features), 1),
            whole_block((tokens, features), 2),
            whole_block((rows, features), 0),
            pl.BlockSpec((1, 1, rows), lambda head: (head, 0, 0)),
        ],
        out_specs=whole_block((tokens, 3 * features), 0),
        out_shape=jax.ShapeDtypeStruct((tokens, 3 * features), kind),
        scratch_shapes=[pltpu.VMEM((tokens, WINDOW), F32), pltpu.VMEM((tokens, WINDOW), F32)],
        compiler_params=pltpu.CompilerParams(vmem_limit_bytes=56 * 1024 * 1024),
        cost_estimate=pl.CostEstimate(
            flops=10 * rows * tokens * HEADS * WINDOW,
            bytes_accessed=2 * (rows * 2 + tokens * 5) * features,
            transcendentals=rows * tokens * HEADS,
        ),
    )(projected, everyone, everyone, incoming, log_total)


class Layout:
    def __init__(self, micro, local, tokens, seq):
        self.micro, self.local, self.tokens, self.seq = micro, local, tokens, seq
        self.latents = micro * local
        self.sharers = max(1, seq // self.latents)
        self.held = max(1, self.latents // seq)
        self.span = seq // self.sharers

    def gather(self, values):
        values = values.reshape(self.latents, self.tokens, values.shape[-1])
        if self.sharers > 1:
            values = jnp.repeat(values, self.sharers, axis=0)
        moved = lax.all_to_all(values, "seq", split_axis=0, concat_axis=1, tiled=True)
        if self.sharers > 1:
            part = lax.axis_index("seq") % self.sharers
            count = self.span * self.tokens
            moved = lax.dynamic_slice_in_dim(moved, part * count, count, axis=1)
        return moved

    def scatter(self, values):
        if self.sharers > 1:
            values = jnp.concatenate([values] * self.sharers, axis=1)
        moved = lax.all_to_all(values, "seq", split_axis=1, concat_axis=0, tiled=True)
        if self.sharers > 1:
            part = lax.axis_index("seq") // self.span
            moved = moved.reshape(self.latents, self.sharers, self.tokens, values.shape[-1])
            moved = lax.dynamic_index_in_dim(moved, part, axis=1, keepdims=False)
        return moved.reshape(self.micro, self.local, self.tokens, values.shape[-1])

    def own_group(self, values, axis):
        if self.sharers == self.seq:
            return values
        count = values.shape[axis] // self.seq * self.sharers
        return lax.dynamic_slice_in_dim(
            values, lax.axis_index("seq") // self.sharers * count, count, axis=axis
        )


def on_device(
    latents,
    condition,
    cotangent,
    modulate_weight,
    modulate_bias,
    triple_weight,
    triple_bias,
    output_weight,
    output_bias,
    expand_weight,
    expand_bias,
    shrink_weight,
    shrink_bias,
):
    micro, local, tokens, features = latents.shape
    hidden = expand_weight.shape[1]
    groups = lax.axis_size("dp")
    seq = lax.axis_size("seq")
    devices = groups * seq
    place = Layout(micro, local, tokens, seq)
    held = place.held
    me = lax.axis_index("dp") * seq + lax.axis_index("seq")

    everyone_cond = lax.all_gather(condition.reshape(micro * local, features), "dp", axis=0, tiled=True)
    bias_shard = jnp.concatenate([modulate_bias, triple_bias, output_bias, expand_bias, shrink_bias])
    biases = lax.all_gather(bias_shard, AXES, axis=0, tiled=False).astype(F32)
    cuts = []
    offset = 0
    for shard in (modulate_bias, triple_bias, output_bias, expand_bias, shrink_bias):
        cuts.append(biases[:, offset : offset + shard.shape[0]].reshape(-1))
        offset += shard.shape[0]
    modulate_offset, triple_offset, output_offset, expand_offset, shrink_offset = cuts

    latent_rows = place.gather(latents)
    first_shard = jnp.concatenate([triple_weight, output_weight], axis=1)
    first_full = lax.all_gather(first_shard, AXES, axis=0, tiled=True)
    triple_full = first_full[:, : 3 * features]
    output_full = first_full[:, 3 * features :]
    expand_full = lax.all_gather(expand_weight, AXES, axis=0, tiled=True)
    shrink_full = lax.all_gather(shrink_weight, AXES, axis=0, tiled=True)

    owned = modulate_weight.shape[0]
    cond_act = jax.nn.silu(everyone_cond.astype(F32)).astype(BF16)
    act_owned = lax.dynamic_slice_in_dim(cond_act, me * owned, owned, axis=1)
    modulation_part = dot_nn(act_owned, modulate_weight)
    if place.sharers > 1:
        modulation_part = jnp.repeat(modulation_part, place.sharers, axis=0)
    modulation_parts = lax.all_to_all(modulation_part, AXES, split_axis=0, concat_axis=0, tiled=True)
    modulation = jnp.sum(modulation_parts.reshape(devices, held, -1), axis=0) + modulate_offset
    shift_one, scale_one, gate_one, shift_two, scale_two, gate_two = jnp.split(
        modulation[:, None, :], 6, axis=-1
    )

    latent_float = latent_rows.astype(F32)
    normed_one, inverse_one = norm_parts(latent_float)
    hidden_one = (normed_one * (1.0 + scale_one) + shift_one).astype(BF16)
    rows = held * latent_rows.shape[1]

    def flat(values):
        return values.reshape(rows, values.shape[-1])

    def unflat(values):
        return values.reshape(held, rows // held, values.shape[-1])

    zero = jnp.zeros((features,), F32)
    full_bias = jnp.concatenate([triple_offset[:features], zero, triple_offset[features:]])
    projected = unflat((dot_nn(flat(hidden_one), triple_full) + full_bias).astype(BF16))
    if place.sharers > 1:
        everyone = place.own_group(lax.all_gather(projected, "seq", axis=1, tiled=True), 1)
    else:
        everyone = projected
    mixed_parts, log_parts = zip(
        *(attend_forward(projected[index], everyone[index]) for index in range(held))
    )
    mixed = jnp.stack(mixed_parts) if held > 1 else mixed_parts[0][None]
    branch_one = unflat(dot_nn(flat(mixed), output_full)) + output_offset
    middle = latent_float + gate_one * branch_one
    normed_two, inverse_two = norm_parts(middle)
    hidden_two = (normed_two * (1.0 + scale_two) + shift_two).astype(BF16)
    pre_act = dot_nn(flat(hidden_two), expand_full) + expand_offset
    activated = gelu_parts(pre_act)[0].astype(BF16)
    branch_two = unflat(dot_nn(activated, shrink_full)) + shrink_offset
    output = place.scatter((middle + gate_two * branch_two).astype(BF16))

    incoming = place.gather(cotangent).astype(F32)
    branch_two_grad = (gate_two * incoming).astype(BF16)
    gate_two_grad = jnp.sum(incoming * branch_two, axis=1)
    shrink_offset_grad = jnp.sum(branch_two_grad.astype(F32), axis=(0, 1))
    shrink_grad = dot_tn(activated, flat(branch_two_grad)).astype(BF16)
    shrink_total = lax.psum_scatter(shrink_grad, AXES, scatter_dimension=0, tiled=True).astype(F32)
    act_grad = dot_nt(flat(branch_two_grad), shrink_full)
    pre_grad = (act_grad * gelu_parts(pre_act)[1]).astype(BF16)
    expand_offset_grad = jnp.sum(pre_grad.astype(F32), axis=0)
    expand_grad = dot_tn(flat(hidden_two), pre_grad).astype(BF16)
    expand_total = scatter_rows(expand_grad, devices)
    hidden_two_grad = unflat(dot_nt(pre_grad, expand_full))
    norm_grad_two, shift_two_grad, scale_two_grad = norm_back(
        hidden_two_grad, normed_two, inverse_two, scale_two
    )
    middle_grad = incoming + norm_grad_two
    branch_one_grad = (gate_one * middle_grad).astype(BF16)
    gate_one_grad = jnp.sum(middle_grad * branch_one, axis=1)
    output_offset_grad = jnp.sum(branch_one_grad.astype(F32), axis=(0, 1))
    output_grad = dot_tn(flat(mixed), flat(branch_one_grad)).astype(BF16)
    mixed_grad = unflat(dot_nt(flat(branch_one_grad), output_full).astype(BF16))
    grads = []
    for index in range(held):
        grad = attend_backward(projected[index], everyone[index], mixed_grad[index], log_parts[index])
        if place.sharers > 1:
            key_value = grad[:, features:]
            key_value = lax.psum_scatter(
                own_slots(key_value, place), "seq", scatter_dimension=0, tiled=True
            ).astype(BF16)
            grad = jnp.concatenate([grad[: rows // held, :features].astype(BF16), key_value], axis=1)
        grads.append(grad)
    triple_rows = jnp.concatenate(grads) if held > 1 else grads[0]
    column_sums = jnp.sum(triple_rows.astype(F32), axis=0)
    triple_offset_grad = jnp.concatenate([column_sums[:features], column_sums[2 * features :]])
    triple_grad = dot_tn(flat(hidden_one), triple_rows).astype(BF16)
    first_grad = jnp.concatenate([triple_grad, output_grad], axis=1)
    first_total = scatter_rows(first_grad, devices)
    hidden_one_grad = unflat(dot_nt(triple_rows, triple_full))
    norm_grad_one, shift_one_grad, scale_one_grad = norm_back(
        hidden_one_grad, normed_one, inverse_one, scale_one
    )
    latents_gradient = place.scatter((middle_grad + norm_grad_one).astype(BF16)).astype(F32)

    modulation_grad = jnp.concatenate(
        [shift_one_grad, scale_one_grad, gate_one_grad, shift_two_grad, scale_two_grad, gate_two_grad],
        axis=-1,
    )
    if place.sharers > 1:
        parts = lax.all_gather(modulation_grad, "seq", axis=0, tiled=True)
        modulation_grad = jnp.sum(place.own_group(parts, 0), axis=0, keepdims=True)
    all_grads = lax.all_gather(modulation_grad.astype(BF16), AXES, axis=0, tiled=True)
    if place.sharers > 1:
        all_grads = all_grads[:: place.sharers]
    modulate_total = dot_tn(act_owned, all_grads)
    shard = modulate_bias.shape[0]
    modulate_offset_total = jnp.sum(
        lax.dynamic_slice_in_dim(all_grads, me * shard, shard, axis=1).astype(F32), axis=0
    )
    cond_back = dot_nt(all_grads, modulate_weight)
    everyone_back = lax.all_gather(cond_back, AXES, axis=1, tiled=True)
    group_back = lax.dynamic_slice_in_dim(
        everyone_back, lax.axis_index("dp") * micro * local, micro * local, axis=0
    ).reshape(condition.shape)
    cond_float = condition.astype(F32)
    sigmoid_cond = jax.nn.sigmoid(cond_float)
    condition_gradient = group_back * (sigmoid_cond * (1.0 + cond_float * (1.0 - sigmoid_cond)))

    bias_grads = jnp.concatenate(
        [
            values.reshape(devices, -1)
            for values in (triple_offset_grad, output_offset_grad, expand_offset_grad, shrink_offset_grad)
        ],
        axis=1,
    )
    bias_total = jnp.sum(
        lax.all_to_all(bias_grads, AXES, split_axis=0, concat_axis=0, tiled=True), axis=0
    )
    bias_cuts = []
    offset = 0
    for part in (triple_bias, output_bias, expand_bias, shrink_bias):
        bias_cuts.append(bias_total[offset : offset + part.shape[0]])
        offset += part.shape[0]
    return (
        output,
        latents_gradient,
        condition_gradient,
        modulate_total,
        modulate_offset_total,
        first_total[:, : 3 * features],
        bias_cuts[0],
        first_total[:, 3 * features :],
        bias_cuts[1],
        expand_total,
        bias_cuts[2],
        shrink_total,
        bias_cuts[3],
    )


def scatter_rows(values, devices):
    rows, columns = values.shape
    slots = values.reshape(rows * columns // 1152, 1152)
    total = lax.psum_scatter(slots, AXES, scatter_dimension=0, tiled=True)
    return total.reshape(rows // devices, columns).astype(F32)


def own_slots(values, place):
    group = lax.axis_index("seq") // place.sharers
    slots = jnp.zeros((place.seq // place.sharers,) + values.shape, values.dtype)
    slots = lax.dynamic_update_index_in_dim(slots, values, group, axis=0)
    return slots.reshape(-1, values.shape[-1])


MESH = pl.DeviceIdType.MESH
ANY = pl.BlockSpec(memory_space=pl.ANY)
ROWS = 144


class Here:
    def __init__(self):
        dp, self.member = lax.axis_index("dp"), lax.axis_index("seq")
        self.group = dp
        self.z, self.core = dp // 2, dp % 2
        self.index = dp * 4 + self.member
        y, x = self.member // 2, self.member % 2
        self.across_x = y * 2 + (1 - x)
        self.across_y = (1 - y) * 2 + x
        self.across = (1 - y) * 2 + (1 - x)

    def at_x(self):
        return (self.group, self.across_x)

    def at_y(self):
        return (self.group, self.across_y)

    def at_core(self):
        return (self.z * 2 + (1 - self.core), self.member)

    def at_z(self, step):
        return (lax.rem(self.z + step, 4) * 2 + self.core, self.member)

    def at_member(self, step):
        return (self.group, lax.rem(self.member + step, 4))

    def at_index(self, step):
        place = lax.rem(self.index + step, 32)
        return (place // 4, lax.rem(place, 4))


def greet(partners):
    barrier = pltpu.get_barrier_semaphore()
    for partner in partners:
        pl.semaphore_signal(barrier, inc=1, device_id=partner, device_id_type=MESH)
    pl.semaphore_wait(barrier, len(partners))


def greet_all(here):
    barrier = pltpu.get_barrier_semaphore()

    def signal(step, carry):
        pl.semaphore_signal(barrier, inc=1, device_id=here.at_index(step), device_id_type=MESH)
        return carry

    lax.fori_loop(1, 32, signal, 0)
    pl.semaphore_wait(barrier, 31)


class Wires:
    def __init__(self, sent, landed):
        self.sent, self.landed = sent, landed

    def copy(self, number, source, target, partner):
        return pltpu.make_async_remote_copy(
            src_ref=source,
            dst_ref=target,
            send_sem=self.sent.at[number],
            recv_sem=self.landed.at[number],
            device_id=partner,
            device_id_type=MESH,
        )


def everyone(here, source_of, target, sent, landed):
    def copy_of(step):
        place = lax.rem(here.index + step, 32)
        return pltpu.make_async_remote_copy(
            src_ref=source_of(place),
            dst_ref=target.at[here.index],
            send_sem=sent.at[step],
            recv_sem=landed.at[step],
            device_id=here.at_index(step),
            device_id_type=MESH,
        )

    def start(step, carry):
        copy_of(step).start()
        return carry

    def wait(step, carry):
        copy_of(step).wait()
        return carry

    lax.fori_loop(1, 32, start, 0)
    return lambda: lax.fori_loop(1, 32, wait, 0)


def same_core(here, source, target, sent, landed):
    mine = here.z * 4 + here.member

    def copy_of(step):
        place = lax.rem(mine + step, 16)
        return pltpu.make_async_remote_copy(
            src_ref=source.at[place],
            dst_ref=target.at[mine],
            send_sem=sent.at[step],
            recv_sem=landed.at[step],
            device_id=(place // 4 * 2 + here.core, lax.rem(place, 4)),
            device_id_type=MESH,
        )

    def start(step, carry):
        copy_of(step).start()
        return carry

    def wait(step, carry):
        copy_of(step).wait()
        return carry

    lax.fori_loop(1, 16, start, 0)
    return lambda: lax.fori_loop(1, 16, wait, 0)


def introduce_kernel(note_ref, shard_ref, notes_ref, blocks_ref, landing, wide, note_sent, note_landed, sent, landed, local):
    here = Here()
    greet_all(here)
    wires = Wires(sent, landed)

    def columns(place):
        return shard_ref.at[:, :, pl.ds(pl.multiple_of(place * 1152, LANES), 1152)]

    quads = []
    for step in range(1, 4):
        place = lax.rem(here.member + step, 4)
        quads.append(wires.copy(step - 1, columns(place), landing.at[here.member], here.at_member(step)))
    for copy in quads:
        copy.start()
    done = everyone(here, lambda place: note_ref.at[0], notes_ref, note_sent, note_landed)
    own = pltpu.make_async_copy(columns(here.member), landing.at[here.member], local.at[0])
    own.start()
    mine = pltpu.make_async_copy(note_ref.at[0], notes_ref.at[here.index], local.at[1])
    mine.start()
    own.wait()
    for copy in quads:
        copy.wait_recv()
    for part in range(2):
        for member in range(4):
            wide[member * 36 : member * 36 + 36, :] = landing[member, part].astype(F32)[:36]
        blocks_ref[part] = wide[...].astype(BF16)
    for copy in quads:
        copy.wait_send()
    mine.wait()
    done()


def introduce(note, shard):
    return pl.pallas_call(
        introduce_kernel,
        in_specs=[ANY, ANY],
        out_specs=[ANY, pl.BlockSpec(memory_space=pltpu.VMEM)],
        out_shape=[
            jax.ShapeDtypeStruct((32,) + note.shape[1:], note.dtype),
            jax.ShapeDtypeStruct((2, ROWS, 1152), BF16),
        ],
        scratch_shapes=[
            pltpu.VMEM((4,) + shard.shape[:2] + (1152,), BF16),
            pltpu.VMEM((ROWS, 1152), F32),
            pltpu.SemaphoreType.DMA((32,)),
            pltpu.SemaphoreType.DMA((32,)),
            pltpu.SemaphoreType.DMA((3,)),
            pltpu.SemaphoreType.DMA((3,)),
            pltpu.SemaphoreType.DMA((2,)),
        ],
        compiler_params=pltpu.CompilerParams(collective_id=1, has_side_effects=True),
    )(note, shard)


ARRIVALS = (0, 1, 3, 2)


class Gather:
    COPIES = 31

    def __init__(self, here, place, own, sent, landed):
        self.here, self.place, self.own = here, place, own
        self.wires = Wires(sent, landed)

    def z_of(self, order):
        return lax.rem(self.here.z + 4 - ARRIVALS[order], 4)

    def along(self, step, block):
        here = self.here
        return self.wires.copy(step - 1, block, self.own(here.z), here.at_z(step))

    def begin(self, block):
        for step in (1, 3, 2):
            self.along(step, block).start()

    def sideways(self, kind, order):
        here = self.here
        z = self.z_of(order)
        partner = (here.at_x, here.at_y, here.at_core)[kind]()
        return self.wires.copy(
            3 + kind * 4 + order, self.own(z), self.place(here.member, z, here.core), partner
        )

    def passed(self, kind, order):
        here = self.here
        z = self.z_of(order)
        if kind == 3:
            member = here.across_x if order >= 2 else here.across_y
            partner = here.at_y() if order >= 2 else here.at_x()
        else:
            member = (here.across_x, here.across_y, here.across)[kind]
            partner = here.at_core()
        ref = self.place(member, z, here.core)
        return self.wires.copy(15 + kind * 4 + order, ref, ref, partner)

    def spread(self, order):
        for kind in range(3):
            self.sideways(kind, order).start()

    def relay(self, order):
        self.sideways(0, order).wait_recv()
        if order >= 2:
            self.passed(3, order).start()
        self.passed(0, order).start()
        self.sideways(1, order).wait_recv()
        if order < 2:
            self.passed(3, order).start()
        self.passed(1, order).start()

    def close(self, order):
        self.passed(3, order).wait_recv()
        self.passed(2, order).start()

    def end(self):
        for order in range(4):
            self.sideways(2, order).wait_recv()
            for kind in range(3):
                self.passed(kind, order).wait_recv()
        for order in range(4):
            for kind in range(3):
                self.sideways(kind, order).wait_send()
            for kind in range(4):
                self.passed(kind, order).wait_send()


def open_kernel(
    block_ref, shrink_ref, part_ref, token_ref, full_ref, expand_ref, shrinks_ref, parts_ref, tokens_ref,
    part_mine, part_half, part_sent, part_landed, sent, landed, more_sent, more_landed, local,
):
    here = Here()
    greet_all(here)
    more = Wires(more_sent, more_landed)
    half = more.copy(0, part_ref.at[1 - here.core], part_half, here.at_core())
    half.start()
    load = pltpu.make_async_copy(part_ref.at[here.core], part_mine, local.at[0])
    load.start()
    first = Gather(
        here,
        lambda member, z, core: full_ref.at[member, z, core],
        lambda z: full_ref.at[here.member, z, here.core],
        sent.at[0],
        landed.at[0],
    )
    second = Gather(here, None, lambda z: expand_ref.at[z], sent.at[1], landed.at[1])
    third = Gather(here, None, lambda z: shrinks_ref.at[z], sent.at[2], landed.at[2])
    first.begin(block_ref.at[0])
    mine = here.z * 4 + here.member
    own = [
        pltpu.make_async_copy(block_ref.at[0], first.own(here.z), local.at[1]),
        pltpu.make_async_copy(block_ref.at[1], second.own(here.z), local.at[2]),
        pltpu.make_async_copy(shrink_ref, third.own(here.z), local.at[3]),
        pltpu.make_async_copy(token_ref.at[here.member], tokens_ref.at[here.member], local.at[4]),
    ]
    for copy in own:
        copy.start()
    moved = []
    for step in range(1, 4):
        place = lax.rem(here.member + step, 4)
        moved.append(more.copy(step, token_ref.at[place], tokens_ref.at[here.member], here.at_member(step)))
    for copy in moved:
        copy.start()
    load.wait()
    half.wait()

    def add(place, carry):
        part_mine[place] += part_half[place]
        return carry

    lax.fori_loop(0, 16, add, 0)
    done = same_core(here, part_mine, parts_ref, part_sent, part_landed)
    keep = pltpu.make_async_copy(part_mine.at[mine], parts_ref.at[mine], local.at[5])
    keep.start()
    own[0].wait()
    first.spread(0)
    for order in range(1, 4):
        first.along(ARRIVALS[order], block_ref.at[0]).wait_recv()
        first.spread(order)
    second.begin(block_ref.at[1])
    third.begin(shrink_ref)
    for order in range(4):
        first.relay(order)
    for order in range(4):
        first.close(order)
    first.end()
    for step in (1, 3, 2):
        first.along(step, block_ref.at[0]).wait_send()
        second.along(step, block_ref.at[1]).wait()
        third.along(step, shrink_ref).wait()
    for copy in moved:
        copy.wait()
    for copy in own[1:]:
        copy.wait()
    keep.wait()
    done()


def open_up(blocks, shrink, parts, tokens):
    column = jax.ShapeDtypeStruct((4, ROWS, 1152), BF16)
    return pl.pallas_call(
        open_kernel,
        in_specs=[ANY] * 4,
        out_specs=[ANY] * 5,
        out_shape=[
            jax.ShapeDtypeStruct((4, 4, 2, ROWS, 1152), BF16),
            column,
            column,
            jax.ShapeDtypeStruct(parts.shape[1:], parts.dtype),
            jax.ShapeDtypeStruct(tokens.shape, tokens.dtype),
        ],
        scratch_shapes=[
            pltpu.VMEM(parts.shape[1:], F32),
            pltpu.VMEM(parts.shape[1:], F32),
            pltpu.SemaphoreType.DMA((16,)),
            pltpu.SemaphoreType.DMA((16,)),
            pltpu.SemaphoreType.DMA((3, 31)),
            pltpu.SemaphoreType.DMA((3, 31)),
            pltpu.SemaphoreType.DMA((4,)),
            pltpu.SemaphoreType.DMA((4,)),
            pltpu.SemaphoreType.DMA((6,)),
        ],
        compiler_params=pltpu.CompilerParams(collective_id=2, has_side_effects=True),
    )(blocks, shrink, parts, tokens)


def forward_gather_kernel(
    query_ref, key_ref, value_ref, expand_column, shrink_column, mixed_ref, log_ref, expand_full, shrink_full,
    sent, landed, local,
):
    head = pl.program_id(0)
    here = Here()
    second = Gather(
        here,
        lambda member, z, core: expand_full.at[member, z, core],
        lambda z: expand_column.at[z],
        sent.at[0],
        landed.at[0],
    )
    third = Gather(
        here,
        lambda member, z, core: shrink_full.at[z, core, member],
        lambda z: shrink_column.at[z],
        sent.at[1],
        landed.at[1],
    )
    own = (
        pltpu.make_async_copy(expand_column, expand_full.at[here.member, :, here.core], local.at[0]),
        pltpu.make_async_copy(shrink_column, shrink_full.at[:, here.core, here.member], local.at[1]),
    )

    @pl.when(head == 0)
    def _():
        greet((here.at_x(), here.at_y(), here.at_core()))
        for gather in (second, third):
            for order in range(4):
                gather.spread(order)
        for copy in own:
            copy.start()

    for order, turn in enumerate((6, 8, 10, 12)):

        @pl.when(head == turn)
        def _():
            second.relay(order)

    attend_forward_kernel(query_ref, key_ref, value_ref, mixed_ref, log_ref)

    @pl.when(head == HEADS - 1)
    def _():
        for order in range(4):
            third.relay(order)
        for gather in (second, third):
            for order in range(4):
                gather.close(order)
        for gather in (second, third):
            gather.end()
        for copy in own:
            copy.wait()


def attend_forward_gather(projected, expand_column, shrink_column):
    rows = projected.shape[0]
    features = projected.shape[1] // 3
    return pl.pallas_call(
        forward_gather_kernel,
        grid=(HEADS,),
        in_specs=[whole_block((rows, features), part) for part in range(3)] + [ANY] * 2,
        out_specs=[
            whole_block((rows, features), 0),
            pl.BlockSpec((1, 1, rows), lambda head: (head, 0, 0)),
            ANY,
            ANY,
        ],
        out_shape=[
            jax.ShapeDtypeStruct((rows, features), BF16),
            jax.ShapeDtypeStruct((HEADS, 1, rows), F32),
            jax.ShapeDtypeStruct((4, 4, 2, ROWS, 1152), BF16),
            jax.ShapeDtypeStruct((4, 2, 4, ROWS, 1152), BF16),
        ],
        scratch_shapes=[
            pltpu.SemaphoreType.DMA((2, 31)),
            pltpu.SemaphoreType.DMA((2, 31)),
            pltpu.SemaphoreType.DMA((2,)),
        ],
        compiler_params=pltpu.CompilerParams(
            collective_id=5, has_side_effects=True, vmem_limit_bytes=56 * 1024 * 1024
        ),
    )(projected, projected, projected, expand_column, shrink_column)


class Reduce:
    SCRATCH = (
        pltpu.VMEM((4, 4, ROWS, 1152), BF16),
        pltpu.VMEM((4, 4, ROWS, 1152), BF16),
        pltpu.VMEM((2, 2, ROWS, 1152), BF16),
        pltpu.VMEM((2, 4, ROWS, 1152), BF16),
        pltpu.VMEM((3, ROWS, 1152), BF16),
        pltpu.SemaphoreType.DMA((13,)),
        pltpu.SemaphoreType.DMA((13,)),
        pltpu.SemaphoreType.DMA((4,)),
    )

    def __init__(self, here, source, total, kept, crossed, relayed, beside, along, sent, landed, local):
        self.here, self.source, self.total, self.local = here, source, total, local
        self.kept, self.crossed, self.relayed, self.beside, self.pieces = kept, crossed, relayed, beside, along
        self.wires = Wires(sent, landed)
        self.order = (here.across, here.across_x, here.across_y, here.member)

    def load(self, turn):
        return pltpu.make_async_copy(
            self.source.at[self.order[turn], :, self.here.core], self.kept.at[turn], self.local.at[turn]
        )

    def cross(self, turn):
        here = self.here
        return self.wires.copy(
            turn, self.source.at[self.order[turn], :, 1 - here.core], self.crossed.at[turn], here.at_core()
        )

    def relay(self, way):
        partner = (self.here.at_x, self.here.at_y)[way]()
        half = pl.ds(2 - 2 * way, 2)
        return self.wires.copy(4 + way, self.kept.at[0, half], self.relayed.at[way], partner)

    def side(self, way, part):
        partner = (self.here.at_x, self.here.at_y)[way]()
        half = pl.ds(2 * part, 2)
        return self.wires.copy(
            6 + 2 * way + part, self.kept.at[1 + way, half], self.beside.at[way, half], partner
        )

    def along(self, step):
        z = lax.rem(self.here.z + step, 4)
        return self.wires.copy(9 + step, self.kept.at[3, z], self.pieces.at[step - 1], self.here.at_z(step))

    def begin(self):
        for turn in range(4):
            self.cross(turn).start()
            self.load(turn).start()

    def add_crossed(self, turn):
        self.load(turn).wait()
        self.cross(turn).wait_recv()

        def add(z, carry):
            self.kept[turn, z] = (self.kept[turn, z].astype(F32) + self.crossed[turn, z].astype(F32)).astype(BF16)
            return carry

        lax.fori_loop(0, 4, add, 0)

    def add_relayed(self, turn, way, first):
        def add(z, carry):
            self.kept[turn, first + z] = (
                self.kept[turn, first + z].astype(F32) + self.relayed[way, z].astype(F32)
            ).astype(BF16)
            return carry

        lax.fori_loop(0, 2, add, 0)

    def diagonal(self):
        self.add_crossed(0)
        self.relay(1).start()
        self.relay(0).start()

    def direct_x(self):
        self.add_crossed(1)
        self.side(0, 1).start()

    def direct_y(self):
        self.add_crossed(2)
        self.side(1, 0).start()

    def relay_x(self):
        self.relay(1).wait_recv()
        self.add_relayed(1, 1, 0)
        self.side(0, 0).start()

    def relay_y(self):
        self.relay(0).wait_recv()
        self.add_relayed(2, 0, 2)
        self.side(1, 1).start()

    def keep_own(self):
        self.add_crossed(3)

    def three(self, z):
        return (
            self.kept[3, z].astype(F32) + self.beside[0, z].astype(F32) + self.beside[1, z].astype(F32)
        )

    def along_z(self):
        here = self.here
        for way in range(2):
            for part in range(2):
                self.side(way, part).wait_recv()
        for step in (2, 1, 3):
            z = lax.rem(here.z + step, 4)
            self.kept[3, z] = self.three(z).astype(BF16)
            self.along(step).start()
        self.total[...] = self.three(here.z)

    def finish(self):
        for step in (1, 3, 2):
            self.along(step).wait_recv()
        self.total[...] += self.pieces[0].astype(F32) + self.pieces[1].astype(F32) + self.pieces[2].astype(F32)
        for turn in range(4):
            self.cross(turn).wait_send()
        for way in range(2):
            self.relay(way).wait_send()
            for part in range(2):
                self.side(way, part).wait_send()
        for step in range(1, 4):
            self.along(step).wait_send()

    def steps(self):
        return (
            self.begin,
            self.diagonal,
            self.direct_x,
            self.direct_y,
            self.keep_own,
            self.relay_x,
            self.relay_y,
            self.along_z,
            self.finish,
        )


def backward_reduce_kernel(
    query_ref, key_ref, value_ref, incoming_ref, log_ref, source_ref, grad_ref, total_ref,
    key_total, value_total, *scratch
):
    head = pl.program_id(0)
    here = Here()
    reduce = Reduce(here, source_ref, total_ref, *scratch)

    @pl.when(head == 0)
    def _():
        greet((here.at_x(), here.at_y(), here.at_core(), here.at_z(1), here.at_z(2), here.at_z(3)))

    steps = reduce.steps()
    for step, turn in zip(steps[:-1], (0, 1, 1, 2, 2, 4, 4, 10)):
        pl.when(head == turn)(step)
    attend_backward_kernel(
        query_ref, key_ref, value_ref, incoming_ref, log_ref, grad_ref, key_total, value_total
    )
    pl.when(head == HEADS - 1)(steps[-1])


def attend_backward_reduce(projected, incoming, log_total, source):
    rows = projected.shape[0]
    features = projected.shape[1] // 3
    return pl.pallas_call(
        backward_reduce_kernel,
        grid=(HEADS,),
        in_specs=[whole_block((rows, features), part) for part in (0, 1, 2, 0)]
        + [pl.BlockSpec((1, 1, rows), lambda head: (head, 0, 0)), ANY],
        out_specs=[whole_block((rows, 3 * features), 0), whole_block((ROWS, features), 0)],
        out_shape=[
            jax.ShapeDtypeStruct((rows, 3 * features), BF16),
            jax.ShapeDtypeStruct((ROWS, features), F32),
        ],
        scratch_shapes=[pltpu.VMEM((rows, WINDOW), F32), pltpu.VMEM((rows, WINDOW), F32), *Reduce.SCRATCH],
        compiler_params=pltpu.CompilerParams(
            collective_id=6, has_side_effects=True, vmem_limit_bytes=58 * 1024 * 1024
        ),
    )(projected, projected, projected, incoming, log_total, source)


def close_kernel(
    grad_ref, token_ref, row_ref, bias_ref, block_ref, share_ref, tokens_ref, rows_ref, biases_ref,
    total, pieces, row_sent, row_landed, bias_sent, bias_landed, more_sent, more_landed, more_local, *scratch
):
    here = Here()
    greet_all(here)
    reduce = Reduce(here, grad_ref, total, *scratch)
    reduce.begin()
    rows_done = everyone(here, lambda place: row_ref.at[0], rows_ref, row_sent, row_landed)
    bias_done = everyone(here, lambda place: bias_ref.at[place], biases_ref, bias_sent, bias_landed)
    wires = Wires(more_sent, more_landed)

    def move(step):
        place = lax.rem(here.member + step, 4)
        return wires.copy(step - 1, token_ref.at[place], tokens_ref.at[here.member], here.at_member(step))

    def cut(part, source):
        for member in range(4):
            pieces[part, member, :36] = source[member * 36 : member * 36 + 36, :]

    def share(part, step):
        place = lax.rem(here.member + step, 4)
        return wires.copy(
            3 * part + 2 + step, pieces.at[part, place], share_ref.at[part, here.member], here.at_member(step)
        )

    def keep(part):
        return pltpu.make_async_copy(
            pieces.at[part, here.member], share_ref.at[part, here.member], more_local.at[3 + part]
        )

    own = [
        pltpu.make_async_copy(token_ref.at[here.member], tokens_ref.at[here.member], more_local.at[0]),
        pltpu.make_async_copy(row_ref.at[0], rows_ref.at[here.index], more_local.at[1]),
        pltpu.make_async_copy(bias_ref.at[here.index], biases_ref.at[here.index], more_local.at[2]),
    ]
    for copy in own:
        copy.start()
    cut(1, block_ref)
    for step in range(1, 4):
        share(1, step).start()
    keep(1).start()
    move(2).start()
    for step in reduce.steps()[1:-1]:
        step()
    move(1).start()
    move(3).start()
    reduce.finish()
    cut(0, total)
    for step in range(1, 4):
        share(0, step).start()
    keep(0).start()
    for step in range(1, 4):
        move(step).wait()
        share(0, step).wait()
        share(1, step).wait()
    for copy in own:
        copy.wait()
    keep(0).wait()
    keep(1).wait()
    rows_done()
    bias_done()


def close_down(grad, tokens, row, bias, block):
    return pl.pallas_call(
        close_kernel,
        in_specs=[ANY] * 4 + [pl.BlockSpec(memory_space=pltpu.VMEM)],
        out_specs=[ANY] * 4,
        out_shape=[
            jax.ShapeDtypeStruct((2, 4, 40, 1152), F32),
            jax.ShapeDtypeStruct(tokens.shape, tokens.dtype),
            jax.ShapeDtypeStruct((32,) + row.shape[1:], row.dtype),
            jax.ShapeDtypeStruct(bias.shape, bias.dtype),
        ],
        scratch_shapes=[pltpu.VMEM((ROWS, 1152), F32), pltpu.VMEM((2, 4, 40, 1152), F32)]
        + [pltpu.SemaphoreType.DMA((32,))] * 4
        + [pltpu.SemaphoreType.DMA((9,))] * 2
        + [pltpu.SemaphoreType.DMA((5,))]
        + list(Reduce.SCRATCH),
        compiler_params=pltpu.CompilerParams(
            collective_id=3, has_side_effects=True, vmem_limit_bytes=48 * 1024 * 1024
        ),
    )(grad, tokens, row, bias, block)


def swap_kernel(part_ref, parts_ref, sent, landed, local):
    here = Here()
    greet_all(here)
    done = everyone(here, lambda place: part_ref.at[place // 4], parts_ref, sent, landed)
    own = pltpu.make_async_copy(part_ref.at[here.group], parts_ref.at[here.index], local.at[0])
    own.start()
    own.wait()
    done()


def swap(parts):
    return pl.pallas_call(
        swap_kernel,
        in_specs=[ANY],
        out_specs=ANY,
        out_shape=jax.ShapeDtypeStruct((32,) + parts.shape[1:], parts.dtype),
        scratch_shapes=[
            pltpu.SemaphoreType.DMA((32,)),
            pltpu.SemaphoreType.DMA((32,)),
            pltpu.SemaphoreType.DMA((1,)),
        ],
        compiler_params=pltpu.CompilerParams(collective_id=4, has_side_effects=True),
    )(parts)


def pad_lanes(values, width):
    return jnp.pad(values, ((0, 0), (0, width - values.shape[1])))


def on_device_fast(
    latents,
    condition,
    cotangent,
    modulate_weight,
    modulate_bias,
    triple_weight,
    triple_bias,
    output_weight,
    output_bias,
    expand_weight,
    expand_bias,
    shrink_weight,
    shrink_bias,
):
    micro, local, tokens, features = latents.shape
    devices = 32
    me = lax.axis_index("dp") * 4 + lax.axis_index("seq")
    hidden = expand_weight.shape[1]
    shard = jnp.stack([jnp.concatenate([triple_weight, output_weight], axis=1), expand_weight])
    shard = jnp.pad(shard, ((0, 0), (0, 12), (0, 0)))
    own_cond = lax.dynamic_index_in_dim(condition.reshape(4, features), lax.axis_index("seq"), axis=0, keepdims=False)
    biases = (modulate_bias, triple_bias, output_bias, expand_bias, shrink_bias)
    note = jnp.concatenate([own_cond, *biases]).astype(F32)
    note = jnp.pad(note, (0, 1664 - note.shape[0])).reshape(1, 1, 1664)
    notes, blocks = introduce(note, shard)
    notes = notes.reshape(32, 1664)
    cond_act = jax.nn.silu(notes[:, :features]).astype(BF16)
    cuts = []
    offset = features
    for bias in biases:
        cuts.append(notes[:, offset : offset + bias.shape[0]].reshape(-1))
        offset += bias.shape[0]
    modulate_offset, triple_offset, output_offset, expand_offset, shrink_offset = cuts
    owned = modulate_weight.shape[0]
    act_owned = lax.dynamic_slice_in_dim(cond_act, me * owned, owned, axis=1)
    parts = pad_lanes(dot_nn(act_owned, modulate_weight), 56 * LANES).reshape(4, 2, 4, 56, LANES)
    parts = jnp.swapaxes(parts, 0, 1).reshape(2, 16, 56, LANES)
    first_full, expand_column, shrink_column, parts, token_rows = open_up(
        blocks, shrink_weight, parts, latents.reshape(4, tokens, features)
    )
    first_full = first_full.reshape(4, features, features)
    modulation = jnp.sum(parts, axis=0).reshape(-1)[: 6 * features] + modulate_offset
    shift_one, scale_one, gate_one, shift_two, scale_two, gate_two = jnp.split(modulation[None, :], 6, axis=-1)

    latent_float = token_rows.reshape(4 * tokens, features).astype(F32)
    normed_one, inverse_one = norm_parts(latent_float)
    hidden_one = (normed_one * (1.0 + scale_one) + shift_one).astype(BF16)
    zero = jnp.zeros((features,), F32)
    full_bias = jnp.concatenate([triple_offset[:features], zero, triple_offset[features:]])
    triple_full = first_full[:3]
    output_full = first_full[3]
    projected = (
        jnp.concatenate([dot_nn(hidden_one, first_full[part]) for part in range(3)], axis=1) + full_bias
    ).astype(BF16)
    mixed, log_total, expand_full, shrink_full = attend_forward_gather(projected, expand_column, shrink_column)
    mixed, cotangent = lax.optimization_barrier((mixed, cotangent))
    expand_full = expand_full.reshape(4, features, features)
    shrink_full = shrink_full.reshape(hidden, features)
    branch_one = dot_nn(mixed, output_full) + output_offset
    middle = latent_float + gate_one * branch_one
    normed_two, inverse_two = norm_parts(middle)
    hidden_two = (normed_two * (1.0 + scale_two) + shift_two).astype(BF16)
    pre_act = jnp.concatenate([dot_nn(hidden_two, expand_full[part]) for part in range(4)], axis=1) + expand_offset
    activated = gelu_parts(pre_act)[0].astype(BF16)
    branch_two = dot_nn(activated, shrink_full) + shrink_offset

    def exchange(values):
        return lax.all_to_all(values.reshape(4, tokens, features), "seq", split_axis=0, concat_axis=0, tiled=True)

    output = exchange((middle + gate_two * branch_two).astype(BF16))
    incoming = exchange(cotangent).reshape(4 * tokens, features).astype(F32)
    branch_two_grad = (gate_two * incoming).astype(BF16)
    gate_two_grad = jnp.sum(incoming * branch_two, axis=0)
    shrink_offset_grad = jnp.sum(branch_two_grad.astype(F32), axis=0)
    shrink_grad = dot_tn(activated, branch_two_grad).astype(BF16)
    shrink_total = lax.psum_scatter(shrink_grad, AXES, scatter_dimension=0, tiled=True).astype(F32)
    act_grad = dot_nt(branch_two_grad, shrink_full)
    pre_grad = (act_grad * gelu_parts(pre_act)[1]).astype(BF16)
    expand_offset_grad = jnp.sum(pre_grad.astype(F32), axis=0)
    expand_grad = jnp.stack(
        [dot_tn(hidden_two, pre_grad[:, part * features : (part + 1) * features]).astype(BF16) for part in range(4)]
    ).reshape(4, 4, 2, ROWS, features)
    hidden_two_grad = sum(
        dot_nt(pre_grad[:, part * features : (part + 1) * features], expand_full[part]) for part in range(4)
    )
    norm_grad_two, shift_two_grad, scale_two_grad = norm_back(
        hidden_two_grad[None], normed_two[None], inverse_two[None], scale_two[None]
    )
    middle_grad = incoming + norm_grad_two[0]
    branch_one_grad = (gate_one * middle_grad).astype(BF16)
    gate_one_grad = jnp.sum(middle_grad * branch_one, axis=0)
    output_offset_grad = jnp.sum(branch_one_grad.astype(F32), axis=0)
    output_grad = dot_tn(mixed, branch_one_grad).astype(BF16)
    mixed_grad = dot_nt(branch_one_grad, output_full).astype(BF16)
    triple_rows, expand_block = attend_backward_reduce(projected, mixed_grad, log_total, expand_grad)
    column_sums = jnp.sum(triple_rows.astype(F32), axis=0)
    triple_offset_grad = jnp.concatenate([column_sums[:features], column_sums[2 * features :]])
    first_grad = jnp.stack(
        [dot_tn(hidden_one, triple_rows[:, part * features : (part + 1) * features]).astype(BF16) for part in range(3)]
        + [output_grad]
    ).reshape(4, 4, 2, ROWS, features)
    hidden_one_grad = sum(
        dot_nt(triple_rows[:, part * features : (part + 1) * features], first_full[part]) for part in range(3)
    )
    norm_grad_one, shift_one_grad, scale_one_grad = norm_back(
        hidden_one_grad[None], normed_one[None], inverse_one[None], scale_one[None]
    )
    token_grad = (middle_grad + norm_grad_one[0]).astype(BF16).reshape(4, tokens, features)
    modulation_grad = jnp.concatenate(
        [
            shift_one_grad[0],
            scale_one_grad[0],
            gate_one_grad,
            shift_two_grad[0],
            scale_two_grad[0],
            gate_two_grad,
        ]
    ).astype(BF16)
    row = jnp.pad(modulation_grad, (0, 8192 - 6 * features)).reshape(1, 64, LANES)
    bias_grads = jnp.concatenate(
        [
            values.reshape(devices, -1)
            for values in (triple_offset_grad, output_offset_grad, expand_offset_grad, shrink_offset_grad)
        ],
        axis=1,
    )
    bias_grads = pad_lanes(bias_grads, 1024).reshape(32, 8, LANES)
    shares, token_grad, all_grads, bias_parts = close_down(
        first_grad, token_grad, row, bias_grads, expand_block
    )
    all_grads = all_grads.reshape(32, 8192)[:, : 6 * features]
    modulate_total = dot_tn(act_owned, all_grads)
    width = modulate_bias.shape[0]
    modulate_offset_total = jnp.sum(
        lax.dynamic_slice_in_dim(all_grads, me * width, width, axis=1).astype(F32), axis=0
    )
    cond_back = dot_nt(all_grads, modulate_weight)
    cond_back = jnp.pad(cond_back.reshape(8, 4, owned), ((0, 0), (0, 4), (0, LANES - owned)))
    cond_back = swap(cond_back)[:, :4, :owned]
    cond_back = jnp.swapaxes(cond_back, 0, 1).reshape(condition.shape)
    cond_float = condition.astype(F32)
    sigmoid_cond = jax.nn.sigmoid(cond_float)
    condition_gradient = cond_back * (sigmoid_cond * (1.0 + cond_float * (1.0 - sigmoid_cond)))
    bias_total = jnp.sum(bias_parts.reshape(32, 1024), axis=0)
    bias_cuts = []
    offset = 0
    for bias in biases[1:]:
        bias_cuts.append(bias_total[offset : offset + bias.shape[0]])
        offset += bias.shape[0]
    first_share = shares[0, :, :owned]
    expand_total = jnp.swapaxes(shares[1, :, :owned], 0, 1).reshape(expand_weight.shape)
    return (
        output.reshape(latents.shape),
        token_grad.reshape(latents.shape).astype(F32),
        condition_gradient,
        modulate_total,
        modulate_offset_total,
        jnp.concatenate([first_share[0], first_share[1], first_share[2]], axis=1),
        bias_cuts[0],
        first_share[3],
        bias_cuts[1],
        expand_total,
        bias_cuts[2],
        shrink_total,
        bias_cuts[3],
    )


def solution(mesh):
    tokens = P(None, "dp", "seq", None)
    conditions = P(None, "dp", None)
    weight = P(AXES, None)
    bias = P(AXES)
    parameters = (weight, bias) * 5
    fast = mesh.shape["dp"] == 8 and mesh.shape["seq"] == 4
    return jax.shard_map(
        on_device_fast if fast else on_device,
        mesh=mesh,
        in_specs=(tokens, conditions, tokens) + parameters,
        out_specs=(tokens, tokens, conditions) + parameters,
        check_vma=False,
    )
```

```python
import functools

import jax
import jax.numpy as jnp
from jax import lax
from jax.experimental import pallas as pl
from jax.experimental.pallas import tpu as pltpu
from jax.sharding import PartitionSpec as P

HEADS = 16
HD = 72
LANES = 128
WINDOW = 256
QUERY_BLOCK = 256

EPSILON = 1e-06
GELU_COEF = 0.7978845608028654
CUBIC = 0.044715
LOG2E = 1.4426950408889634
AXES = ("dp", "seq")
F32 = jnp.float32
BF16 = jnp.bfloat16


def gelu_parts(values):
    square = values * values
    tangent = jnp.tanh(GELU_COEF * values * (1.0 + CUBIC * square))
    half = 0.5 * (1.0 + tangent)
    slope = half + (0.5 * GELU_COEF) * values * (1.0 - tangent * tangent) * (1.0 + 3.0 * CUBIC * square)
    return (values * half, slope)


def norm_parts(values):
    centered = values - jnp.mean(values, axis=-1, keepdims=True)
    variance = jnp.mean(centered * centered, axis=-1, keepdims=True)
    inverse = lax.rsqrt(variance + EPSILON)
    return (centered * inverse, inverse)


def norm_back(incoming, normed, inverse, scaling):
    shift_grad = jnp.sum(incoming, axis=1)
    scale_grad = jnp.sum(incoming * normed, axis=1)
    normed_grad = incoming * (1.0 + scaling)
    mean_first = jnp.mean(normed_grad, axis=-1, keepdims=True)
    mean_second = jnp.mean(normed_grad * normed, axis=-1, keepdims=True)
    return (inverse * (normed_grad - mean_first - normed * mean_second), shift_grad, scale_grad)


def dot_nt(left, right):
    return lax.dot_general(left, right, (((1,), (1,)), ((), ())), preferred_element_type=F32)


def dot_tn(left, right):
    return lax.dot_general(left, right, (((0,), (0,)), ((), ())), preferred_element_type=F32)


def dot_nn(left, right):
    return jnp.dot(left, right, preferred_element_type=F32)


def head_window(features):
    head = pl.program_id(0)
    last = features // LANES - WINDOW // LANES
    tile = jnp.minimum(head * HD // LANES, last)
    start = pl.multiple_of(tile * LANES, LANES)
    first = head * HD - start
    lane = lax.broadcasted_iota(jnp.int32, (1, WINDOW), 1)
    return start, (lane >= first) & (lane < first + HD)


def attend_forward_kernel(query_ref, key_ref, value_ref, mixed_ref, log_ref):
    features = query_ref.shape[1]
    start, inside = head_window(features)
    window = pl.ds(start, WINDOW)
    keys = jnp.where(inside, key_ref[:, window], 0)
    values = jnp.where(inside, value_ref[:, window], 0)
    factor = HD**-0.5 * LOG2E
    for block in range(query_ref.shape[0] // QUERY_BLOCK):
        rows = pl.ds(block * QUERY_BLOCK, QUERY_BLOCK)
        scores = dot_nt(keys, query_ref[rows, window])
        peak = jnp.max(scores, axis=0, keepdims=True)
        powers = jnp.exp2((scores - peak) * factor)
        total = jnp.sum(powers, axis=0, keepdims=True)
        log_ref[0, :, rows] = peak * factor + jnp.log2(total)
        weights = (powers * (1.0 / total)).astype(BF16)
        mixed = dot_tn(values, weights).T.astype(BF16)
        mixed_ref[rows, window] = jnp.where(inside, mixed, mixed_ref[rows, window])


def attend_backward_kernel(
    query_ref, key_ref, value_ref, incoming_ref, log_ref, grad_ref, score_grads, weights
):
    features = query_ref.shape[1]
    start, inside = head_window(features)
    window = pl.ds(start, WINDOW)
    keys = jnp.where(inside, key_ref[:, window], 0)
    values = jnp.where(inside, value_ref[:, window], 0)
    scale = HD**-0.5
    factor = scale * LOG2E
    count = query_ref.shape[0] // QUERY_BLOCK
    turned = keys.T

    def begin(block):
        rows = pl.ds(block * QUERY_BLOCK, QUERY_BLOCK)
        return dot_nt(keys, query_ref[rows, window]), dot_nt(values, incoming_ref[rows, window])

    following = begin(0)
    for block in range(count):
        rows = pl.ds(block * QUERY_BLOCK, QUERY_BLOCK)
        scores, prob_grad = following
        if block + 1 < count:
            following = begin(block + 1)
        probs = jnp.exp2(scores * factor - log_ref[0, :, rows])
        centre = jnp.sum(probs * prob_grad, axis=0, keepdims=True)
        score_grads[:, rows] = (probs * (prob_grad - centre) * scale).astype(BF16)
        weights[:, rows] = probs.astype(BF16)
        query_grad = dot_nn(turned, score_grads[:, rows]).T.astype(grad_ref.dtype)
        grad_ref[rows, window] = jnp.where(inside, query_grad, grad_ref[rows, window])
    key_total = dot_nn(score_grads[...], query_ref[:, window])
    value_total = dot_nn(weights[...], incoming_ref[:, window])
    for part, total in ((1, key_total), (2, value_total)):
        place = pl.ds(pl.multiple_of(start + part * features, LANES), WINDOW)
        grad_ref[:, place] = jnp.where(inside, total.astype(grad_ref.dtype), grad_ref[:, place])


def whole_block(shape, column):
    return pl.BlockSpec(shape, lambda head: (0, column), pipeline_mode=pl.Buffered(1))


def attend_forward(projected, everyone):
    rows = projected.shape[0]
    features = projected.shape[1] // 3
    tokens = everyone.shape[0]
    return pl.pallas_call(
        attend_forward_kernel,
        grid=(HEADS,),
        in_specs=[
            whole_block((rows, features), 0),
            whole_block((tokens, features), 1),
            whole_block((tokens, features), 2),
        ],
        out_specs=[
            whole_block((rows, features), 0),
            pl.BlockSpec((1, 1, rows), lambda head: (head, 0, 0)),
        ],
        out_shape=[
            jax.ShapeDtypeStruct((rows, features), BF16),
            jax.ShapeDtypeStruct((HEADS, 1, rows), F32),
        ],
        compiler_params=pltpu.CompilerParams(vmem_limit_bytes=56 * 1024 * 1024),
        cost_estimate=pl.CostEstimate(
            flops=4 * rows * tokens * HEADS * WINDOW,
            bytes_accessed=2 * (rows * 2 + tokens * 2) * features,
            transcendentals=rows * tokens * HEADS,
        ),
    )(projected, everyone, everyone)


def attend_backward(projected, everyone, incoming, log_total):
    rows = projected.shape[0]
    features = projected.shape[1] // 3
    tokens = everyone.shape[0]
    kind = BF16 if rows == tokens else F32
    return pl.pallas_call(
        attend_backward_kernel,
        grid=(HEADS,),
        in_specs=[
            whole_block((rows, features), 0),
            whole_block((tokens, features), 1),
            whole_block((tokens, features), 2),
            whole_block((rows, features), 0),
            pl.BlockSpec((1, 1, rows), lambda head: (head, 0, 0)),
        ],
        out_specs=whole_block((tokens, 3 * features), 0),
        out_shape=jax.ShapeDtypeStruct((tokens, 3 * features), kind),
        scratch_shapes=[pltpu.VMEM((tokens, rows), BF16), pltpu.VMEM((tokens, rows), BF16)],
        compiler_params=pltpu.CompilerParams(vmem_limit_bytes=56 * 1024 * 1024),
        cost_estimate=pl.CostEstimate(
            flops=10 * rows * tokens * HEADS * WINDOW,
            bytes_accessed=2 * (rows * 2 + tokens * 5) * features,
            transcendentals=rows * tokens * HEADS,
        ),
    )(projected, everyone, everyone, incoming, log_total)


class Layout:
    def __init__(self, micro, local, tokens, seq):
        self.micro, self.local, self.tokens, self.seq = micro, local, tokens, seq
        self.latents = micro * local
        self.sharers = max(1, seq // self.latents)
        self.held = max(1, self.latents // seq)
        self.span = seq // self.sharers

    def gather(self, values):
        values = values.reshape(self.latents, self.tokens, values.shape[-1])
        if self.sharers > 1:
            values = jnp.repeat(values, self.sharers, axis=0)
        moved = lax.all_to_all(values, "seq", split_axis=0, concat_axis=1, tiled=True)
        if self.sharers > 1:
            part = lax.axis_index("seq") % self.sharers
            count = self.span * self.tokens
            moved = lax.dynamic_slice_in_dim(moved, part * count, count, axis=1)
        return moved

    def scatter(self, values):
        if self.sharers > 1:
            values = jnp.concatenate([values] * self.sharers, axis=1)
        moved = lax.all_to_all(values, "seq", split_axis=1, concat_axis=0, tiled=True)
        if self.sharers > 1:
            part = lax.axis_index("seq") // self.span
            moved = moved.reshape(self.latents, self.sharers, self.tokens, values.shape[-1])
            moved = lax.dynamic_index_in_dim(moved, part, axis=1, keepdims=False)
        return moved.reshape(self.micro, self.local, self.tokens, values.shape[-1])

    def own_group(self, values, axis):
        if self.sharers == self.seq:
            return values
        count = values.shape[axis] // self.seq * self.sharers
        return lax.dynamic_slice_in_dim(
            values, lax.axis_index("seq") // self.sharers * count, count, axis=axis
        )


def on_device(
    latents,
    condition,
    cotangent,
    modulate_weight,
    modulate_bias,
    triple_weight,
    triple_bias,
    output_weight,
    output_bias,
    expand_weight,
    expand_bias,
    shrink_weight,
    shrink_bias,
):
    micro, local, tokens, features = latents.shape
    hidden = expand_weight.shape[1]
    groups = lax.axis_size("dp")
    seq = lax.axis_size("seq")
    devices = groups * seq
    place = Layout(micro, local, tokens, seq)
    held = place.held
    me = lax.axis_index("dp") * seq + lax.axis_index("seq")

    everyone_cond = lax.all_gather(condition.reshape(micro * local, features), "dp", axis=0, tiled=True)
    bias_shard = jnp.concatenate([modulate_bias, triple_bias, output_bias, expand_bias, shrink_bias])
    biases = lax.all_gather(bias_shard, AXES, axis=0, tiled=False).astype(F32)
    cuts = []
    offset = 0
    for shard in (modulate_bias, triple_bias, output_bias, expand_bias, shrink_bias):
        cuts.append(biases[:, offset : offset + shard.shape[0]].reshape(-1))
        offset += shard.shape[0]
    modulate_offset, triple_offset, output_offset, expand_offset, shrink_offset = cuts

    latent_rows = place.gather(latents)
    first_shard = jnp.concatenate([triple_weight, output_weight], axis=1)
    first_full = lax.all_gather(first_shard, AXES, axis=0, tiled=True)
    triple_full = first_full[:, : 3 * features]
    output_full = first_full[:, 3 * features :]
    expand_full = lax.all_gather(expand_weight, AXES, axis=0, tiled=True)
    shrink_full = lax.all_gather(shrink_weight, AXES, axis=0, tiled=True)

    owned = modulate_weight.shape[0]
    cond_act = jax.nn.silu(everyone_cond.astype(F32)).astype(BF16)
    act_owned = lax.dynamic_slice_in_dim(cond_act, me * owned, owned, axis=1)
    modulation_part = dot_nn(act_owned, modulate_weight)
    if place.sharers > 1:
        modulation_part = jnp.repeat(modulation_part, place.sharers, axis=0)
    modulation_parts = lax.all_to_all(modulation_part, AXES, split_axis=0, concat_axis=0, tiled=True)
    modulation = jnp.sum(modulation_parts.reshape(devices, held, -1), axis=0) + modulate_offset
    shift_one, scale_one, gate_one, shift_two, scale_two, gate_two = jnp.split(
        modulation[:, None, :], 6, axis=-1
    )

    latent_float = latent_rows.astype(F32)
    normed_one, inverse_one = norm_parts(latent_float)
    hidden_one = (normed_one * (1.0 + scale_one) + shift_one).astype(BF16)
    rows = held * latent_rows.shape[1]

    def flat(values):
        return values.reshape(rows, values.shape[-1])

    def unflat(values):
        return values.reshape(held, rows // held, values.shape[-1])

    zero = jnp.zeros((features,), F32)
    full_bias = jnp.concatenate([triple_offset[:features], zero, triple_offset[features:]])
    projected = unflat((dot_nn(flat(hidden_one), triple_full) + full_bias).astype(BF16))
    if place.sharers > 1:
        everyone = place.own_group(lax.all_gather(projected, "seq", axis=1, tiled=True), 1)
    else:
        everyone = projected
    mixed_parts, log_parts = zip(
        *(attend_forward(projected[index], everyone[index]) for index in range(held))
    )
    mixed = jnp.stack(mixed_parts) if held > 1 else mixed_parts[0][None]
    branch_one = unflat(dot_nn(flat(mixed), output_full)) + output_offset
    middle = latent_float + gate_one * branch_one
    normed_two, inverse_two = norm_parts(middle)
    hidden_two = (normed_two * (1.0 + scale_two) + shift_two).astype(BF16)
    pre_act = dot_nn(flat(hidden_two), expand_full) + expand_offset
    activated = gelu_parts(pre_act)[0].astype(BF16)
    branch_two = unflat(dot_nn(activated, shrink_full)) + shrink_offset
    output = place.scatter((middle + gate_two * branch_two).astype(BF16))

    incoming = place.gather(cotangent).astype(F32)
    branch_two_grad = (gate_two * incoming).astype(BF16)
    gate_two_grad = jnp.sum(incoming * branch_two, axis=1)
    shrink_offset_grad = jnp.sum(branch_two_grad.astype(F32), axis=(0, 1))
    shrink_grad = dot_tn(activated, flat(branch_two_grad)).astype(BF16)
    shrink_total = lax.psum_scatter(shrink_grad, AXES, scatter_dimension=0, tiled=True).astype(F32)
    act_grad = dot_nt(flat(branch_two_grad), shrink_full)
    pre_grad = (act_grad * gelu_parts(pre_act)[1]).astype(BF16)
    expand_offset_grad = jnp.sum(pre_grad.astype(F32), axis=0)
    expand_grad = dot_tn(flat(hidden_two), pre_grad).astype(BF16)
    expand_total = scatter_rows(expand_grad, devices)
    hidden_two_grad = unflat(dot_nt(pre_grad, expand_full))
    norm_grad_two, shift_two_grad, scale_two_grad = norm_back(
        hidden_two_grad, normed_two, inverse_two, scale_two
    )
    middle_grad = incoming + norm_grad_two
    branch_one_grad = (gate_one * middle_grad).astype(BF16)
    gate_one_grad = jnp.sum(middle_grad * branch_one, axis=1)
    output_offset_grad = jnp.sum(branch_one_grad.astype(F32), axis=(0, 1))
    output_grad = dot_tn(flat(mixed), flat(branch_one_grad)).astype(BF16)
    mixed_grad = unflat(dot_nt(flat(branch_one_grad), output_full).astype(BF16))
    grads = []
    for index in range(held):
        grad = attend_backward(projected[index], everyone[index], mixed_grad[index], log_parts[index])
        if place.sharers > 1:
            key_value = grad[:, features:]
            key_value = lax.psum_scatter(
                own_slots(key_value, place), "seq", scatter_dimension=0, tiled=True
            ).astype(BF16)
            grad = jnp.concatenate([grad[: rows // held, :features].astype(BF16), key_value], axis=1)
        grads.append(grad)
    triple_rows = jnp.concatenate(grads) if held > 1 else grads[0]
    column_sums = jnp.sum(triple_rows.astype(F32), axis=0)
    triple_offset_grad = jnp.concatenate([column_sums[:features], column_sums[2 * features :]])
    triple_grad = dot_tn(flat(hidden_one), triple_rows).astype(BF16)
    first_grad = jnp.concatenate([triple_grad, output_grad], axis=1)
    first_total = scatter_rows(first_grad, devices)
    hidden_one_grad = unflat(dot_nt(triple_rows, triple_full))
    norm_grad_one, shift_one_grad, scale_one_grad = norm_back(
        hidden_one_grad, normed_one, inverse_one, scale_one
    )
    latents_gradient = place.scatter((middle_grad + norm_grad_one).astype(BF16)).astype(F32)

    modulation_grad = jnp.concatenate(
        [shift_one_grad, scale_one_grad, gate_one_grad, shift_two_grad, scale_two_grad, gate_two_grad],
        axis=-1,
    )
    if place.sharers > 1:
        parts = lax.all_gather(modulation_grad, "seq", axis=0, tiled=True)
        modulation_grad = jnp.sum(place.own_group(parts, 0), axis=0, keepdims=True)
    all_grads = lax.all_gather(modulation_grad.astype(BF16), AXES, axis=0, tiled=True)
    if place.sharers > 1:
        all_grads = all_grads[:: place.sharers]
    modulate_total = dot_tn(act_owned, all_grads)
    shard = modulate_bias.shape[0]
    modulate_offset_total = jnp.sum(
        lax.dynamic_slice_in_dim(all_grads, me * shard, shard, axis=1).astype(F32), axis=0
    )
    cond_back = dot_nt(all_grads, modulate_weight)
    everyone_back = lax.all_gather(cond_back, AXES, axis=1, tiled=True)
    group_back = lax.dynamic_slice_in_dim(
        everyone_back, lax.axis_index("dp") * micro * local, micro * local, axis=0
    ).reshape(condition.shape)
    cond_float = condition.astype(F32)
    sigmoid_cond = jax.nn.sigmoid(cond_float)
    condition_gradient = group_back * (sigmoid_cond * (1.0 + cond_float * (1.0 - sigmoid_cond)))

    bias_grads = jnp.concatenate(
        [
            values.reshape(devices, -1)
            for values in (triple_offset_grad, output_offset_grad, expand_offset_grad, shrink_offset_grad)
        ],
        axis=1,
    )
    bias_total = jnp.sum(
        lax.all_to_all(bias_grads, AXES, split_axis=0, concat_axis=0, tiled=True), axis=0
    )
    bias_cuts = []
    offset = 0
    for part in (triple_bias, output_bias, expand_bias, shrink_bias):
        bias_cuts.append(bias_total[offset : offset + part.shape[0]])
        offset += part.shape[0]
    return (
        output,
        latents_gradient,
        condition_gradient,
        modulate_total,
        modulate_offset_total,
        first_total[:, : 3 * features],
        bias_cuts[0],
        first_total[:, 3 * features :],
        bias_cuts[1],
        expand_total,
        bias_cuts[2],
        shrink_total,
        bias_cuts[3],
    )


def scatter_rows(values, devices):
    rows, columns = values.shape
    slots = values.reshape(rows * columns // 1152, 1152)
    total = lax.psum_scatter(slots, AXES, scatter_dimension=0, tiled=True)
    return total.reshape(rows // devices, columns).astype(F32)


def own_slots(values, place):
    group = lax.axis_index("seq") // place.sharers
    slots = jnp.zeros((place.seq // place.sharers,) + values.shape, values.dtype)
    slots = lax.dynamic_update_index_in_dim(slots, values, group, axis=0)
    return slots.reshape(-1, values.shape[-1])


MESH = pl.DeviceIdType.MESH
ANY = pl.BlockSpec(memory_space=pl.ANY)
ROWS = 144
MATMUL_ROWS = 1024


class Here:
    def __init__(self):
        dp, self.member = lax.axis_index("dp"), lax.axis_index("seq")
        self.group = dp
        self.z, self.core = dp // 2, dp % 2
        self.index = dp * 4 + self.member
        y, x = self.member // 2, self.member % 2
        self.across_x = y * 2 + (1 - x)
        self.across_y = (1 - y) * 2 + x
        self.across = (1 - y) * 2 + (1 - x)

    def at_x(self):
        return (self.group, self.across_x)

    def at_y(self):
        return (self.group, self.across_y)

    def at_core(self):
        return (self.z * 2 + (1 - self.core), self.member)

    def at_z(self, step):
        return (lax.rem(self.z + step, 4) * 2 + self.core, self.member)

    def at_member(self, step):
        return (self.group, lax.rem(self.member + step, 4))

    def at_index(self, step):
        place = lax.rem(self.index + step, 32)
        return (place // 4, lax.rem(place, 4))


def greet(partners):
    barrier = pltpu.get_barrier_semaphore()
    for partner in partners:
        pl.semaphore_signal(barrier, inc=1, device_id=partner, device_id_type=MESH)
    pl.semaphore_wait(barrier, len(partners))


def greet_all(here):
    barrier = pltpu.get_barrier_semaphore()

    def signal(step, carry):
        pl.semaphore_signal(barrier, inc=1, device_id=here.at_index(step), device_id_type=MESH)
        return carry

    lax.fori_loop(1, 32, signal, 0)
    pl.semaphore_wait(barrier, 31)


class Wires:
    def __init__(self, sent, landed):
        self.sent, self.landed = sent, landed

    def copy(self, number, source, target, partner):
        return pltpu.make_async_remote_copy(
            src_ref=source,
            dst_ref=target,
            send_sem=self.sent.at[number],
            recv_sem=self.landed.at[number],
            device_id=partner,
            device_id_type=MESH,
        )


def everyone(here, source_of, target, sent, landed):
    def copy_of(step):
        place = lax.rem(here.index + step, 32)
        return pltpu.make_async_remote_copy(
            src_ref=source_of(place),
            dst_ref=target.at[here.index],
            send_sem=sent.at[step],
            recv_sem=landed.at[step],
            device_id=here.at_index(step),
            device_id_type=MESH,
        )

    def start(step, carry):
        copy_of(step).start()
        return carry

    def wait(step, carry):
        copy_of(step).wait()
        return carry

    lax.fori_loop(1, 32, start, 0)
    return lambda: lax.fori_loop(1, 32, wait, 0)


def same_core(here, source, target, sent, landed):
    mine = here.z * 4 + here.member

    def copy_of(step):
        place = lax.rem(mine + step, 16)
        return pltpu.make_async_remote_copy(
            src_ref=source.at[place],
            dst_ref=target.at[mine],
            send_sem=sent.at[step],
            recv_sem=landed.at[step],
            device_id=(place // 4 * 2 + here.core, lax.rem(place, 4)),
            device_id_type=MESH,
        )

    def start(step, carry):
        copy_of(step).start()
        return carry

    def wait(step, carry):
        copy_of(step).wait()
        return carry

    lax.fori_loop(1, 16, start, 0)
    return lambda: lax.fori_loop(1, 16, wait, 0)


def introduce_kernel(
    note_ref, shard_ref, shrink_ref, notes_ref, blocks_ref, quad_ref, landing, wide, buffer,
    note_sent, note_landed, sent, landed, local,
):
    here = Here()
    greet_all(here)
    wires = Wires(sent, landed)

    def columns(place):
        return shard_ref.at[:, :, pl.ds(pl.multiple_of(place * 1152, LANES), 1152)]

    quads = []
    for step in range(1, 4):
        place = lax.rem(here.member + step, 4)
        quads.append(wires.copy(step - 1, columns(place), landing.at[here.member], here.at_member(step)))
    shrinks = [
        wires.copy(2 + step, shrink_ref, quad_ref.at[here.member], here.at_member(step)) for step in range(1, 4)
    ]
    for copy in quads:
        copy.start()
    keep = Bounce(shrink_ref, buffer, quad_ref.at[here.member], local.at[2])
    keep.start()
    done = everyone(here, lambda place: note_ref.at[0], notes_ref, note_sent, note_landed)
    own = pltpu.make_async_copy(columns(here.member), landing.at[here.member], local.at[0])
    own.start()
    mine = pltpu.make_async_copy(note_ref.at[0], notes_ref.at[here.index], local.at[1])
    mine.start()
    for copy in shrinks:
        copy.start()
    own.wait()
    keep.go_on()
    for copy in quads:
        copy.wait_recv()
    for part in range(2):
        for member in range(4):
            wide[member * 36 : member * 36 + 36, :] = landing[member, part].astype(F32)[:36]
        blocks_ref[part] = wide[...].astype(BF16)
    for copy in quads:
        copy.wait_send()
    for copy in shrinks:
        copy.wait()
    keep.wait()
    mine.wait()
    done()


def introduce(note, shard, shrink):
    return pl.pallas_call(
        introduce_kernel,
        in_specs=[ANY, ANY, ANY],
        out_specs=[ANY, pl.BlockSpec(memory_space=pltpu.VMEM), ANY],
        out_shape=[
            jax.ShapeDtypeStruct((32,) + note.shape[1:], note.dtype),
            jax.ShapeDtypeStruct((2, ROWS, 1152), BF16),
            jax.ShapeDtypeStruct((4, ROWS, 1152), BF16),
        ],
        scratch_shapes=[
            pltpu.VMEM((4,) + shard.shape[:2] + (1152,), BF16),
            pltpu.VMEM((ROWS, 1152), F32),
            pltpu.VMEM((ROWS, 1152), BF16),
            pltpu.SemaphoreType.DMA((32,)),
            pltpu.SemaphoreType.DMA((32,)),
            pltpu.SemaphoreType.DMA((6,)),
            pltpu.SemaphoreType.DMA((6,)),
            pltpu.SemaphoreType.DMA((3,)),
        ],
        compiler_params=pltpu.CompilerParams(collective_id=1, has_side_effects=True),
    )(note, shard, shrink)


class Bounce:
    def __init__(self, source, buffer, target, semaphore):
        self.first = pltpu.make_async_copy(source, buffer, semaphore)
        self.second = pltpu.make_async_copy(buffer, target, semaphore)

    def start(self):
        self.first.start()

    def go_on(self):
        self.first.wait()
        self.second.start()

    def wait(self):
        self.second.wait()


ARRIVALS = (0, 1, 3, 2)


class Gather:
    COPIES = 31

    def __init__(self, here, place, own, sent, landed):
        self.here, self.place, self.own = here, place, own
        self.wires = Wires(sent, landed)

    def z_of(self, order):
        return lax.rem(self.here.z + 4 - ARRIVALS[order], 4)

    def along(self, step, block):
        here = self.here
        return self.wires.copy(step - 1, block, self.own(here.z), here.at_z(step))

    def begin(self, block):
        for step in (1, 3, 2):
            self.along(step, block).start()

    def sideways(self, kind, order):
        here = self.here
        z = self.z_of(order)
        partner = (here.at_x, here.at_y, here.at_core)[kind]()
        return self.wires.copy(
            3 + kind * 4 + order, self.own(z), self.place(here.member, z, here.core), partner
        )

    def passed(self, kind, order):
        here = self.here
        z = self.z_of(order)
        if kind == 3:
            member = here.across_x if order >= 2 else here.across_y
            partner = here.at_y() if order >= 2 else here.at_x()
        else:
            member = (here.across_x, here.across_y, here.across)[kind]
            partner = here.at_core()
        ref = self.place(member, z, here.core)
        return self.wires.copy(15 + kind * 4 + order, ref, ref, partner)

    def spread(self, order):
        for kind in range(3):
            self.sideways(kind, order).start()

    def relay(self, order):
        self.sideways(0, order).wait_recv()
        if order >= 2:
            self.passed(3, order).start()
        self.passed(0, order).start()
        self.sideways(1, order).wait_recv()
        if order < 2:
            self.passed(3, order).start()
        self.passed(1, order).start()

    def close(self, order):
        self.passed(3, order).wait_recv()
        self.passed(2, order).start()

    def end(self):
        for order in range(4):
            self.sideways(2, order).wait_recv()
            for kind in range(3):
                self.passed(kind, order).wait_recv()
        for order in range(4):
            for kind in range(3):
                self.sideways(kind, order).wait_send()
            for kind in range(4):
                self.passed(kind, order).wait_send()


def open_kernel(
    block_ref, part_ref, token_ref, full_ref, expand_ref, parts_ref, tokens_ref,
    part_mine, part_half, block_buffer, token_buffer, part_sent, part_landed, sent, landed, more_sent, more_landed, local,
):
    here = Here()
    greet_all(here)
    more = Wires(more_sent, more_landed)
    half = more.copy(0, part_ref.at[1 - here.core], part_half, here.at_core())
    half.start()
    load = pltpu.make_async_copy(part_ref.at[here.core], part_mine, local.at[0])
    load.start()
    first = Gather(
        here,
        lambda member, z, core: full_ref.at[member, z, core],
        lambda z: full_ref.at[here.member, z, here.core],
        sent.at[0],
        landed.at[0],
    )
    second = Gather(here, None, lambda z: expand_ref.at[z], sent.at[1], landed.at[1])
    first.begin(block_ref.at[0])
    mine = here.z * 4 + here.member
    own = [
        Bounce(block_ref.at[0], block_buffer.at[0], first.own(here.z), local.at[1]),
        Bounce(block_ref.at[1], block_buffer.at[1], second.own(here.z), local.at[2]),
        Bounce(token_ref.at[here.member], token_buffer, tokens_ref.at[here.member], local.at[3]),
    ]
    for copy in own:
        copy.start()
    moved = []
    for step in range(1, 4):
        place = lax.rem(here.member + step, 4)
        moved.append(more.copy(step, token_ref.at[place], tokens_ref.at[here.member], here.at_member(step)))
    for copy in moved:
        copy.start()
    for copy in own:
        copy.go_on()
    load.wait()
    half.wait()

    def add(place, carry):
        part_mine[place] += part_half[place]
        return carry

    lax.fori_loop(0, 16, add, 0)
    done = same_core(here, part_mine, parts_ref, part_sent, part_landed)
    keep = pltpu.make_async_copy(part_mine.at[mine], parts_ref.at[mine], local.at[4])
    keep.start()
    own[0].wait()
    first.spread(0)
    for order in range(1, 4):
        first.along(ARRIVALS[order], block_ref.at[0]).wait_recv()
        first.spread(order)
    second.begin(block_ref.at[1])
    for order in range(4):
        first.relay(order)
    for order in range(4):
        first.close(order)
    first.end()
    for step in (1, 3, 2):
        first.along(step, block_ref.at[0]).wait_send()
        second.along(step, block_ref.at[1]).wait()
    for copy in moved:
        copy.wait()
    for copy in own[1:]:
        copy.wait()
    keep.wait()
    done()


def open_up(blocks, parts, tokens):
    column = jax.ShapeDtypeStruct((4, ROWS, 1152), BF16)
    return pl.pallas_call(
        open_kernel,
        in_specs=[ANY] * 3,
        out_specs=[ANY] * 4,
        out_shape=[
            jax.ShapeDtypeStruct((4, 4, 2, ROWS, 1152), BF16),
            column,
            jax.ShapeDtypeStruct(parts.shape[1:], parts.dtype),
            jax.ShapeDtypeStruct(tokens.shape, tokens.dtype),
        ],
        scratch_shapes=[
            pltpu.VMEM(parts.shape[1:], F32),
            pltpu.VMEM(parts.shape[1:], F32),
            pltpu.VMEM((2, ROWS, 1152), BF16),
            pltpu.VMEM(tokens.shape[1:], BF16),
            pltpu.SemaphoreType.DMA((16,)),
            pltpu.SemaphoreType.DMA((16,)),
            pltpu.SemaphoreType.DMA((2, 31)),
            pltpu.SemaphoreType.DMA((2, 31)),
            pltpu.SemaphoreType.DMA((7,)),
            pltpu.SemaphoreType.DMA((7,)),
            pltpu.SemaphoreType.DMA((6,)),
        ],
        compiler_params=pltpu.CompilerParams(collective_id=2, has_side_effects=True),
    )(blocks, parts, tokens)


class Column:
    COPIES = 13

    def __init__(self, here, full, quad, sent, landed):
        self.here, self.full, self.quad = here, full, quad
        self.wires = Wires(sent, landed)

    def pass_on(self, way, turn):
        here = self.here
        source = self.quad if turn == 0 else self.full.at[here.z - way * turn, here.core]
        target = self.full.at[here.z - way * turn, here.core]
        partner = ((here.z + way) * 2 + here.core, here.member)
        return self.wires.copy(turn + (3 if way < 0 else 0), source, target, partner)

    def arrival(self, way, turn):
        here = self.here
        ref = self.full.at[here.z - way * (turn + 1), here.core]
        return self.wires.copy(turn + (3 if way < 0 else 0), ref, ref, here.at_core())

    def across(self, way, turn):
        here = self.here
        ref = self.full.at[here.z - way * (turn + 1), here.core]
        return self.wires.copy(6 + turn + (3 if way < 0 else 0), ref, ref, here.at_core())

    def own_across(self):
        here = self.here
        return self.wires.copy(12, self.quad, self.full.at[here.z, here.core], here.at_core())

    def sends(self, way, turn):
        z = self.here.z
        return (z < 3) & (z >= turn) if way > 0 else (z > 0) & (z <= 3 - turn)

    def comes(self, way, turn):
        z = self.here.z
        return z >= turn + 1 if way > 0 else z <= 2 - turn

    def start(self, turn):
        for way in (1, -1):
            pl.when(self.sends(way, turn))(lambda way=way: self.pass_on(way, turn).start())
        if turn == 0:
            self.own_across().start()

    def take(self, turn):
        for way in (1, -1):

            @pl.when(self.comes(way, turn))
            def _():
                self.arrival(way, turn).wait_recv()
                self.across(way, turn).start()

    def step(self, turn):
        for way in (1, -1):

            @pl.when(self.comes(way, turn - 1))
            def _():
                self.arrival(way, turn - 1).wait_recv()
            if turn < 3:
                pl.when(self.sends(way, turn))(lambda way=way: self.pass_on(way, turn).start())
            pl.when(self.comes(way, turn - 1))(lambda way=way: self.across(way, turn - 1).start())

    def end(self):
        self.own_across().wait()
        for way in (1, -1):
            for turn in range(3):
                pl.when(self.comes(way, turn))(lambda way=way, turn=turn: self.across(way, turn).wait())
                pl.when(self.sends(way, turn))(lambda way=way, turn=turn: self.pass_on(way, turn).wait_send())


MIX_AT = 19
EXPAND_AT = MIX_AT + 4
FORWARD_STEPS = EXPAND_AT + 4


def forward_kernel(
    hidden_ref, weight_ref, bias_ref, latent_ref, scaling_ref, expand_bias_ref, expand_column, shrink_quad, incoming_ref,
    projected_ref, mixed_ref, log_ref, branch_ref, middle_ref, second_ref, pre_ref, active_ref,
    expand_full, shrink_full, incomings_ref,
    chunk, token_buffer, sent, landed, more_sent, more_landed, local, fetch,
):
    step = pl.program_id(0)
    here = Here()
    features = hidden_ref.shape[1]
    second = Gather(
        here,
        lambda member, z, core: expand_full.at[member, z, core],
        lambda z: expand_column.at[z],
        sent,
        landed,
    )
    third = Column(here, shrink_full, shrink_quad, more_sent.at[pl.ds(0, 13)], more_landed.at[pl.ds(0, 13)])
    more = Wires(more_sent, more_landed)
    own = (
        Bounce(expand_column, chunk.at[0, :, 0], expand_full.at[here.member, :, here.core], local.at[0]),
        Bounce(shrink_quad, chunk.at[1, :, 0], shrink_full.at[here.z, here.core], local.at[1]),
        Bounce(incoming_ref.at[here.member], token_buffer, incomings_ref.at[here.member], local.at[2]),
    )

    def fetch_chunk(part):
        return pltpu.make_async_copy(expand_full.at[part], chunk.at[part % 2], fetch.at[part % 2])

    def move(number):
        place = lax.rem(here.member + number, 4)
        return more.copy(
            12 + number, incoming_ref.at[place], incomings_ref.at[here.member], here.at_member(number)
        )

    @pl.when(step == 0)
    def _():
        greet_near(here)
        for order in range(4):
            second.spread(order)
        third.start(0)
        for copy in own:
            copy.start()

    @pl.when(step == 1)
    def _():
        for copy in own:
            copy.go_on()

    def relay_expand():
        for order in range(4):
            second.relay(order)
        for number in (2, 1, 3):
            move(number).start()

    def close_expand():
        for order in range(4):
            second.close(order)

    def finish_expand():
        second.end()
        for copy in own:
            copy.wait()
        fetch_chunk(0).start()
        fetch_chunk(1).start()

    def finish():
        third.step(3)
        third.end()
        for number in (1, 2, 3):
            move(number).wait()

    for turn, action in (
        (12, relay_expand),
        (12, functools.partial(third.step, 1)),
        (19, close_expand),
        (EXPAND_AT + 1, functools.partial(third.step, 2)),
        (EXPAND_AT - 1, finish_expand),
    ):
        pl.when(step == turn)(action)

    def row_blocks(body):
        def one(block, carry):
            body(pl.ds(pl.multiple_of(block * MATMUL_ROWS, MATMUL_ROWS), MATMUL_ROWS))
            return carry

        lax.fori_loop(0, hidden_ref.shape[0] // MATMUL_ROWS, one, 0)

    for part in range(3):

        @pl.when(step == part)
        def _():
            def project(rows):
                values = dot_nn(hidden_ref[rows, :], weight_ref[0]) + bias_ref[part]
                projected_ref[rows, part * features : (part + 1) * features] = values.astype(BF16)

            row_blocks(project)

    @pl.when((step >= 3) & (step < MIX_AT))
    def _():
        forward_head(step - 3, features, projected_ref, mixed_ref, log_ref)

    @pl.when((step >= MIX_AT) & (step < EXPAND_AT))
    def _():
        rows = pl.ds(pl.multiple_of((step - MIX_AT) * 256, 256), 256)
        branch = dot_nn(mixed_ref[rows, :], weight_ref[0]) + bias_ref[3]
        branch_ref[...] = branch
        middle = latent_ref[...].astype(F32) + scaling_ref[0] * branch
        middle_ref[...] = middle
        normed, _ = norm_parts(middle)
        second_ref[rows, :] = (normed * (1.0 + scaling_ref[2]) + scaling_ref[1]).astype(BF16)

    for part in range(4):

        @pl.when(step == EXPAND_AT + part)
        def _():
            fetch_chunk(part).wait()

            def expand(rows):
                weight = chunk[part % 2].reshape(features, features)
                values = dot_nn(second_ref[rows, :], weight) + expand_bias_ref[part]
                pre_ref[rows, :] = values
                active_ref[rows, :] = gelu_parts(values)[0].astype(BF16)

            row_blocks(expand)
            if part + 2 < 4:
                fetch_chunk(part + 2).start()

    pl.when(step == FORWARD_STEPS - 1)(finish)


def forward_head(head, features, projected_ref, mixed_ref, log_ref):
    last = features // LANES - WINDOW // LANES
    start = jnp.minimum(head * HD // LANES, last) * LANES
    first = head * HD - start
    lane = lax.broadcasted_iota(jnp.int32, (1, WINDOW), 1)
    inside = (lane >= first) & (lane < first + HD)

    def window(part):
        return pl.ds(pl.multiple_of(start + part * features, LANES), WINDOW)

    keys = jnp.where(inside, projected_ref[:, window(1)], 0)
    values = jnp.where(inside, projected_ref[:, window(2)], 0)
    turned = values.T
    factor = HD**-0.5 * LOG2E
    count = projected_ref.shape[0] // QUERY_BLOCK

    def score(block):
        return dot_nt(keys, projected_ref[pl.ds(block * QUERY_BLOCK, QUERY_BLOCK), window(0)])

    following = score(0)
    for block in range(count):
        rows = pl.ds(block * QUERY_BLOCK, QUERY_BLOCK)
        scores = following
        if block + 1 < count:
            following = score(block + 1)
        peak = jnp.max(scores, axis=0, keepdims=True)
        powers = jnp.exp2(scores * factor - peak * factor)
        total = jnp.sum(powers, axis=0, keepdims=True)
        log_ref[0, :, rows] = peak * factor + jnp.log2(total)
        weights = (powers * (1.0 / total)).astype(BF16)
        mixed = dot_nn(turned, weights).T.astype(BF16)
        mixed_ref[rows, window(0)] = jnp.where(inside, mixed, mixed_ref[rows, window(0)])


def greet_near(here):
    greet(
        [here.at_member(step) for step in range(1, 4)]
        + [here.at_z(step) for step in range(1, 4)]
        + [here.at_core()]
    )


def forward(hidden, weights, biases, latents, scalings, expand_bias, expand_column, shrink_quad, incoming):
    rows, features = hidden.shape

    def clip(step, low, high):
        return jnp.minimum(jnp.maximum(step - low, 0), high)

    def everything(shape):
        return pl.BlockSpec(shape, lambda step: (0,) * len(shape), pipeline_mode=pl.Buffered(1))

    by_rows = pl.BlockSpec((256, features), lambda step: (clip(step, MIX_AT, 3), 0))
    by_part = pl.BlockSpec((rows, features), lambda step: (0, clip(step, EXPAND_AT, 3)))
    tokens = jax.ShapeDtypeStruct((rows, features), BF16)
    wide = jax.ShapeDtypeStruct((rows, features), F32)
    return pl.pallas_call(
        forward_kernel,
        grid=(FORWARD_STEPS,),
        in_specs=[
            everything((rows, features)),
            pl.BlockSpec((1, features, features), lambda step: (jnp.minimum(step, 3), 0, 0)),
            everything((4, 1, features)),
            by_rows,
            everything((3, 1, features)),
            everything((4, 1, features)),
            ANY,
            ANY,
            ANY,
        ],
        out_specs=[
            everything((rows, 3 * features)),
            everything((rows, features)),
            pl.BlockSpec((1, 1, rows), lambda step: (clip(step, 3, HEADS - 1), 0, 0)),
            by_rows,
            by_rows,
            everything((rows, features)),
            by_part,
            by_part,
            ANY,
            ANY,
            ANY,
        ],
        out_shape=[
            jax.ShapeDtypeStruct((rows, 3 * features), BF16),
            tokens,
            jax.ShapeDtypeStruct((HEADS, 1, rows), F32),
            wide,
            wide,
            tokens,
            jax.ShapeDtypeStruct((rows, 4 * features), F32),
            jax.ShapeDtypeStruct((rows, 4 * features), BF16),
            jax.ShapeDtypeStruct((4, 4, 2, ROWS, 1152), BF16),
            jax.ShapeDtypeStruct((4, 2, 4, ROWS, 1152), BF16),
            jax.ShapeDtypeStruct(incoming.shape, BF16),
        ],
        scratch_shapes=[
            pltpu.VMEM((2, 4, 2, ROWS, 1152), BF16),
            pltpu.VMEM(incoming.shape[1:], BF16),
            pltpu.SemaphoreType.DMA((31,)),
            pltpu.SemaphoreType.DMA((31,)),
            pltpu.SemaphoreType.DMA((16,)),
            pltpu.SemaphoreType.DMA((16,)),
            pltpu.SemaphoreType.DMA((3,)),
            pltpu.SemaphoreType.DMA((2,)),
        ],
        compiler_params=pltpu.CompilerParams(
            collective_id=5, has_side_effects=True, vmem_limit_bytes=60 * 1024 * 1024
        ),
    )(hidden, weights, biases, latents, scalings, expand_bias, expand_column, shrink_quad, incoming)


class Reduce:
    SCRATCH = (
        pltpu.VMEM((4, 4, ROWS, 1152), BF16),
        pltpu.VMEM((4, 4, ROWS, 1152), BF16),
        pltpu.VMEM((2, 2, ROWS, 1152), BF16),
        pltpu.VMEM((2, 4, ROWS, 1152), BF16),
        pltpu.VMEM((3, ROWS, 1152), BF16),
        pltpu.SemaphoreType.DMA((13,)),
        pltpu.SemaphoreType.DMA((13,)),
        pltpu.SemaphoreType.DMA((4,)),
    )

    def __init__(self, here, source, total, kept, crossed, relayed, beside, along, sent, landed, local):
        self.here, self.source, self.total, self.local = here, source, total, local
        self.kept, self.crossed, self.relayed, self.beside, self.pieces = kept, crossed, relayed, beside, along
        self.wires = Wires(sent, landed)
        self.order = (here.across, here.across_x, here.across_y, here.member)

    def load(self, turn):
        return pltpu.make_async_copy(
            self.source(self.order[turn], self.here.core), self.kept.at[turn], self.local.at[turn]
        )

    def cross(self, turn):
        here = self.here
        return self.wires.copy(
            turn, self.source(self.order[turn], 1 - here.core), self.crossed.at[turn], here.at_core()
        )

    def relay(self, way):
        partner = (self.here.at_x, self.here.at_y)[way]()
        half = pl.ds(2 - 2 * way, 2)
        return self.wires.copy(4 + way, self.kept.at[0, half], self.relayed.at[way], partner)

    def side(self, way, part):
        partner = (self.here.at_x, self.here.at_y)[way]()
        half = pl.ds(2 * part, 2)
        return self.wires.copy(
            6 + 2 * way + part, self.kept.at[1 + way, half], self.beside.at[way, half], partner
        )

    def along(self, step):
        z = lax.rem(self.here.z + step, 4)
        return self.wires.copy(9 + step, self.kept.at[3, z], self.pieces.at[step - 1], self.here.at_z(step))

    def begin(self):
        for turn in range(4):
            self.cross(turn).start()
            self.load(turn).start()

    def add_crossed(self, turn):
        self.load(turn).wait()
        self.cross(turn).wait_recv()

        def add(z, carry):
            self.kept[turn, z] = (self.kept[turn, z].astype(F32) + self.crossed[turn, z].astype(F32)).astype(BF16)
            return carry

        lax.fori_loop(0, 4, add, 0)

    def add_relayed(self, turn, way, first):
        def add(z, carry):
            self.kept[turn, first + z] = (
                self.kept[turn, first + z].astype(F32) + self.relayed[way, z].astype(F32)
            ).astype(BF16)
            return carry

        lax.fori_loop(0, 2, add, 0)

    def diagonal(self):
        self.add_crossed(0)
        self.relay(1).start()
        self.relay(0).start()

    def direct_x(self):
        self.add_crossed(1)
        self.side(0, 1).start()

    def direct_y(self):
        self.add_crossed(2)
        self.side(1, 0).start()

    def relay_x(self):
        self.relay(1).wait_recv()
        self.add_relayed(1, 1, 0)
        self.side(0, 0).start()

    def relay_y(self):
        self.relay(0).wait_recv()
        self.add_relayed(2, 0, 2)
        self.side(1, 1).start()

    def keep_own(self):
        self.add_crossed(3)

    def three(self, z):
        return (
            self.kept[3, z].astype(F32) + self.beside[0, z].astype(F32) + self.beside[1, z].astype(F32)
        )

    def along_z(self):
        here = self.here
        for way in range(2):
            for part in range(2):
                self.side(way, part).wait_recv()
        for step in (2, 1, 3):
            z = lax.rem(here.z + step, 4)
            self.kept[3, z] = self.three(z).astype(BF16)
            self.along(step).start()
        self.total[...] = self.three(here.z)

    def finish(self):
        for step in (1, 3, 2):
            self.along(step).wait_recv()
        self.total[...] += self.pieces[0].astype(F32) + self.pieces[1].astype(F32) + self.pieces[2].astype(F32)
        for turn in range(4):
            self.cross(turn).wait_send()
        for way in range(2):
            self.relay(way).wait_send()
            for part in range(2):
                self.side(way, part).wait_send()
        for step in range(1, 4):
            self.along(step).wait_send()

    def steps(self):
        return (
            self.begin,
            self.diagonal,
            self.direct_x,
            self.direct_y,
            self.keep_own,
            self.relay_x,
            self.relay_y,
            self.along_z,
            self.finish,
        )


def backward_reduce_kernel(
    query_ref, key_ref, value_ref, incoming_ref, log_ref, source_ref, grad_ref, total_ref,
    key_total, value_total, *scratch
):
    head = pl.program_id(0)
    here = Here()
    reduce = Reduce(here, lambda member, core: source_ref.at[member, :, core], total_ref, *scratch)

    @pl.when(head == 0)
    def _():
        greet((here.at_x(), here.at_y(), here.at_core(), here.at_z(1), here.at_z(2), here.at_z(3)))

    steps = reduce.steps()
    for step, turn in zip(steps[:-1], (0, 2, 6, 6, 6, 6, 6, 13)):
        pl.when(head == turn)(step)
    attend_backward_kernel(
        query_ref, key_ref, value_ref, incoming_ref, log_ref, grad_ref, key_total, value_total
    )
    pl.when(head == HEADS - 1)(steps[-1])


def attend_backward_reduce(projected, incoming, log_total, source):
    rows = projected.shape[0]
    features = projected.shape[1] // 3
    return pl.pallas_call(
        backward_reduce_kernel,
        grid=(HEADS,),
        in_specs=[whole_block((rows, features), part) for part in (0, 1, 2, 0)]
        + [pl.BlockSpec((1, 1, rows), lambda head: (head, 0, 0)), ANY],
        out_specs=[whole_block((rows, 3 * features), 0), whole_block((ROWS, features), 0)],
        out_shape=[
            jax.ShapeDtypeStruct((rows, 3 * features), BF16),
            jax.ShapeDtypeStruct((ROWS, features), F32),
        ],
        scratch_shapes=[pltpu.VMEM((rows, rows), BF16), pltpu.VMEM((rows, rows), BF16), *Reduce.SCRATCH],
        compiler_params=pltpu.CompilerParams(
            collective_id=6, has_side_effects=True, vmem_limit_bytes=58 * 1024 * 1024
        ),
    )(projected, projected, projected, incoming, log_total, source)


def clipped(step, low, high):
    return jnp.minimum(jnp.maximum(step - low, 0), high)


def everything(shape):
    return pl.BlockSpec(shape, lambda step: (0,) * len(shape), pipeline_mode=pl.Buffered(1))


def turn_kernel(
    active_ref, shrink_ref, middle_ref, incoming_ref, gate_ref, bias_ref,
    tokens_ref, back_ref, grads_ref, sums_ref, total, token, sent, landed, local,
):
    step = pl.program_id(0)
    here = Here()
    wires = Wires(sent, landed)

    def move(number):
        place = lax.rem(here.member + number, 4)
        return wires.copy(number - 1, token.at[place], tokens_ref.at[here.member], here.at_member(number))

    own = pltpu.make_async_copy(token.at[here.member], tokens_ref.at[here.member], local.at[0])

    @pl.when(step == 0)
    def _():
        greet([here.at_member(number) for number in range(1, 4)])
        sums_ref[...] = jnp.zeros_like(sums_ref)

    def blocks(body):
        def one(block, carry):
            body(pl.ds(pl.multiple_of(block * MATMUL_ROWS, MATMUL_ROWS), MATMUL_ROWS))
            return carry

        lax.fori_loop(0, total.shape[0] // MATMUL_ROWS, one, 0)

    @pl.when(step == 0)
    def _():
        def first(rows):
            total[rows, :] = dot_nn(active_ref[rows, :], shrink_ref[...])

        blocks(first)

    @pl.when((step > 0) & (step < 4))
    def _():
        def more(rows):
            total[rows, :] += dot_nn(active_ref[rows, :], shrink_ref[...])

        blocks(more)

    @pl.when((step >= 4) & (step < 8))
    def _():
        rows = pl.ds(pl.multiple_of((step - 4) * 256, 256), 256)
        branch = total[rows, :] + bias_ref[...]
        incoming = incoming_ref[0].astype(F32)
        token[step - 4] = (middle_ref[...] + gate_ref[...] * branch).astype(BF16)
        back = (gate_ref[...] * incoming).astype(BF16)
        back_ref[rows, :] = back
        sums_ref[0:1, :] += jnp.sum(incoming * branch, axis=0, keepdims=True)
        sums_ref[1:2, :] += jnp.sum(back.astype(F32), axis=0, keepdims=True)

    for number in range(1, 4):

        @pl.when(step - 4 == lax.rem(here.member + number, 4))
        def _():
            move(number).start()

    @pl.when(step - 4 == here.member)
    def _():
        own.start()

    @pl.when(step >= 8)
    def _():
        width = active_ref.shape[1] // 3
        for part in range(3):
            columns = slice(part * width, (part + 1) * width)
            grads_ref[0, columns, :] = dot_tn(active_ref[:, columns], back_ref[...]).astype(BF16)

    @pl.when(step == 11)
    def _():
        for number in range(1, 4):
            move(number).wait()
        own.wait()


def turn(active, shrink, middle, incoming, gate, bias):
    rows, features = middle.shape
    return pl.pallas_call(
        turn_kernel,
        grid=(12,),
        in_specs=[
            pl.BlockSpec((rows, features), lambda step: (0, jnp.where(step < 8, jnp.minimum(step, 3), step - 8))),
            pl.BlockSpec((features, features), lambda step: (jnp.minimum(step, 3), 0)),
            pl.BlockSpec((256, features), lambda step: (clipped(step, 4, 3), 0)),
            pl.BlockSpec((1, 256, features), lambda step: (clipped(step, 4, 3), 0, 0)),
            everything((1, features)),
            everything((1, features)),
        ],
        out_specs=[
            ANY,
            everything((rows, features)),
            pl.BlockSpec((1, features, features), lambda step: (clipped(step, 8, 3), 0, 0)),
            everything((8, features)),
        ],
        out_shape=[
            jax.ShapeDtypeStruct(incoming.shape, BF16),
            jax.ShapeDtypeStruct((rows, features), BF16),
            jax.ShapeDtypeStruct((4, features, features), BF16),
            jax.ShapeDtypeStruct((8, features), F32),
        ],
        scratch_shapes=[
            pltpu.VMEM((rows, features), F32),
            pltpu.VMEM(incoming.shape, BF16),
            pltpu.SemaphoreType.DMA((3,)),
            pltpu.SemaphoreType.DMA((3,)),
            pltpu.SemaphoreType.DMA((1,)),
        ],
        compiler_params=pltpu.CompilerParams(
            collective_id=7, has_side_effects=True, vmem_limit_bytes=56 * 1024 * 1024
        ),
    )(active, shrink, middle, incoming, gate, bias)


NORM_AT = 12
BACK_STEPS = NORM_AT + 5


def back_kernel(
    back_ref, second_ref, pre_ref, shrink_ref, expand_ref, middle_ref, branch_ref, incoming_ref, mixed_ref, weight_ref,
    scaling_ref, source_ref, expand_grad_ref, expand_sum_ref, middle_grad_ref, mixed_grad_ref, output_grad_ref, sums_ref,
    block_ref, total, slope, branch_back, *scratch
):
    step = pl.program_id(0)
    here = Here()
    reduce = Reduce(here, lambda member, core: source_ref.at[:, core, member], block_ref, *scratch)

    @pl.when(step == 0)
    def _():
        greet((here.at_x(), here.at_y(), here.at_core(), here.at_z(1), here.at_z(2), here.at_z(3)))
        sums_ref[...] = jnp.zeros_like(sums_ref)
        total[...] = jnp.zeros_like(total)

    steps = reduce.steps()
    for action, turn in zip(steps[:-1], (0, 2, 5, 5, 5, 5, 5, 11)):
        pl.when(step == turn)(action)

    @pl.when(step < NORM_AT)
    def _():
        def one(block, carry):
            rows = pl.ds(pl.multiple_of(block * MATMUL_ROWS, MATMUL_ROWS), MATMUL_ROWS)
            active_grad = dot_nt(back_ref[rows, :], shrink_ref[...])
            grad = (active_grad * gelu_parts(pre_ref[rows, :])[1]).astype(BF16)
            slope[rows, :] = grad
            total[rows, :] += dot_nt(grad, expand_ref[0])
            return carry

        lax.fori_loop(0, total.shape[0] // MATMUL_ROWS, one, 0)
        expand_sum_ref[0] = jnp.sum(slope[...].astype(F32), axis=0, keepdims=True)
        expand_grad_ref[0] = dot_tn(second_ref[...], slope[...]).astype(BF16)

    @pl.when((step >= NORM_AT) & (step < NORM_AT + 4))
    def _():
        rows = pl.ds(pl.multiple_of((step - NORM_AT) * 256, 256), 256)
        grad = total[rows, :]
        normed, inverse = norm_parts(middle_ref[...])
        sums_ref[1:2, :] += jnp.sum(grad, axis=0, keepdims=True)
        sums_ref[2:3, :] += jnp.sum(grad * normed, axis=0, keepdims=True)
        normed_grad = grad * (1.0 + scaling_ref[1])
        mean_first = jnp.mean(normed_grad, axis=-1, keepdims=True)
        mean_second = jnp.mean(normed_grad * normed, axis=-1, keepdims=True)
        middle_grad = incoming_ref[0].astype(F32) + inverse * (normed_grad - mean_first - normed * mean_second)
        middle_grad_ref[...] = middle_grad
        sums_ref[0:1, :] += jnp.sum(middle_grad * branch_ref[...], axis=0, keepdims=True)
        branch_grad = (scaling_ref[0] * middle_grad).astype(BF16)
        branch_back[rows, :] = branch_grad
        sums_ref[3:4, :] += jnp.sum(branch_grad.astype(F32), axis=0, keepdims=True)
        mixed_grad_ref[...] = dot_nt(branch_grad, weight_ref[0]).astype(BF16)

    @pl.when(step == BACK_STEPS - 1)
    def _():
        width = mixed_ref.shape[1] // 3
        for part in range(3):
            columns = slice(part * width, (part + 1) * width)
            output_grad_ref[columns, :] = dot_tn(mixed_ref[:, columns], branch_back[...]).astype(BF16)

    pl.when(step == BACK_STEPS - 1)(steps[-1])


def back(back_rows, second, pre, shrink, expand, middle, branch, incoming, mixed, weights, scalings, source):
    rows, features = middle.shape
    third = features // 3
    by_rows = pl.BlockSpec((256, features), lambda step: (clipped(step, NORM_AT, 3), 0))

    def piece(step):
        return jnp.minimum(step, NORM_AT - 1)

    wide = jax.ShapeDtypeStruct((rows, features), F32)
    return pl.pallas_call(
        back_kernel,
        grid=(BACK_STEPS,),
        in_specs=[
            everything((rows, features)),
            everything((rows, features)),
            pl.BlockSpec((rows, third), lambda step: (0, piece(step))),
            pl.BlockSpec((third, features), lambda step: (piece(step), 0)),
            pl.BlockSpec((1, features, third), lambda step: (piece(step) // 3, 0, piece(step) % 3)),
            by_rows,
            by_rows,
            pl.BlockSpec((1, 256, features), lambda step: (clipped(step, NORM_AT, 3), 0, 0)),
            everything((rows, features)),
            pl.BlockSpec((1, features, features), lambda step: (3, 0, 0), pipeline_mode=pl.Buffered(1)),
            everything((2, 1, features)),
            ANY,
        ],
        out_specs=[
            pl.BlockSpec((1, features, third), lambda step: (piece(step) // 3, 0, piece(step) % 3)),
            pl.BlockSpec((1, 1, third), lambda step: (piece(step), 0, 0)),
            by_rows,
            by_rows,
            everything((features, features)),
            everything((8, features)),
            everything((ROWS, features)),
        ],
        out_shape=[
            jax.ShapeDtypeStruct((4, features, features), BF16),
            jax.ShapeDtypeStruct((NORM_AT, 1, third), F32),
            wide,
            jax.ShapeDtypeStruct((rows, features), BF16),
            jax.ShapeDtypeStruct((features, features), BF16),
            jax.ShapeDtypeStruct((8, features), F32),
            jax.ShapeDtypeStruct((ROWS, features), F32),
        ],
        scratch_shapes=[
            pltpu.VMEM((rows, features), F32),
            pltpu.VMEM((rows, third), BF16),
            pltpu.VMEM((rows, features), BF16),
            *Reduce.SCRATCH,
        ],
        compiler_params=pltpu.CompilerParams(
            collective_id=8, has_side_effects=True, vmem_limit_bytes=60 * 1024 * 1024
        ),
    )(back_rows, second, pre, shrink, expand, middle, branch, incoming, mixed, weights, scalings, source)


class Shares:
    def __init__(self, here, block, pieces, target, wires, local):
        self.block, self.pieces = block, pieces
        self.copies = [
            wires.copy(
                step - 1,
                pieces.at[lax.rem(here.member + step, 4)],
                target.at[here.member],
                here.at_member(step),
            )
            for step in range(1, 4)
        ]
        self.copies.append(pltpu.make_async_copy(pieces.at[here.member], target.at[here.member], local))

    def start(self):
        for member in range(4):
            self.pieces[member, :36] = self.block[member * 36 : member * 36 + 36, :]
        for copy in self.copies:
            copy.start()

    def wait(self):
        for copy in self.copies:
            copy.wait()


def close_kernel(
    grad_ref, triple_ref, weight_ref, latent_ref, middle_ref, scale_ref, vector_ref, bias_ref, block_ref,
    total, tokens_ref, rows_ref, biases_ref, share_ref,
    pieces, triple, weight, latent, middle, token, wide, row, row_sent, row_landed, bias_sent, bias_landed,
    more_sent, more_landed, local, *scratch
):
    here = Here()
    features = latent_ref.shape[1]
    greet_all(here)
    reduce = Reduce(here, lambda member, core: grad_ref.at[member, :, core], total, *scratch)
    loads = [
        pltpu.make_async_copy(weight_ref.at[pl.ds(0, 3)], weight, local.at[0]),
        pltpu.make_async_copy(triple_ref, triple, local.at[1]),
        pltpu.make_async_copy(latent_ref, latent, local.at[2]),
        pltpu.make_async_copy(middle_ref, middle, local.at[3]),
    ]
    for copy in loads:
        copy.start()
    reduce.begin()
    bias_done = everyone(here, lambda place: bias_ref.at[place], biases_ref, bias_sent, bias_landed)
    own_bias = pltpu.make_async_copy(bias_ref.at[here.index], biases_ref.at[here.index], local.at[4])
    own_bias.start()
    wires = Wires(more_sent, more_landed)

    shares = Shares(here, block_ref, pieces, share_ref, Wires(more_sent.at[pl.ds(3, 3)], more_landed.at[pl.ds(3, 3)]), local.at[7])
    shares.start()

    def move(step):
        place = lax.rem(here.member + step, 4)
        return wires.copy(step - 1, token.at[place], tokens_ref.at[here.member], here.at_member(step))

    def compute(step):
        place = lax.rem(here.member + step, 4)
        rows = pl.ds(pl.multiple_of(place * 256, 256), 256)
        hidden_grad = dot_nt(triple[rows, :features], weight[0])
        hidden_grad += dot_nt(triple[rows, features : 2 * features], weight[1])
        hidden_grad += dot_nt(triple[rows, 2 * features :], weight[2])
        normed, inverse = norm_parts(latent[rows, :].astype(F32))
        shift = jnp.sum(hidden_grad, axis=0, keepdims=True)
        scale = jnp.sum(hidden_grad * normed, axis=0, keepdims=True)
        normed_grad = hidden_grad * (1.0 + scale_ref[...])
        mean_first = jnp.mean(normed_grad, axis=-1, keepdims=True)
        mean_second = jnp.mean(normed_grad * normed, axis=-1, keepdims=True)
        result = middle[rows, :] + inverse * (normed_grad - mean_first - normed * mean_second)
        token[place] = result.astype(BF16)
        return shift, scale

    for copy in loads:
        copy.wait()
    sums = [compute(2)]
    reduce.diagonal()
    sums.append(compute(1))
    reduce.direct_x()
    reduce.direct_y()
    reduce.keep_own()
    reduce.relay_x()
    reduce.relay_y()
    sums.append(compute(3))
    sums.append(compute(0))
    own = pltpu.make_async_copy(token.at[here.member], tokens_ref.at[here.member], local.at[5])
    own.start()
    wide[...] = vector_ref[...]
    for part in range(2):
        vector = sums[0][part] + sums[1][part] + sums[2][part] + sums[3][part]
        for tile in range(features // LANES):
            place = part * (features // LANES) + tile
            wide[place : place + 1, :] = vector[:, tile * LANES : (tile + 1) * LANES]
    row[...] = wide[...].astype(BF16)
    rows_done = everyone(here, lambda place: row, rows_ref, row_sent, row_landed)
    own_row = pltpu.make_async_copy(row, rows_ref.at[here.index], local.at[6])
    own_row.start()
    reduce.along_z()
    for step in (2, 1, 3):
        move(step).start()
    reduce.finish()
    shares.wait()
    for step in range(1, 4):
        move(step).wait()
    own.wait()
    own_bias.wait()
    own_row.wait()
    rows_done()
    bias_done()


def close_down(grad, triple, weight, latents, middle_grad, scale, vectors, bias, block):
    rows, features = latents.shape
    whole = pl.BlockSpec(memory_space=pltpu.VMEM)
    return pl.pallas_call(
        close_kernel,
        in_specs=[ANY] * 5 + [whole, whole, ANY, whole],
        out_specs=[whole, ANY, ANY, ANY, ANY],
        out_shape=[
            jax.ShapeDtypeStruct((ROWS, 1152), F32),
            jax.ShapeDtypeStruct((4, rows // 4, features), BF16),
            jax.ShapeDtypeStruct((32,) + vectors.shape, BF16),
            jax.ShapeDtypeStruct(bias.shape, bias.dtype),
            jax.ShapeDtypeStruct((4, 40, 1152), F32),
        ],
        scratch_shapes=[
            pltpu.VMEM((4, 40, 1152), F32),
            pltpu.VMEM(triple.shape, BF16),
            pltpu.VMEM((3, features, features), BF16),
            pltpu.VMEM(latents.shape, BF16),
            pltpu.VMEM(latents.shape, F32),
            pltpu.VMEM((4, rows // 4, features), BF16),
            pltpu.VMEM(vectors.shape, F32),
            pltpu.VMEM(vectors.shape, BF16),
        ]
        + [pltpu.SemaphoreType.DMA((32,))] * 4
        + [pltpu.SemaphoreType.DMA((6,))] * 2
        + [pltpu.SemaphoreType.DMA((8,))]
        + list(Reduce.SCRATCH),
        compiler_params=pltpu.CompilerParams(
            collective_id=3, has_side_effects=True, vmem_limit_bytes=60 * 1024 * 1024
        ),
    )(grad, triple, weight, latents, middle_grad, scale, vectors, bias, block)


def swap_kernel(part_ref, block_ref, parts_ref, share_ref, pieces, sent, landed, more_sent, more_landed, local):
    here = Here()
    greet_all(here)
    shares = Shares(here, block_ref, pieces, share_ref, Wires(more_sent, more_landed), local.at[1])
    done = everyone(here, lambda place: part_ref.at[place // 4], parts_ref, sent, landed)
    own = pltpu.make_async_copy(part_ref.at[here.group], parts_ref.at[here.index], local.at[0])
    own.start()
    shares.start()
    shares.wait()
    own.wait()
    done()


def swap(parts, block):
    return pl.pallas_call(
        swap_kernel,
        in_specs=[ANY, pl.BlockSpec(memory_space=pltpu.VMEM)],
        out_specs=[ANY, ANY],
        out_shape=[
            jax.ShapeDtypeStruct((32,) + parts.shape[1:], parts.dtype),
            jax.ShapeDtypeStruct((4, 40, 1152), F32),
        ],
        scratch_shapes=[
            pltpu.VMEM((4, 40, 1152), F32),
            pltpu.SemaphoreType.DMA((32,)),
            pltpu.SemaphoreType.DMA((32,)),
            pltpu.SemaphoreType.DMA((3,)),
            pltpu.SemaphoreType.DMA((3,)),
            pltpu.SemaphoreType.DMA((2,)),
        ],
        compiler_params=pltpu.CompilerParams(collective_id=4, has_side_effects=True),
    )(parts, block)


def pad_lanes(values, width):
    return jnp.pad(values, ((0, 0), (0, width - values.shape[1])))


def on_device_fast(
    latents,
    condition,
    cotangent,
    modulate_weight,
    modulate_bias,
    triple_weight,
    triple_bias,
    output_weight,
    output_bias,
    expand_weight,
    expand_bias,
    shrink_weight,
    shrink_bias,
):
    micro, local, tokens, features = latents.shape
    devices = 32
    me = lax.axis_index("dp") * 4 + lax.axis_index("seq")
    hidden = expand_weight.shape[1]
    shard = jnp.stack([jnp.concatenate([triple_weight, output_weight], axis=1), expand_weight])
    shard = jnp.pad(shard, ((0, 0), (0, 12), (0, 0)))
    own_cond = lax.dynamic_index_in_dim(condition.reshape(4, features), lax.axis_index("seq"), axis=0, keepdims=False)
    biases = (modulate_bias, triple_bias, output_bias, expand_bias, shrink_bias)
    note = jnp.concatenate([own_cond, *biases]).astype(F32)
    note = jnp.pad(note, (0, 1664 - note.shape[0])).reshape(1, 1, 1664)
    notes, blocks, shrink_quad = introduce(note, shard, shrink_weight)
    notes = notes.reshape(32, 1664)
    cond_act = jax.nn.silu(notes[:, :features]).astype(BF16)
    cuts = []
    offset = features
    for bias in biases:
        cuts.append(notes[:, offset : offset + bias.shape[0]].reshape(-1))
        offset += bias.shape[0]
    modulate_offset, triple_offset, output_offset, expand_offset, shrink_offset = cuts
    owned = modulate_weight.shape[0]
    act_owned = lax.dynamic_slice_in_dim(cond_act, me * owned, owned, axis=1)
    parts = pad_lanes(dot_nn(act_owned, modulate_weight), 56 * LANES).reshape(4, 2, 4, 56, LANES)
    parts = jnp.swapaxes(parts, 0, 1).reshape(2, 16, 56, LANES)
    first_full, expand_column, parts, token_rows = open_up(
        blocks, parts, latents.reshape(4, tokens, features)
    )
    first_full = first_full.reshape(4, features, features)
    modulation = jnp.sum(parts, axis=0).reshape(-1)[: 6 * features] + modulate_offset
    shift_one, scale_one, gate_one, shift_two, scale_two, gate_two = jnp.split(modulation[None, :], 6, axis=-1)

    token_rows = token_rows.reshape(4 * tokens, features)
    latent_float = token_rows.astype(F32)
    normed_one, inverse_one = norm_parts(latent_float)
    hidden_one = (normed_one * (1.0 + scale_one) + shift_one).astype(BF16)
    zero = jnp.zeros((features,), F32)
    first_bias = jnp.stack(
        [triple_offset[:features], zero, triple_offset[features:], output_offset]
    ).reshape(4, 1, features)
    output_full = first_full[3]
    (
        projected,
        mixed,
        log_total,
        branch_one,
        middle,
        hidden_two,
        pre_act,
        activated,
        expand_full,
        shrink_full,
        incoming,
    ) = forward(
        hidden_one,
        first_full,
        first_bias,
        token_rows,
        jnp.stack([gate_one, shift_two, scale_two]),
        expand_offset.reshape(4, 1, features),
        expand_column,
        shrink_quad,
        cotangent.reshape(4, tokens, features),
    )
    expand_full = expand_full.reshape(4, features, features)
    shrink_full = shrink_full.reshape(hidden, features)
    output, back_rows, shrink_grad, turn_sums = turn(
        activated, shrink_full, middle, incoming, gate_two, shrink_offset[None]
    )
    expand_grad, expand_offset_grad, middle_grad, mixed_grad, output_grad, back_sums, shrink_total = back(
        back_rows,
        hidden_two,
        pre_act,
        shrink_full,
        expand_full,
        middle,
        branch_one,
        incoming,
        mixed,
        first_full,
        jnp.stack([gate_one, scale_two]),
        shrink_grad.reshape(4, 2, 4, ROWS, features),
    )
    expand_grad = expand_grad.reshape(4, 4, 2, ROWS, features)
    gate_two_grad, shrink_offset_grad = turn_sums[0], turn_sums[1]
    gate_one_grad, output_offset_grad = back_sums[0], back_sums[3]
    triple_rows, expand_block = attend_backward_reduce(projected, mixed_grad, log_total, expand_grad)
    column_sums = jnp.sum(triple_rows.astype(F32), axis=0)
    triple_offset_grad = jnp.concatenate([column_sums[:features], column_sums[2 * features :]])
    first_grad = jnp.stack(
        [dot_tn(hidden_one, triple_rows[:, part * features : (part + 1) * features]).astype(BF16) for part in range(3)]
        + [output_grad]
    ).reshape(4, 4, 2, ROWS, features)
    vectors = jnp.concatenate(
        [
            jnp.zeros((2 * features,), F32),
            gate_one_grad,
            back_sums[1],
            back_sums[2],
            gate_two_grad,
            jnp.zeros((64 * LANES - 6 * features,), F32),
        ]
    ).reshape(64, LANES)
    bias_grads = jnp.concatenate(
        [
            values.reshape(devices, -1)
            for values in (triple_offset_grad, output_offset_grad, expand_offset_grad, shrink_offset_grad)
        ],
        axis=1,
    )
    bias_grads = pad_lanes(bias_grads, 1024).reshape(32, 8, LANES)
    first_block, token_grad, all_grads, bias_parts, expand_share = close_down(
        first_grad, triple_rows, first_full, token_rows, middle_grad, scale_one, vectors, bias_grads, expand_block
    )
    all_grads = all_grads.reshape(32, 8192)[:, : 6 * features]
    modulate_total = dot_tn(act_owned, all_grads)
    width = modulate_bias.shape[0]
    modulate_offset_total = jnp.sum(
        lax.dynamic_slice_in_dim(all_grads, me * width, width, axis=1).astype(F32), axis=0
    )
    cond_back = dot_nt(all_grads, modulate_weight)
    cond_back = jnp.pad(cond_back.reshape(8, 4, owned), ((0, 0), (0, 4), (0, LANES - owned)))
    cond_back, first_share = swap(cond_back, first_block)
    cond_back = cond_back[:, :4, :owned]
    cond_back = jnp.swapaxes(cond_back, 0, 1).reshape(condition.shape)
    cond_float = condition.astype(F32)
    sigmoid_cond = jax.nn.sigmoid(cond_float)
    condition_gradient = cond_back * (sigmoid_cond * (1.0 + cond_float * (1.0 - sigmoid_cond)))
    bias_total = jnp.sum(bias_parts.reshape(32, 1024), axis=0)
    bias_cuts = []
    offset = 0
    for bias in biases[1:]:
        bias_cuts.append(bias_total[offset : offset + bias.shape[0]])
        offset += bias.shape[0]
    first_share = first_share[:, :owned]
    expand_total = jnp.swapaxes(expand_share[:, :owned], 0, 1).reshape(expand_weight.shape)
    return (
        output.reshape(latents.shape),
        token_grad.reshape(latents.shape).astype(F32),
        condition_gradient,
        modulate_total,
        modulate_offset_total,
        jnp.concatenate([first_share[0], first_share[1], first_share[2]], axis=1),
        bias_cuts[0],
        first_share[3],
        bias_cuts[1],
        expand_total,
        bias_cuts[2],
        shrink_total,
        bias_cuts[3],
    )


def solution(mesh):
    tokens = P(None, "dp", "seq", None)
    conditions = P(None, "dp", None)
    weight = P(AXES, None)
    bias = P(AXES)
    parameters = (weight, bias) * 5
    fast = mesh.shape["dp"] == 8 and mesh.shape["seq"] == 4
    return jax.shard_map(
        on_device_fast if fast else on_device,
        mesh=mesh,
        in_specs=(tokens, conditions, tokens) + parameters,
        out_specs=(tokens, tokens, conditions) + parameters,
        check_vma=False,
    )
```

```python
import functools

import jax
import jax.numpy as jnp
from jax import lax
from jax.experimental import pallas as pl
from jax.experimental.pallas import tpu as pltpu
from jax.sharding import PartitionSpec as P

HEADS = 16
HD = 72
LANES = 128
WINDOW = 256
QUERY_BLOCK = 256

EPSILON = 1e-06
GELU_COEF = 0.7978845608028654
CUBIC = 0.044715
LOG2E = 1.4426950408889634
AXES = ("dp", "seq")
F32 = jnp.float32
BF16 = jnp.bfloat16


def gelu_parts(values):
    square = values * values
    tangent = jnp.tanh(GELU_COEF * values * (1.0 + CUBIC * square))
    half = 0.5 * (1.0 + tangent)
    slope = half + (0.5 * GELU_COEF) * values * (1.0 - tangent * tangent) * (1.0 + 3.0 * CUBIC * square)
    return (values * half, slope)


def norm_parts(values):
    centered = values - jnp.mean(values, axis=-1, keepdims=True)
    variance = jnp.mean(centered * centered, axis=-1, keepdims=True)
    inverse = lax.rsqrt(variance + EPSILON)
    return (centered * inverse, inverse)


def norm_back(incoming, normed, inverse, scaling):
    shift_grad = jnp.sum(incoming, axis=1)
    scale_grad = jnp.sum(incoming * normed, axis=1)
    normed_grad = incoming * (1.0 + scaling)
    mean_first = jnp.mean(normed_grad, axis=-1, keepdims=True)
    mean_second = jnp.mean(normed_grad * normed, axis=-1, keepdims=True)
    return (inverse * (normed_grad - mean_first - normed * mean_second), shift_grad, scale_grad)


def dot_nt(left, right):
    return lax.dot_general(left, right, (((1,), (1,)), ((), ())), preferred_element_type=F32)


def dot_tn(left, right):
    return lax.dot_general(left, right, (((0,), (0,)), ((), ())), preferred_element_type=F32)


def dot_nn(left, right):
    return jnp.dot(left, right, preferred_element_type=F32)


def head_window(features):
    head = pl.program_id(0)
    last = features // LANES - WINDOW // LANES
    tile = jnp.minimum(head * HD // LANES, last)
    start = pl.multiple_of(tile * LANES, LANES)
    first = head * HD - start
    lane = lax.broadcasted_iota(jnp.int32, (1, WINDOW), 1)
    return start, (lane >= first) & (lane < first + HD)


def attend_forward_kernel(query_ref, key_ref, value_ref, mixed_ref, log_ref):
    features = query_ref.shape[1]
    start, inside = head_window(features)
    window = pl.ds(start, WINDOW)
    keys = jnp.where(inside, key_ref[:, window], 0)
    values = jnp.where(inside, value_ref[:, window], 0)
    factor = HD**-0.5 * LOG2E
    for block in range(query_ref.shape[0] // QUERY_BLOCK):
        rows = pl.ds(block * QUERY_BLOCK, QUERY_BLOCK)
        scores = dot_nt(keys, query_ref[rows, window])
        peak = jnp.max(scores, axis=0, keepdims=True)
        powers = jnp.exp2((scores - peak) * factor)
        total = jnp.sum(powers, axis=0, keepdims=True)
        log_ref[0, :, rows] = peak * factor + jnp.log2(total)
        weights = (powers * (1.0 / total)).astype(BF16)
        mixed = dot_tn(values, weights).T.astype(BF16)
        mixed_ref[rows, window] = jnp.where(inside, mixed, mixed_ref[rows, window])


def attend_backward_kernel(
    query_ref, key_ref, value_ref, incoming_ref, log_ref, grad_ref, score_grads, weights
):
    features = query_ref.shape[1]
    start, inside = head_window(features)
    window = pl.ds(start, WINDOW)
    keys = jnp.where(inside, key_ref[:, window], 0)
    values = jnp.where(inside, value_ref[:, window], 0)
    scale = HD**-0.5
    factor = scale * LOG2E
    count = query_ref.shape[0] // QUERY_BLOCK
    turned = keys.T

    def begin(block):
        rows = pl.ds(block * QUERY_BLOCK, QUERY_BLOCK)
        return dot_nt(keys, query_ref[rows, window]), dot_nt(values, incoming_ref[rows, window])

    following = begin(0)
    for block in range(count):
        rows = pl.ds(block * QUERY_BLOCK, QUERY_BLOCK)
        scores, prob_grad = following
        if block + 1 < count:
            following = begin(block + 1)
        probs = jnp.exp2(scores * factor - log_ref[0, :, rows])
        centre = jnp.sum(probs * prob_grad, axis=0, keepdims=True)
        score_grads[:, rows] = (probs * (prob_grad - centre) * scale).astype(BF16)
        weights[:, rows] = probs.astype(BF16)
        query_grad = dot_nn(turned, score_grads[:, rows]).T.astype(grad_ref.dtype)
        grad_ref[rows, window] = jnp.where(inside, query_grad, grad_ref[rows, window])
    key_total = dot_nn(score_grads[...], query_ref[:, window])
    value_total = dot_nn(weights[...], incoming_ref[:, window])
    for part, total in ((1, key_total), (2, value_total)):
        place = pl.ds(pl.multiple_of(start + part * features, LANES), WINDOW)
        grad_ref[:, place] = jnp.where(inside, total.astype(grad_ref.dtype), grad_ref[:, place])


def whole_block(shape, column):
    return pl.BlockSpec(shape, lambda head: (0, column), pipeline_mode=pl.Buffered(1))


def attend_forward(projected, everyone):
    rows = projected.shape[0]
    features = projected.shape[1] // 3
    tokens = everyone.shape[0]
    return pl.pallas_call(
        attend_forward_kernel,
        grid=(HEADS,),
        in_specs=[
            whole_block((rows, features), 0),
            whole_block((tokens, features), 1),
            whole_block((tokens, features), 2),
        ],
        out_specs=[
            whole_block((rows, features), 0),
            pl.BlockSpec((1, 1, rows), lambda head: (head, 0, 0)),
        ],
        out_shape=[
            jax.ShapeDtypeStruct((rows, features), BF16),
            jax.ShapeDtypeStruct((HEADS, 1, rows), F32),
        ],
        compiler_params=pltpu.CompilerParams(vmem_limit_bytes=56 * 1024 * 1024),
        cost_estimate=pl.CostEstimate(
            flops=4 * rows * tokens * HEADS * WINDOW,
            bytes_accessed=2 * (rows * 2 + tokens * 2) * features,
            transcendentals=rows * tokens * HEADS,
        ),
    )(projected, everyone, everyone)


def attend_backward(projected, everyone, incoming, log_total):
    rows = projected.shape[0]
    features = projected.shape[1] // 3
    tokens = everyone.shape[0]
    kind = BF16 if rows == tokens else F32
    return pl.pallas_call(
        attend_backward_kernel,
        grid=(HEADS,),
        in_specs=[
            whole_block((rows, features), 0),
            whole_block((tokens, features), 1),
            whole_block((tokens, features), 2),
            whole_block((rows, features), 0),
            pl.BlockSpec((1, 1, rows), lambda head: (head, 0, 0)),
        ],
        out_specs=whole_block((tokens, 3 * features), 0),
        out_shape=jax.ShapeDtypeStruct((tokens, 3 * features), kind),
        scratch_shapes=[pltpu.VMEM((tokens, rows), BF16), pltpu.VMEM((tokens, rows), BF16)],
        compiler_params=pltpu.CompilerParams(vmem_limit_bytes=56 * 1024 * 1024),
        cost_estimate=pl.CostEstimate(
            flops=10 * rows * tokens * HEADS * WINDOW,
            bytes_accessed=2 * (rows * 2 + tokens * 5) * features,
            transcendentals=rows * tokens * HEADS,
        ),
    )(projected, everyone, everyone, incoming, log_total)


class Layout:
    def __init__(self, micro, local, tokens, seq):
        self.micro, self.local, self.tokens, self.seq = micro, local, tokens, seq
        self.latents = micro * local
        self.sharers = max(1, seq // self.latents)
        self.held = max(1, self.latents // seq)
        self.span = seq // self.sharers

    def gather(self, values):
        values = values.reshape(self.latents, self.tokens, values.shape[-1])
        if self.sharers > 1:
            values = jnp.repeat(values, self.sharers, axis=0)
        moved = lax.all_to_all(values, "seq", split_axis=0, concat_axis=1, tiled=True)
        if self.sharers > 1:
            part = lax.axis_index("seq") % self.sharers
            count = self.span * self.tokens
            moved = lax.dynamic_slice_in_dim(moved, part * count, count, axis=1)
        return moved

    def scatter(self, values):
        if self.sharers > 1:
            values = jnp.concatenate([values] * self.sharers, axis=1)
        moved = lax.all_to_all(values, "seq", split_axis=1, concat_axis=0, tiled=True)
        if self.sharers > 1:
            part = lax.axis_index("seq") // self.span
            moved = moved.reshape(self.latents, self.sharers, self.tokens, values.shape[-1])
            moved = lax.dynamic_index_in_dim(moved, part, axis=1, keepdims=False)
        return moved.reshape(self.micro, self.local, self.tokens, values.shape[-1])

    def own_group(self, values, axis):
        if self.sharers == self.seq:
            return values
        count = values.shape[axis] // self.seq * self.sharers
        return lax.dynamic_slice_in_dim(
            values, lax.axis_index("seq") // self.sharers * count, count, axis=axis
        )


def on_device(
    latents,
    condition,
    cotangent,
    modulate_weight,
    modulate_bias,
    triple_weight,
    triple_bias,
    output_weight,
    output_bias,
    expand_weight,
    expand_bias,
    shrink_weight,
    shrink_bias,
):
    micro, local, tokens, features = latents.shape
    hidden = expand_weight.shape[1]
    groups = lax.axis_size("dp")
    seq = lax.axis_size("seq")
    devices = groups * seq
    place = Layout(micro, local, tokens, seq)
    held = place.held
    me = lax.axis_index("dp") * seq + lax.axis_index("seq")

    everyone_cond = lax.all_gather(condition.reshape(micro * local, features), "dp", axis=0, tiled=True)
    bias_shard = jnp.concatenate([modulate_bias, triple_bias, output_bias, expand_bias, shrink_bias])
    biases = lax.all_gather(bias_shard, AXES, axis=0, tiled=False).astype(F32)
    cuts = []
    offset = 0
    for shard in (modulate_bias, triple_bias, output_bias, expand_bias, shrink_bias):
        cuts.append(biases[:, offset : offset + shard.shape[0]].reshape(-1))
        offset += shard.shape[0]
    modulate_offset, triple_offset, output_offset, expand_offset, shrink_offset = cuts

    latent_rows = place.gather(latents)
    first_shard = jnp.concatenate([triple_weight, output_weight], axis=1)
    first_full = lax.all_gather(first_shard, AXES, axis=0, tiled=True)
    triple_full = first_full[:, : 3 * features]
    output_full = first_full[:, 3 * features :]
    expand_full = lax.all_gather(expand_weight, AXES, axis=0, tiled=True)
    shrink_full = lax.all_gather(shrink_weight, AXES, axis=0, tiled=True)

    owned = modulate_weight.shape[0]
    cond_act = jax.nn.silu(everyone_cond.astype(F32)).astype(BF16)
    act_owned = lax.dynamic_slice_in_dim(cond_act, me * owned, owned, axis=1)
    modulation_part = dot_nn(act_owned, modulate_weight)
    if place.sharers > 1:
        modulation_part = jnp.repeat(modulation_part, place.sharers, axis=0)
    modulation_parts = lax.all_to_all(modulation_part, AXES, split_axis=0, concat_axis=0, tiled=True)
    modulation = jnp.sum(modulation_parts.reshape(devices, held, -1), axis=0) + modulate_offset
    shift_one, scale_one, gate_one, shift_two, scale_two, gate_two = jnp.split(
        modulation[:, None, :], 6, axis=-1
    )

    latent_float = latent_rows.astype(F32)
    normed_one, inverse_one = norm_parts(latent_float)
    hidden_one = (normed_one * (1.0 + scale_one) + shift_one).astype(BF16)
    rows = held * latent_rows.shape[1]

    def flat(values):
        return values.reshape(rows, values.shape[-1])

    def unflat(values):
        return values.reshape(held, rows // held, values.shape[-1])

    zero = jnp.zeros((features,), F32)
    full_bias = jnp.concatenate([triple_offset[:features], zero, triple_offset[features:]])
    projected = unflat((dot_nn(flat(hidden_one), triple_full) + full_bias).astype(BF16))
    if place.sharers > 1:
        everyone = place.own_group(lax.all_gather(projected, "seq", axis=1, tiled=True), 1)
    else:
        everyone = projected
    mixed_parts, log_parts = zip(
        *(attend_forward(projected[index], everyone[index]) for index in range(held))
    )
    mixed = jnp.stack(mixed_parts) if held > 1 else mixed_parts[0][None]
    branch_one = unflat(dot_nn(flat(mixed), output_full)) + output_offset
    middle = latent_float + gate_one * branch_one
    normed_two, inverse_two = norm_parts(middle)
    hidden_two = (normed_two * (1.0 + scale_two) + shift_two).astype(BF16)
    pre_act = dot_nn(flat(hidden_two), expand_full) + expand_offset
    activated = gelu_parts(pre_act)[0].astype(BF16)
    branch_two = unflat(dot_nn(activated, shrink_full)) + shrink_offset
    output = place.scatter((middle + gate_two * branch_two).astype(BF16))

    incoming = place.gather(cotangent).astype(F32)
    branch_two_grad = (gate_two * incoming).astype(BF16)
    gate_two_grad = jnp.sum(incoming * branch_two, axis=1)
    shrink_offset_grad = jnp.sum(branch_two_grad.astype(F32), axis=(0, 1))
    shrink_grad = dot_tn(activated, flat(branch_two_grad)).astype(BF16)
    shrink_total = lax.psum_scatter(shrink_grad, AXES, scatter_dimension=0, tiled=True).astype(F32)
    act_grad = dot_nt(flat(branch_two_grad), shrink_full)
    pre_grad = (act_grad * gelu_parts(pre_act)[1]).astype(BF16)
    expand_offset_grad = jnp.sum(pre_grad.astype(F32), axis=0)
    expand_grad = dot_tn(flat(hidden_two), pre_grad).astype(BF16)
    expand_total = scatter_rows(expand_grad, devices)
    hidden_two_grad = unflat(dot_nt(pre_grad, expand_full))
    norm_grad_two, shift_two_grad, scale_two_grad = norm_back(
        hidden_two_grad, normed_two, inverse_two, scale_two
    )
    middle_grad = incoming + norm_grad_two
    branch_one_grad = (gate_one * middle_grad).astype(BF16)
    gate_one_grad = jnp.sum(middle_grad * branch_one, axis=1)
    output_offset_grad = jnp.sum(branch_one_grad.astype(F32), axis=(0, 1))
    output_grad = dot_tn(flat(mixed), flat(branch_one_grad)).astype(BF16)
    mixed_grad = unflat(dot_nt(flat(branch_one_grad), output_full).astype(BF16))
    grads = []
    for index in range(held):
        grad = attend_backward(projected[index], everyone[index], mixed_grad[index], log_parts[index])
        if place.sharers > 1:
            key_value = grad[:, features:]
            key_value = lax.psum_scatter(
                own_slots(key_value, place), "seq", scatter_dimension=0, tiled=True
            ).astype(BF16)
            grad = jnp.concatenate([grad[: rows // held, :features].astype(BF16), key_value], axis=1)
        grads.append(grad)
    triple_rows = jnp.concatenate(grads) if held > 1 else grads[0]
    column_sums = jnp.sum(triple_rows.astype(F32), axis=0)
    triple_offset_grad = jnp.concatenate([column_sums[:features], column_sums[2 * features :]])
    triple_grad = dot_tn(flat(hidden_one), triple_rows).astype(BF16)
    first_grad = jnp.concatenate([triple_grad, output_grad], axis=1)
    first_total = scatter_rows(first_grad, devices)
    hidden_one_grad = unflat(dot_nt(triple_rows, triple_full))
    norm_grad_one, shift_one_grad, scale_one_grad = norm_back(
        hidden_one_grad, normed_one, inverse_one, scale_one
    )
    latents_gradient = place.scatter((middle_grad + norm_grad_one).astype(BF16)).astype(F32)

    modulation_grad = jnp.concatenate(
        [shift_one_grad, scale_one_grad, gate_one_grad, shift_two_grad, scale_two_grad, gate_two_grad],
        axis=-1,
    )
    if place.sharers > 1:
        parts = lax.all_gather(modulation_grad, "seq", axis=0, tiled=True)
        modulation_grad = jnp.sum(place.own_group(parts, 0), axis=0, keepdims=True)
    all_grads = lax.all_gather(modulation_grad.astype(BF16), AXES, axis=0, tiled=True)
    if place.sharers > 1:
        all_grads = all_grads[:: place.sharers]
    modulate_total = dot_tn(act_owned, all_grads)
    shard = modulate_bias.shape[0]
    modulate_offset_total = jnp.sum(
        lax.dynamic_slice_in_dim(all_grads, me * shard, shard, axis=1).astype(F32), axis=0
    )
    cond_back = dot_nt(all_grads, modulate_weight)
    everyone_back = lax.all_gather(cond_back, AXES, axis=1, tiled=True)
    group_back = lax.dynamic_slice_in_dim(
        everyone_back, lax.axis_index("dp") * micro * local, micro * local, axis=0
    ).reshape(condition.shape)
    cond_float = condition.astype(F32)
    sigmoid_cond = jax.nn.sigmoid(cond_float)
    condition_gradient = group_back * (sigmoid_cond * (1.0 + cond_float * (1.0 - sigmoid_cond)))

    bias_grads = jnp.concatenate(
        [
            values.reshape(devices, -1)
            for values in (triple_offset_grad, output_offset_grad, expand_offset_grad, shrink_offset_grad)
        ],
        axis=1,
    )
    bias_total = jnp.sum(
        lax.all_to_all(bias_grads, AXES, split_axis=0, concat_axis=0, tiled=True), axis=0
    )
    bias_cuts = []
    offset = 0
    for part in (triple_bias, output_bias, expand_bias, shrink_bias):
        bias_cuts.append(bias_total[offset : offset + part.shape[0]])
        offset += part.shape[0]
    return (
        output,
        latents_gradient,
        condition_gradient,
        modulate_total,
        modulate_offset_total,
        first_total[:, : 3 * features],
        bias_cuts[0],
        first_total[:, 3 * features :],
        bias_cuts[1],
        expand_total,
        bias_cuts[2],
        shrink_total,
        bias_cuts[3],
    )


def scatter_rows(values, devices):
    rows, columns = values.shape
    slots = values.reshape(rows * columns // 1152, 1152)
    total = lax.psum_scatter(slots, AXES, scatter_dimension=0, tiled=True)
    return total.reshape(rows // devices, columns).astype(F32)


def own_slots(values, place):
    group = lax.axis_index("seq") // place.sharers
    slots = jnp.zeros((place.seq // place.sharers,) + values.shape, values.dtype)
    slots = lax.dynamic_update_index_in_dim(slots, values, group, axis=0)
    return slots.reshape(-1, values.shape[-1])


MESH = pl.DeviceIdType.MESH
ANY = pl.BlockSpec(memory_space=pl.ANY)
ROWS = 144
MATMUL_ROWS = 1024
LOW, HIGH = pl.ds(0, 80), pl.ds(80, 64)


class Here:
    def __init__(self):
        dp, self.member = lax.axis_index("dp"), lax.axis_index("seq")
        self.group = dp
        self.z, self.core = dp // 2, dp % 2
        self.index = dp * 4 + self.member
        y, x = self.member // 2, self.member % 2
        self.across_x = y * 2 + (1 - x)
        self.across_y = (1 - y) * 2 + x
        self.across = (1 - y) * 2 + (1 - x)

    def at_x(self):
        return (self.group, self.across_x)

    def at_y(self):
        return (self.group, self.across_y)

    def at_core(self):
        return (self.z * 2 + (1 - self.core), self.member)

    def at_z(self, step):
        return (lax.rem(self.z + step, 4) * 2 + self.core, self.member)

    def at_member(self, step):
        return (self.group, lax.rem(self.member + step, 4))

    def at_index(self, step):
        place = lax.rem(self.index + step, 32)
        return (place // 4, lax.rem(place, 4))


def greet(partners):
    barrier = pltpu.get_barrier_semaphore()
    for partner in partners:
        pl.semaphore_signal(barrier, inc=1, device_id=partner, device_id_type=MESH)
    pl.semaphore_wait(barrier, len(partners))


def greet_all(here):
    barrier = pltpu.get_barrier_semaphore()

    def signal(step, carry):
        pl.semaphore_signal(barrier, inc=1, device_id=here.at_index(step), device_id_type=MESH)
        return carry

    lax.fori_loop(1, 32, signal, 0)
    pl.semaphore_wait(barrier, 31)


class Wires:
    def __init__(self, sent, landed):
        self.sent, self.landed = sent, landed

    def copy(self, number, source, target, partner):
        return pltpu.make_async_remote_copy(
            src_ref=source,
            dst_ref=target,
            send_sem=self.sent.at[number],
            recv_sem=self.landed.at[number],
            device_id=partner,
            device_id_type=MESH,
        )


def everyone(here, source_of, target, sent, landed):
    def copy_of(step):
        place = lax.rem(here.index + step, 32)
        return pltpu.make_async_remote_copy(
            src_ref=source_of(place),
            dst_ref=target.at[here.index],
            send_sem=sent.at[step],
            recv_sem=landed.at[step],
            device_id=here.at_index(step),
            device_id_type=MESH,
        )

    def start(step, carry):
        copy_of(step).start()
        return carry

    def wait(step, carry):
        copy_of(step).wait()
        return carry

    lax.fori_loop(1, 32, start, 0)
    return lambda: lax.fori_loop(1, 32, wait, 0)


def same_core(here, source, target, sent, landed):
    mine = here.z * 4 + here.member

    def copy_of(step):
        place = lax.rem(mine + step, 16)
        return pltpu.make_async_remote_copy(
            src_ref=source.at[place],
            dst_ref=target.at[mine],
            send_sem=sent.at[step],
            recv_sem=landed.at[step],
            device_id=(place // 4 * 2 + here.core, lax.rem(place, 4)),
            device_id_type=MESH,
        )

    def start(step, carry):
        copy_of(step).start()
        return carry

    def wait(step, carry):
        copy_of(step).wait()
        return carry

    lax.fori_loop(1, 16, start, 0)
    return lambda: lax.fori_loop(1, 16, wait, 0)


def introduce_kernel(
    note_ref, shard_ref, shrink_ref, notes_ref, blocks_ref, quad_ref, column_ref, landing, wide, buffer,
    note_sent, note_landed, sent, landed, local,
):
    here = Here()
    greet_all(here)
    wires = Wires(sent, landed)

    def columns(place):
        return shard_ref.at[:, :, pl.ds(pl.multiple_of(place * 1152, LANES), 1152)]

    quads = []
    for step in range(1, 4):
        place = lax.rem(here.member + step, 4)
        quads.append(wires.copy(step - 1, columns(place), landing.at[here.member], here.at_member(step)))
    highs = [
        wires.copy(2 + step, shrink_ref.at[HIGH], quad_ref.at[here.member], here.at_member(step))
        for step in range(1, 4)
    ]
    lows = [
        wires.copy(5 + step, shrink_ref.at[LOW], column_ref.at[here.z], here.at_z(step)) for step in range(1, 4)
    ]
    for copy in quads + lows:
        copy.start()
    keeps = [
        Bounce(shrink_ref.at[LOW], buffer.at[LOW], column_ref.at[here.z], local.at[2]),
        Bounce(shrink_ref.at[HIGH], buffer.at[HIGH], quad_ref.at[here.member], local.at[3]),
    ]
    for keep in keeps:
        keep.start()
    done = everyone(here, lambda place: note_ref.at[0], notes_ref, note_sent, note_landed)
    own = pltpu.make_async_copy(columns(here.member), landing.at[here.member], local.at[0])
    own.start()
    mine = pltpu.make_async_copy(note_ref.at[0], notes_ref.at[here.index], local.at[1])
    mine.start()
    for copy in highs:
        copy.start()
    own.wait()
    for keep in keeps:
        keep.go_on()
    for copy in quads:
        copy.wait_recv()
    for part in range(2):
        for member in range(4):
            wide[member * 36 : member * 36 + 36, :] = landing[member, part].astype(F32)[:36]
        blocks_ref[part] = wide[...].astype(BF16)
    for copy in quads:
        copy.wait_send()
    for copy in highs + lows + keeps:
        copy.wait()
    mine.wait()
    done()


def introduce(note, shard, shrink):
    return pl.pallas_call(
        introduce_kernel,
        in_specs=[ANY, ANY, ANY],
        out_specs=[ANY, pl.BlockSpec(memory_space=pltpu.VMEM), ANY, ANY],
        out_shape=[
            jax.ShapeDtypeStruct((32,) + note.shape[1:], note.dtype),
            jax.ShapeDtypeStruct((2, ROWS, 1152), BF16),
            jax.ShapeDtypeStruct((4, HIGH.size, 1152), BF16),
            jax.ShapeDtypeStruct((4, LOW.size, 1152), BF16),
        ],
        scratch_shapes=[
            pltpu.VMEM((4,) + shard.shape[:2] + (1152,), BF16),
            pltpu.VMEM((ROWS, 1152), F32),
            pltpu.VMEM((ROWS, 1152), BF16),
            pltpu.SemaphoreType.DMA((32,)),
            pltpu.SemaphoreType.DMA((32,)),
            pltpu.SemaphoreType.DMA((9,)),
            pltpu.SemaphoreType.DMA((9,)),
            pltpu.SemaphoreType.DMA((4,)),
        ],
        compiler_params=pltpu.CompilerParams(collective_id=1, has_side_effects=True),
    )(note, shard, shrink)


class Bounce:
    def __init__(self, source, buffer, target, semaphore):
        self.first = pltpu.make_async_copy(source, buffer, semaphore)
        self.second = pltpu.make_async_copy(buffer, target, semaphore)

    def start(self):
        self.first.start()

    def go_on(self):
        self.first.wait()
        self.second.start()

    def wait(self):
        self.second.wait()


ARRIVALS = (0, 1, 3, 2)


class Gather:
    COPIES = 31

    def __init__(self, here, place, own, sent, landed):
        self.here, self.place, self.own = here, place, own
        self.wires = Wires(sent, landed)

    def z_of(self, order):
        return lax.rem(self.here.z + 4 - ARRIVALS[order], 4)

    def along(self, step, block):
        here = self.here
        return self.wires.copy(step - 1, block, self.own(here.z), here.at_z(step))

    def begin(self, block):
        for step in (1, 3, 2):
            self.along(step, block).start()

    def sideways(self, kind, order):
        here = self.here
        z = self.z_of(order)
        partner = (here.at_x, here.at_y, here.at_core)[kind]()
        return self.wires.copy(
            3 + kind * 4 + order, self.own(z), self.place(here.member, z, here.core), partner
        )

    def passed(self, kind, order):
        here = self.here
        z = self.z_of(order)
        if kind == 3:
            member = here.across_x if order >= 2 else here.across_y
            partner = here.at_y() if order >= 2 else here.at_x()
        else:
            member = (here.across_x, here.across_y, here.across)[kind]
            partner = here.at_core()
        ref = self.place(member, z, here.core)
        return self.wires.copy(15 + kind * 4 + order, ref, ref, partner)

    def spread(self, order):
        for kind in range(3):
            self.sideways(kind, order).start()

    def relay(self, order):
        self.sideways(0, order).wait_recv()
        if order >= 2:
            self.passed(3, order).start()
        self.passed(0, order).start()
        self.sideways(1, order).wait_recv()
        if order < 2:
            self.passed(3, order).start()
        self.passed(1, order).start()

    def close(self, order):
        self.passed(3, order).wait_recv()
        self.passed(2, order).start()

    def end(self):
        for order in range(4):
            self.sideways(2, order).wait_recv()
            for kind in range(3):
                self.passed(kind, order).wait_recv()
        for order in range(4):
            for kind in range(3):
                self.sideways(kind, order).wait_send()
            for kind in range(4):
                self.passed(kind, order).wait_send()


class Column:
    COPIES = 13

    def __init__(self, here, full, quad, sent, landed):
        self.here, self.full, self.quad = here, full, quad
        self.wires = Wires(sent, landed)

    def pass_on(self, way, turn):
        here = self.here
        target = self.full.at[here.z - way * turn, here.core, :, HIGH]
        partner = ((here.z + way) * 2 + here.core, here.member)
        return self.wires.copy(turn + (3 if way < 0 else 0), self.quad if turn == 0 else target, target, partner)

    def came(self, way, turn):
        here = self.here
        return self.full.at[here.z - way * (turn + 1), here.core, :, HIGH]

    def arrival(self, way, turn):
        ref = self.came(way, turn)
        return self.wires.copy(turn + (3 if way < 0 else 0), ref, ref, self.here.at_core())

    def across(self, way, turn):
        ref = self.came(way, turn)
        return self.wires.copy(6 + turn + (3 if way < 0 else 0), ref, ref, self.here.at_core())

    def own_across(self):
        here = self.here
        return self.wires.copy(12, self.quad, self.full.at[here.z, here.core, :, HIGH], here.at_core())

    def sends(self, way, turn):
        z = self.here.z
        return (z < 3) & (z >= turn) if way > 0 else (z > 0) & (z <= 3 - turn)

    def comes(self, way, turn):
        z = self.here.z
        return z >= turn + 1 if way > 0 else z <= 2 - turn

    def each(self, test, turn, action):
        for way in (1, -1):
            pl.when(test(way, turn))(lambda way=way: action(way, turn))

    def begin(self):
        self.each(self.sends, 0, lambda way, turn: self.pass_on(way, turn).start())
        self.own_across().start()

    def end_first(self):
        self.each(self.comes, 0, lambda way, turn: self.arrival(way, turn).wait_recv())
        self.each(self.sends, 0, lambda way, turn: self.pass_on(way, turn).wait_send())
        self.own_across().wait()

    def step(self, turn):
        if turn > 1:
            self.each(self.comes, turn - 1, lambda way, turn: self.arrival(way, turn).wait_recv())
        if turn < 3:
            self.each(self.sends, turn, lambda way, turn: self.pass_on(way, turn).start())
        self.each(self.comes, turn - 1, lambda way, turn: self.across(way, turn).start())

    def end(self):
        for turn in range(3):
            self.each(self.comes, turn, lambda way, turn: self.across(way, turn).wait())
        for turn in range(1, 3):
            self.each(self.sends, turn, lambda way, turn: self.pass_on(way, turn).wait_send())


def open_kernel(
    block_ref, quad_ref, part_ref, token_ref, full_ref, expand_ref, shrink_ref, parts_ref, tokens_ref,
    part_mine, part_half, block_buffer, token_buffer, quad_buffer, part_sent, part_landed, sent, landed, more_sent, more_landed, local,
):
    here = Here()
    greet_all(here)
    more = Wires(more_sent, more_landed)
    half = more.copy(0, part_ref.at[1 - here.core], part_half, here.at_core())
    half.start()
    load = pltpu.make_async_copy(part_ref.at[here.core], part_mine, local.at[0])
    load.start()
    first = Gather(
        here,
        lambda member, z, core: full_ref.at[member, z, core],
        lambda z: full_ref.at[here.member, z, here.core],
        sent.at[0],
        landed.at[0],
    )
    second = Gather(here, None, lambda z: expand_ref.at[z], sent.at[1], landed.at[1])
    third = Column(here, shrink_ref, quad_ref, more_sent.at[pl.ds(4, 13)], more_landed.at[pl.ds(4, 13)])
    first.begin(block_ref.at[0])
    mine = here.z * 4 + here.member
    own = [
        Bounce(block_ref.at[0], block_buffer.at[0], first.own(here.z), local.at[1]),
        Bounce(block_ref.at[1], block_buffer.at[1], second.own(here.z), local.at[2]),
        Bounce(token_ref.at[here.member], token_buffer, tokens_ref.at[here.member], local.at[3]),
        Bounce(quad_ref, quad_buffer, shrink_ref.at[here.z, here.core, :, HIGH], local.at[5]),
    ]
    for copy in own:
        copy.start()
    moved = []
    for step in range(1, 4):
        place = lax.rem(here.member + step, 4)
        moved.append(more.copy(step, token_ref.at[place], tokens_ref.at[here.member], here.at_member(step)))
    for copy in moved:
        copy.start()
    for copy in own:
        copy.go_on()
    load.wait()
    half.wait()

    def add(place, carry):
        part_mine[place] += part_half[place]
        return carry

    lax.fori_loop(0, 16, add, 0)
    done = same_core(here, part_mine, parts_ref, part_sent, part_landed)
    keep = pltpu.make_async_copy(part_mine.at[mine], parts_ref.at[mine], local.at[4])
    keep.start()
    own[0].wait()
    first.spread(0)
    for order in range(1, 4):
        first.along(ARRIVALS[order], block_ref.at[0]).wait_recv()
        first.spread(order)
    second.begin(block_ref.at[1])
    third.begin()
    for order in range(4):
        first.relay(order)
    for order in range(4):
        first.close(order)
    first.end()
    third.end_first()
    for step in (1, 3, 2):
        first.along(step, block_ref.at[0]).wait_send()
        second.along(step, block_ref.at[1]).wait()
    for copy in moved:
        copy.wait()
    for copy in own[1:]:
        copy.wait()
    keep.wait()
    done()


def open_up(blocks, quad, parts, tokens):
    column = jax.ShapeDtypeStruct((4, ROWS, 1152), BF16)
    return pl.pallas_call(
        open_kernel,
        in_specs=[ANY] * 4,
        out_specs=[ANY] * 5,
        out_shape=[
            jax.ShapeDtypeStruct((4, 4, 2, ROWS, 1152), BF16),
            column,
            jax.ShapeDtypeStruct((4, 2, 4, ROWS, 1152), BF16),
            jax.ShapeDtypeStruct(parts.shape[1:], parts.dtype),
            jax.ShapeDtypeStruct(tokens.shape, tokens.dtype),
        ],
        scratch_shapes=[
            pltpu.VMEM(parts.shape[1:], F32),
            pltpu.VMEM(parts.shape[1:], F32),
            pltpu.VMEM((2, ROWS, 1152), BF16),
            pltpu.VMEM(tokens.shape[1:], BF16),
            pltpu.VMEM(quad.shape, BF16),
            pltpu.SemaphoreType.DMA((16,)),
            pltpu.SemaphoreType.DMA((16,)),
            pltpu.SemaphoreType.DMA((2, 31)),
            pltpu.SemaphoreType.DMA((2, 31)),
            pltpu.SemaphoreType.DMA((17,)),
            pltpu.SemaphoreType.DMA((17,)),
            pltpu.SemaphoreType.DMA((6,)),
        ],
        compiler_params=pltpu.CompilerParams(collective_id=2, has_side_effects=True),
    )(blocks, quad, parts, tokens)


MIX_AT = 19
EXPAND_AT = MIX_AT + 4
FORWARD_STEPS = EXPAND_AT + 4


def forward_kernel(
    hidden_ref, weight_ref, bias_ref, latent_ref, scaling_ref, expand_bias_ref, expand_column, shrink_given, shrink_column, incoming_ref,
    projected_ref, mixed_ref, log_ref, branch_ref, middle_ref, second_ref, pre_ref, active_ref,
    expand_full, shrink_full, incomings_ref,
    chunk, token_buffer, sent, landed, more_sent, more_landed, local, fetch,
):
    step = pl.program_id(0)
    here = Here()
    features = hidden_ref.shape[1]
    second = Gather(
        here,
        lambda member, z, core: expand_full.at[member, z, core],
        lambda z: expand_column.at[z],
        sent.at[0],
        landed.at[0],
    )
    fourth = Gather(
        here,
        lambda member, z, core: shrink_full.at[z, core, member, LOW],
        lambda z: shrink_column.at[z],
        sent.at[1],
        landed.at[1],
    )
    third = Column(here, shrink_full, None, more_sent.at[pl.ds(0, 13)], more_landed.at[pl.ds(0, 13)])
    more = Wires(more_sent, more_landed)
    own = (
        Bounce(expand_column, chunk.at[0, :, 0], expand_full.at[here.member, :, here.core], local.at[0]),
        Bounce(incoming_ref.at[here.member], token_buffer, incomings_ref.at[here.member], local.at[1]),
        Bounce(shrink_column, chunk.at[1, :, 0, LOW], shrink_full.at[:, here.core, here.member, LOW], local.at[2]),
    )

    def fetch_chunk(part):
        return pltpu.make_async_copy(expand_full.at[part], chunk.at[part % 2], fetch.at[part % 2])

    def move(number):
        place = lax.rem(here.member + number, 4)
        return more.copy(
            12 + number, incoming_ref.at[place], incomings_ref.at[here.member], here.at_member(number)
        )

    @pl.when(step == 0)
    def _():
        greet_near(here)
        for order in range(4):
            second.spread(order)
        third.step(1)
        for copy in own:
            copy.start()

    @pl.when(step == 1)
    def _():
        for copy in own:
            copy.go_on()

    def relay_expand():
        for order in range(4):
            second.relay(order)

    def spread_shrink():
        for order in range(4):
            fourth.spread(order)

    def relay_shrink():
        for order in range(4):
            fourth.relay(order)

    def start_moves():
        for number in (2, 1, 3):
            move(number).start()

    def close_expand():
        for order in range(4):
            second.close(order)

    def finish_expand():
        second.end()
        for copy in own:
            copy.wait()
        fetch_chunk(0).start()
        fetch_chunk(1).start()

    def finish():
        for order in range(4):
            fourth.close(order)
        third.end()
        fourth.end()
        for number in (1, 2, 3):
            move(number).wait()

    for turn, action in (
        (10, functools.partial(third.step, 2)),
        (12, relay_expand),
        (14, spread_shrink),
        (20, functools.partial(third.step, 3)),
        (21, close_expand),
        (EXPAND_AT - 1, start_moves),
        (EXPAND_AT + 1, relay_shrink),
        (EXPAND_AT - 1, finish_expand),
    ):
        pl.when(step == turn)(action)

    def row_blocks(body):
        def one(block, carry):
            body(pl.ds(pl.multiple_of(block * MATMUL_ROWS, MATMUL_ROWS), MATMUL_ROWS))
            return carry

        lax.fori_loop(0, hidden_ref.shape[0] // MATMUL_ROWS, one, 0)

    for part in range(3):

        @pl.when(step == part)
        def _():
            def project(rows):
                values = dot_nn(hidden_ref[rows, :], weight_ref[0]) + bias_ref[part]
                projected_ref[rows, part * features : (part + 1) * features] = values.astype(BF16)

            row_blocks(project)

    @pl.when((step >= 3) & (step < MIX_AT))
    def _():
        forward_head(step - 3, features, projected_ref, mixed_ref, log_ref)

    @pl.when((step >= MIX_AT) & (step < EXPAND_AT))
    def _():
        rows = pl.ds(pl.multiple_of((step - MIX_AT) * 256, 256), 256)
        branch = dot_nn(mixed_ref[rows, :], weight_ref[0]) + bias_ref[3]
        branch_ref[...] = branch
        middle = latent_ref[...].astype(F32) + scaling_ref[0] * branch
        middle_ref[...] = middle
        normed, _ = norm_parts(middle)
        second_ref[rows, :] = (normed * (1.0 + scaling_ref[2]) + scaling_ref[1]).astype(BF16)

    for part in range(4):

        @pl.when(step == EXPAND_AT + part)
        def _():
            fetch_chunk(part).wait()

            def expand(rows):
                weight = chunk[part % 2].reshape(features, features)
                values = dot_nn(second_ref[rows, :], weight) + expand_bias_ref[part]
                pre_ref[rows, :] = values
                active_ref[rows, :] = gelu_parts(values)[0].astype(BF16)

            row_blocks(expand)
            if part + 2 < 4:
                fetch_chunk(part + 2).start()

    pl.when(step == FORWARD_STEPS - 1)(finish)


def forward_head(head, features, projected_ref, mixed_ref, log_ref):
    last = features // LANES - WINDOW // LANES
    start = jnp.minimum(head * HD // LANES, last) * LANES
    first = head * HD - start
    lane = lax.broadcasted_iota(jnp.int32, (1, WINDOW), 1)
    inside = (lane >= first) & (lane < first + HD)

    def window(part):
        return pl.ds(pl.multiple_of(start + part * features, LANES), WINDOW)

    keys = jnp.where(inside, projected_ref[:, window(1)], 0)
    values = jnp.where(inside, projected_ref[:, window(2)], 0)
    turned = values.T
    factor = HD**-0.5 * LOG2E
    count = projected_ref.shape[0] // QUERY_BLOCK

    def score(block):
        return dot_nt(keys, projected_ref[pl.ds(block * QUERY_BLOCK, QUERY_BLOCK), window(0)])

    following = score(0)
    for block in range(count):
        rows = pl.ds(block * QUERY_BLOCK, QUERY_BLOCK)
        scores = following
        if block + 1 < count:
            following = score(block + 1)
        peak = jnp.max(scores, axis=0, keepdims=True)
        powers = jnp.exp2(scores * factor - peak * factor)
        total = jnp.sum(powers, axis=0, keepdims=True)
        log_ref[0, :, rows] = peak * factor + jnp.log2(total)
        weights = (powers * (1.0 / total)).astype(BF16)
        mixed = dot_nn(turned, weights).T.astype(BF16)
        mixed_ref[rows, window(0)] = jnp.where(inside, mixed, mixed_ref[rows, window(0)])


def greet_near(here):
    greet(
        [here.at_member(step) for step in range(1, 4)]
        + [here.at_z(step) for step in range(1, 4)]
        + [here.at_core()]
    )


def forward(hidden, weights, biases, latents, scalings, expand_bias, expand_column, shrink, shrink_column, incoming):
    rows, features = hidden.shape

    def clip(step, low, high):
        return jnp.minimum(jnp.maximum(step - low, 0), high)

    def everything(shape):
        return pl.BlockSpec(shape, lambda step: (0,) * len(shape), pipeline_mode=pl.Buffered(1))

    by_rows = pl.BlockSpec((256, features), lambda step: (clip(step, MIX_AT, 3), 0))
    by_part = pl.BlockSpec((rows, features), lambda step: (0, clip(step, EXPAND_AT, 3)))
    tokens = jax.ShapeDtypeStruct((rows, features), BF16)
    wide = jax.ShapeDtypeStruct((rows, features), F32)
    return pl.pallas_call(
        forward_kernel,
        grid=(FORWARD_STEPS,),
        input_output_aliases={7: 9},
        in_specs=[
            everything((rows, features)),
            pl.BlockSpec((1, features, features), lambda step: (jnp.minimum(step, 3), 0, 0)),
            everything((4, 1, features)),
            by_rows,
            everything((3, 1, features)),
            everything((4, 1, features)),
            ANY,
            ANY,
            ANY,
            ANY,
        ],
        out_specs=[
            everything((rows, 3 * features)),
            everything((rows, features)),
            pl.BlockSpec((1, 1, rows), lambda step: (clip(step, 3, HEADS - 1), 0, 0)),
            by_rows,
            by_rows,
            everything((rows, features)),
            by_part,
            by_part,
            ANY,
            ANY,
            ANY,
        ],
        out_shape=[
            jax.ShapeDtypeStruct((rows, 3 * features), BF16),
            tokens,
            jax.ShapeDtypeStruct((HEADS, 1, rows), F32),
            wide,
            wide,
            tokens,
            jax.ShapeDtypeStruct((rows, 4 * features), F32),
            jax.ShapeDtypeStruct((rows, 4 * features), BF16),
            jax.ShapeDtypeStruct((4, 4, 2, ROWS, 1152), BF16),
            jax.ShapeDtypeStruct((4, 2, 4, ROWS, 1152), BF16),
            jax.ShapeDtypeStruct(incoming.shape, BF16),
        ],
        scratch_shapes=[
            pltpu.VMEM((2, 4, 2, ROWS, 1152), BF16),
            pltpu.VMEM(incoming.shape[1:], BF16),
            pltpu.SemaphoreType.DMA((2, 31)),
            pltpu.SemaphoreType.DMA((2, 31)),
            pltpu.SemaphoreType.DMA((16,)),
            pltpu.SemaphoreType.DMA((16,)),
            pltpu.SemaphoreType.DMA((3,)),
            pltpu.SemaphoreType.DMA((2,)),
        ],
        compiler_params=pltpu.CompilerParams(
            collective_id=5, has_side_effects=True, vmem_limit_bytes=60 * 1024 * 1024
        ),
    )(hidden, weights, biases, latents, scalings, expand_bias, expand_column, shrink, shrink_column, incoming)


class Half:
    COPIES = 13

    def __init__(self, here, rows, source, total, kept, crossed, relayed, beside, along, sent, landed, local):
        self.here, self.rows, self.source, self.total, self.local = here, rows, source, total, local
        self.kept, self.crossed, self.relayed, self.beside, self.pieces = kept, crossed, relayed, beside, along
        self.wires = Wires(sent, landed)
        self.order = (here.across, here.across_x, here.across_y, here.member)

    def load(self, turn):
        return pltpu.make_async_copy(
            self.source(self.order[turn], self.here.core).at[:, self.rows],
            self.kept.at[turn, :, self.rows],
            self.local.at[turn],
        )

    def cross(self, turn):
        here = self.here
        return self.wires.copy(
            turn,
            self.source(self.order[turn], 1 - here.core).at[:, self.rows],
            self.crossed.at[turn, :, self.rows],
            here.at_core(),
        )

    def relay(self, way):
        partner = (self.here.at_x, self.here.at_y)[way]()
        half = pl.ds(2 - 2 * way, 2)
        return self.wires.copy(
            4 + way, self.kept.at[0, half, self.rows], self.relayed.at[way, :, self.rows], partner
        )

    def side(self, way, part):
        partner = (self.here.at_x, self.here.at_y)[way]()
        half = pl.ds(2 * part, 2)
        return self.wires.copy(
            6 + 2 * way + part,
            self.kept.at[1 + way, half, self.rows],
            self.beside.at[way, half, self.rows],
            partner,
        )

    def along(self, step):
        z = lax.rem(self.here.z + step, 4)
        return self.wires.copy(
            9 + step, self.kept.at[3, z, self.rows], self.pieces.at[step - 1, self.rows], self.here.at_z(step)
        )

    def begin(self):
        for turn in range(4):
            self.cross(turn).start()
            self.load(turn).start()

    def add_crossed(self, turn):
        self.load(turn).wait()
        self.cross(turn).wait_recv()

        def add(z, carry):
            mine = self.kept[turn, z, self.rows, :].astype(F32)
            self.kept[turn, z, self.rows, :] = (mine + self.crossed[turn, z, self.rows, :].astype(F32)).astype(BF16)
            return carry

        lax.fori_loop(0, 4, add, 0)

    def add_relayed(self, turn, way, first):
        def add(z, carry):
            mine = self.kept[turn, first + z, self.rows, :].astype(F32)
            self.kept[turn, first + z, self.rows, :] = (
                mine + self.relayed[way, z, self.rows, :].astype(F32)
            ).astype(BF16)
            return carry

        lax.fori_loop(0, 2, add, 0)

    def diagonal(self):
        self.add_crossed(0)
        self.relay(1).start()
        self.relay(0).start()

    def direct(self):
        self.add_crossed(1)
        self.side(0, 1).start()
        self.add_crossed(2)
        self.side(1, 0).start()
        self.add_crossed(3)

    def relays(self):
        self.relay(1).wait_recv()
        self.add_relayed(1, 1, 0)
        self.side(0, 0).start()
        self.relay(0).wait_recv()
        self.add_relayed(2, 0, 2)
        self.side(1, 1).start()

    def three(self, z):
        return (
            self.kept[3, z, self.rows, :].astype(F32)
            + self.beside[0, z, self.rows, :].astype(F32)
            + self.beside[1, z, self.rows, :].astype(F32)
        )

    def along_z(self):
        here = self.here
        for way in range(2):
            for part in range(2):
                self.side(way, part).wait_recv()
        for step in (2, 1, 3):
            z = lax.rem(here.z + step, 4)
            self.kept[3, z, self.rows, :] = self.three(z).astype(BF16)
            self.along(step).start()
        self.total[self.rows, :] = self.three(here.z)

    def finish(self):
        for step in (1, 3, 2):
            self.along(step).wait_recv()
        pieces = [self.pieces[step, self.rows, :].astype(F32) for step in range(3)]
        self.total[self.rows, :] += pieces[0] + pieces[1] + pieces[2]
        for turn in range(4):
            self.cross(turn).wait_send()
        for way in range(2):
            self.relay(way).wait_send()
            for part in range(2):
                self.side(way, part).wait_send()
        for step in range(1, 4):
            self.along(step).wait_send()


class Reduce:
    SCRATCH = (
        pltpu.VMEM((4, 4, ROWS, 1152), BF16),
        pltpu.VMEM((4, 4, ROWS, 1152), BF16),
        pltpu.VMEM((2, 2, ROWS, 1152), BF16),
        pltpu.VMEM((2, 4, ROWS, 1152), BF16),
        pltpu.VMEM((3, ROWS, 1152), BF16),
        pltpu.SemaphoreType.DMA((26,)),
        pltpu.SemaphoreType.DMA((26,)),
        pltpu.SemaphoreType.DMA((8,)),
    )

    def __init__(self, here, source, total, *scratch):
        buffers, (sent, landed, local) = scratch[:5], scratch[5:]
        self.halves = [
            Half(
                here,
                rows,
                source,
                total,
                *buffers,
                sent.at[pl.ds(13 * part, 13)],
                landed.at[pl.ds(13 * part, 13)],
                local.at[pl.ds(4 * part, 4)],
            )
            for part, rows in enumerate((pl.ds(0, 80), pl.ds(80, 64)))
        ]

    def begin(self):
        for half in self.halves:
            half.begin()

    def steps(self):
        first, second = self.halves
        return (
            (0.0, self.begin),
            (0.11, first.diagonal),
            (0.26, first.direct),
            (0.26, first.relays),
            (0.27, second.diagonal),
            (0.56, second.direct),
            (0.57, second.relays),
            (0.58, first.along_z),
            (0.84, second.along_z),
            (1.0, first.finish),
            (1.0, second.finish),
        )


def backward_reduce_kernel(
    query_ref, key_ref, value_ref, incoming_ref, log_ref, source_ref, grad_ref, total_ref,
    key_total, value_total, *scratch
):
    head = pl.program_id(0)
    here = Here()
    reduce = Reduce(here, lambda member, core: source_ref.at[member, :, core], total_ref, *scratch)

    @pl.when(head == 0)
    def _():
        greet((here.at_x(), here.at_y(), here.at_core(), here.at_z(1), here.at_z(2), here.at_z(3)))

    steps = reduce.steps()
    for share, action in steps[:-2]:
        pl.when(head == round(share * HEADS))(action)
    attend_backward_kernel(
        query_ref, key_ref, value_ref, incoming_ref, log_ref, grad_ref, key_total, value_total
    )
    for _, action in steps[-2:]:
        pl.when(head == HEADS - 1)(action)


def attend_backward_reduce(projected, incoming, log_total, source):
    rows = projected.shape[0]
    features = projected.shape[1] // 3
    return pl.pallas_call(
        backward_reduce_kernel,
        grid=(HEADS,),
        in_specs=[whole_block((rows, features), part) for part in (0, 1, 2, 0)]
        + [pl.BlockSpec((1, 1, rows), lambda head: (head, 0, 0)), ANY],
        out_specs=[whole_block((rows, 3 * features), 0), whole_block((ROWS, features), 0)],
        out_shape=[
            jax.ShapeDtypeStruct((rows, 3 * features), BF16),
            jax.ShapeDtypeStruct((ROWS, features), F32),
        ],
        scratch_shapes=[pltpu.VMEM((rows, rows), BF16), pltpu.VMEM((rows, rows), BF16), *Reduce.SCRATCH],
        compiler_params=pltpu.CompilerParams(
            collective_id=6, has_side_effects=True, vmem_limit_bytes=58 * 1024 * 1024
        ),
    )(projected, projected, projected, incoming, log_total, source)


def clipped(step, low, high):
    return jnp.minimum(jnp.maximum(step - low, 0), high)


def everything(shape):
    return pl.BlockSpec(shape, lambda step: (0,) * len(shape), pipeline_mode=pl.Buffered(1))


def turn_kernel(
    active_ref, shrink_ref, middle_ref, incoming_ref, gate_ref, bias_ref, token_ref, back_ref, grads_ref, sums_ref, total
):
    step = pl.program_id(0)

    @pl.when(step == 0)
    def _():
        sums_ref[...] = jnp.zeros_like(sums_ref)
        total[...] = dot_nn(active_ref[...], shrink_ref[...])

    @pl.when((step > 0) & (step < 4))
    def _():
        total[...] += dot_nn(active_ref[...], shrink_ref[...])

    @pl.when((step >= 4) & (step < 8))
    def _():
        rows = pl.ds(pl.multiple_of((step - 4) * 256, 256), 256)
        branch = total[rows, :] + bias_ref[...]
        incoming = incoming_ref[0].astype(F32)
        token_ref[0] = (middle_ref[...] + gate_ref[...] * branch).astype(BF16)
        back = (gate_ref[...] * incoming).astype(BF16)
        back_ref[rows, :] = back
        sums_ref[0:1, :] += jnp.sum(incoming * branch, axis=0, keepdims=True)
        sums_ref[1:2, :] += jnp.sum(back.astype(F32), axis=0, keepdims=True)

    @pl.when(step >= 8)
    def _():
        width = active_ref.shape[1] // 3
        for part in range(3):
            columns = slice(part * width, (part + 1) * width)
            grads_ref[0, columns, :] = dot_tn(active_ref[:, columns], back_ref[...]).astype(BF16)


def turn(active, shrink, middle, incoming, gate, bias):
    rows, features = middle.shape
    by_member = pl.BlockSpec((1, 256, features), lambda step: (clipped(step, 4, 3), 0, 0))
    return pl.pallas_call(
        turn_kernel,
        grid=(12,),
        in_specs=[
            pl.BlockSpec((rows, features), lambda step: (0, jnp.where(step < 8, jnp.minimum(step, 3), step - 8))),
            pl.BlockSpec((features, features), lambda step: (jnp.minimum(step, 3), 0)),
            pl.BlockSpec((256, features), lambda step: (clipped(step, 4, 3), 0)),
            by_member,
            everything((1, features)),
            everything((1, features)),
        ],
        out_specs=[
            by_member,
            everything((rows, features)),
            pl.BlockSpec((1, features, features), lambda step: (clipped(step, 8, 3), 0, 0)),
            everything((8, features)),
        ],
        out_shape=[
            jax.ShapeDtypeStruct(incoming.shape, BF16),
            jax.ShapeDtypeStruct((rows, features), BF16),
            jax.ShapeDtypeStruct((4, features, features), BF16),
            jax.ShapeDtypeStruct((8, features), F32),
        ],
        scratch_shapes=[pltpu.VMEM((rows, features), F32)],
        compiler_params=pltpu.CompilerParams(vmem_limit_bytes=56 * 1024 * 1024),
    )(active, shrink, middle, incoming, gate, bias)


NORM_AT = 12
BACK_STEPS = NORM_AT + 5
BACK_SHARE = 13


def back_kernel(
    back_ref, second_ref, pre_ref, shrink_ref, expand_ref, middle_ref, branch_ref, incoming_ref, mixed_ref, weight_ref,
    scaling_ref, source_ref, token_ref,
    expand_grad_ref, expand_sum_ref, middle_grad_ref, mixed_grad_ref, output_grad_ref, sums_ref, block_ref, tokens_ref,
    total, slope, branch_back, buffer, sent, landed, local, *scratch
):
    step = pl.program_id(0)
    here = Here()
    reduce = Reduce(here, lambda member, core: source_ref.at[:, core, member], block_ref, *scratch)

    wires = Wires(sent, landed)

    def move(number):
        place = lax.rem(here.member + number, 4)
        return wires.copy(number - 1, token_ref.at[place], tokens_ref.at[here.member], here.at_member(number))

    own = Bounce(token_ref.at[here.member], buffer, tokens_ref.at[here.member], local.at[0])

    @pl.when(step == 0)
    def _():
        greet_near(here)
        own.start()
        sums_ref[...] = jnp.zeros_like(sums_ref)

    @pl.when(step == 9)
    def _():
        own.go_on()
        for number in (2, 1, 3):
            move(number).start()

    @pl.when(step == 0)
    def _():
        total[...] = jnp.zeros_like(total)

    steps = reduce.steps()
    for share, action in steps[:-2]:
        pl.when(step == round(share * BACK_SHARE))(action)

    @pl.when(step < NORM_AT)
    def _():
        def one(block, carry):
            rows = pl.ds(pl.multiple_of(block * MATMUL_ROWS, MATMUL_ROWS), MATMUL_ROWS)
            active_grad = dot_nt(back_ref[rows, :], shrink_ref[...])
            grad = (active_grad * gelu_parts(pre_ref[rows, :])[1]).astype(BF16)
            slope[rows, :] = grad
            total[rows, :] += dot_nt(grad, expand_ref[0])
            return carry

        lax.fori_loop(0, total.shape[0] // MATMUL_ROWS, one, 0)
        expand_sum_ref[0] = jnp.sum(slope[...].astype(F32), axis=0, keepdims=True)
        expand_grad_ref[0] = dot_tn(second_ref[...], slope[...]).astype(BF16)

    @pl.when((step >= NORM_AT) & (step < NORM_AT + 4))
    def _():
        rows = pl.ds(pl.multiple_of((step - NORM_AT) * 256, 256), 256)
        grad = total[rows, :]
        normed, inverse = norm_parts(middle_ref[...])
        sums_ref[1:2, :] += jnp.sum(grad, axis=0, keepdims=True)
        sums_ref[2:3, :] += jnp.sum(grad * normed, axis=0, keepdims=True)
        normed_grad = grad * (1.0 + scaling_ref[1])
        mean_first = jnp.mean(normed_grad, axis=-1, keepdims=True)
        mean_second = jnp.mean(normed_grad * normed, axis=-1, keepdims=True)
        middle_grad = incoming_ref[0].astype(F32) + inverse * (normed_grad - mean_first - normed * mean_second)
        middle_grad_ref[...] = middle_grad
        sums_ref[0:1, :] += jnp.sum(middle_grad * branch_ref[...], axis=0, keepdims=True)
        branch_grad = (scaling_ref[0] * middle_grad).astype(BF16)
        branch_back[rows, :] = branch_grad
        sums_ref[3:4, :] += jnp.sum(branch_grad.astype(F32), axis=0, keepdims=True)
        mixed_grad_ref[...] = dot_nt(branch_grad, weight_ref[0]).astype(BF16)

    @pl.when(step == BACK_STEPS - 1)
    def _():
        width = mixed_ref.shape[1] // 3
        for part in range(3):
            columns = slice(part * width, (part + 1) * width)
            output_grad_ref[0, columns, :] = dot_tn(mixed_ref[:, columns], branch_back[...]).astype(BF16)

    for _, action in steps[-2:]:
        pl.when(step == BACK_STEPS - 1)(action)

    @pl.when(step == BACK_STEPS - 1)
    def _():
        for number in range(1, 4):
            move(number).wait()
        own.wait()


def back(back_rows, second, pre, shrink, expand, middle, branch, incoming, mixed, weights, scalings, source, token):
    rows, features = middle.shape
    third = features // 3
    by_rows = pl.BlockSpec((256, features), lambda step: (clipped(step, NORM_AT, 3), 0))

    def piece(step):
        return jnp.minimum(step, NORM_AT - 1)

    wide = jax.ShapeDtypeStruct((rows, features), F32)
    return pl.pallas_call(
        back_kernel,
        grid=(BACK_STEPS,),
        in_specs=[
            everything((rows, features)),
            everything((rows, features)),
            pl.BlockSpec((rows, third), lambda step: (0, piece(step))),
            pl.BlockSpec((third, features), lambda step: (piece(step), 0)),
            pl.BlockSpec((1, features, third), lambda step: (piece(step) // 3, 0, piece(step) % 3)),
            by_rows,
            by_rows,
            pl.BlockSpec((1, 256, features), lambda step: (clipped(step, NORM_AT, 3), 0, 0)),
            everything((rows, features)),
            pl.BlockSpec((1, features, features), lambda step: (3, 0, 0), pipeline_mode=pl.Buffered(1)),
            everything((2, 1, features)),
            ANY,
            ANY,
        ],
        out_specs=[
            pl.BlockSpec((1, features, third), lambda step: (piece(step) // 3, 0, piece(step) % 3)),
            pl.BlockSpec((1, 1, third), lambda step: (piece(step), 0, 0)),
            by_rows,
            by_rows,
            pl.BlockSpec((1, features, features), lambda step: (3, 0, 0), pipeline_mode=pl.Buffered(1)),
            everything((8, features)),
            everything((ROWS, features)),
            ANY,
        ],
        out_shape=[
            jax.ShapeDtypeStruct((4, features, features), BF16),
            jax.ShapeDtypeStruct((NORM_AT, 1, third), F32),
            wide,
            jax.ShapeDtypeStruct((rows, features), BF16),
            jax.ShapeDtypeStruct((4, features, features), BF16),
            jax.ShapeDtypeStruct((8, features), F32),
            jax.ShapeDtypeStruct((ROWS, features), F32),
            jax.ShapeDtypeStruct(token.shape, BF16),
        ],
        scratch_shapes=[
            pltpu.VMEM((rows, features), F32),
            pltpu.VMEM((rows, third), BF16),
            pltpu.VMEM((rows, features), BF16),
            pltpu.VMEM(token.shape[1:], BF16),
            pltpu.SemaphoreType.DMA((3,)),
            pltpu.SemaphoreType.DMA((3,)),
            pltpu.SemaphoreType.DMA((1,)),
            *Reduce.SCRATCH,
        ],
        compiler_params=pltpu.CompilerParams(
            collective_id=8, has_side_effects=True, vmem_limit_bytes=60 * 1024 * 1024
        ),
    )(back_rows, second, pre, shrink, expand, middle, branch, incoming, mixed, weights, scalings, source, token)


def triple_kernel(given_ref, hidden_ref, triple_ref, grad_ref, sums_ref):
    width = hidden_ref.shape[1] // 3
    for part in range(3):
        columns = slice(part * width, (part + 1) * width)
        grad_ref[0, columns, :] = dot_tn(hidden_ref[:, columns], triple_ref[...]).astype(BF16)
    sums_ref[0] = jnp.sum(triple_ref[...].astype(F32), axis=0, keepdims=True)


def triple_gradient(given, hidden, triple):
    rows, features = hidden.shape
    return pl.pallas_call(
        triple_kernel,
        grid=(3,),
        in_specs=[ANY, everything((rows, features)), pl.BlockSpec((rows, features), lambda step: (0, step))],
        out_specs=[
            pl.BlockSpec((1, features, features), lambda step: (step, 0, 0)),
            pl.BlockSpec((1, 1, features), lambda step: (step, 0, 0)),
        ],
        out_shape=[
            jax.ShapeDtypeStruct(given.shape, BF16),
            jax.ShapeDtypeStruct((3, 1, features), F32),
        ],
        input_output_aliases={0: 0},
        compiler_params=pltpu.CompilerParams(vmem_limit_bytes=56 * 1024 * 1024),
    )(given, hidden, triple)


class Shares:
    def __init__(self, here, block, pieces, target, wires, local):
        self.block, self.pieces = block, pieces
        self.copies = [
            wires.copy(
                step - 1,
                pieces.at[lax.rem(here.member + step, 4)],
                target.at[here.member],
                here.at_member(step),
            )
            for step in range(1, 4)
        ]
        self.copies.append(pltpu.make_async_copy(pieces.at[here.member], target.at[here.member], local))

    def start(self):
        for member in range(4):
            self.pieces[member, :36] = self.block[member * 36 : member * 36 + 36, :]
        for copy in self.copies:
            copy.start()

    def wait(self):
        for copy in self.copies:
            copy.wait()


def close_kernel(
    grad_ref, triple_ref, weight_ref, latent_ref, middle_ref, scale_ref, vector_ref, bias_ref, block_ref,
    total, tokens_ref, rows_ref, biases_ref, share_ref,
    pieces, triple, weight, latent, middle, token, wide, row, row_sent, row_landed, bias_sent, bias_landed,
    more_sent, more_landed, local, *scratch
):
    here = Here()
    features = latent_ref.shape[1]
    greet_all(here)
    reduce = Reduce(here, lambda member, core: grad_ref.at[member, :, core], total, *scratch)
    loads = [
        pltpu.make_async_copy(weight_ref.at[pl.ds(0, 3)], weight, local.at[0]),
        pltpu.make_async_copy(triple_ref, triple, local.at[1]),
        pltpu.make_async_copy(latent_ref, latent, local.at[2]),
        pltpu.make_async_copy(middle_ref, middle, local.at[3]),
    ]
    for copy in loads:
        copy.start()
    reduce.begin()
    bias_done = everyone(here, lambda place: bias_ref.at[place], biases_ref, bias_sent, bias_landed)
    own_bias = pltpu.make_async_copy(bias_ref.at[here.index], biases_ref.at[here.index], local.at[4])
    own_bias.start()
    wires = Wires(more_sent, more_landed)

    shares = Shares(here, block_ref, pieces, share_ref, Wires(more_sent.at[pl.ds(3, 3)], more_landed.at[pl.ds(3, 3)]), local.at[7])
    shares.start()

    def move(step):
        place = lax.rem(here.member + step, 4)
        return wires.copy(step - 1, token.at[place], tokens_ref.at[here.member], here.at_member(step))

    def compute(step):
        place = lax.rem(here.member + step, 4)
        rows = pl.ds(pl.multiple_of(place * 256, 256), 256)
        hidden_grad = dot_nt(triple[rows, :features], weight[0])
        hidden_grad += dot_nt(triple[rows, features : 2 * features], weight[1])
        hidden_grad += dot_nt(triple[rows, 2 * features :], weight[2])
        normed, inverse = norm_parts(latent[rows, :].astype(F32))
        shift = jnp.sum(hidden_grad, axis=0, keepdims=True)
        scale = jnp.sum(hidden_grad * normed, axis=0, keepdims=True)
        normed_grad = hidden_grad * (1.0 + scale_ref[...])
        mean_first = jnp.mean(normed_grad, axis=-1, keepdims=True)
        mean_second = jnp.mean(normed_grad * normed, axis=-1, keepdims=True)
        result = middle[rows, :] + inverse * (normed_grad - mean_first - normed * mean_second)
        token[place] = result.astype(BF16)
        return shift, scale

    for copy in loads:
        copy.wait()
    first, second = reduce.halves
    sums = [compute(2)]
    first.diagonal()
    sums.append(compute(1))
    first.direct()
    first.relays()
    second.diagonal()
    sums.append(compute(3))
    sums.append(compute(0))
    second.direct()
    second.relays()
    first.along_z()
    own = pltpu.make_async_copy(token.at[here.member], tokens_ref.at[here.member], local.at[5])
    own.start()
    wide[...] = vector_ref[...]
    for part in range(2):
        vector = sums[0][part] + sums[1][part] + sums[2][part] + sums[3][part]
        for tile in range(features // LANES):
            place = part * (features // LANES) + tile
            wide[place : place + 1, :] = vector[:, tile * LANES : (tile + 1) * LANES]
    row[...] = wide[...].astype(BF16)
    rows_done = everyone(here, lambda place: row, rows_ref, row_sent, row_landed)
    own_row = pltpu.make_async_copy(row, rows_ref.at[here.index], local.at[6])
    own_row.start()
    second.along_z()
    for step in (2, 1, 3):
        move(step).start()
    first.finish()
    second.finish()
    shares.wait()
    for step in range(1, 4):
        move(step).wait()
    own.wait()
    own_bias.wait()
    own_row.wait()
    rows_done()
    bias_done()


def close_down(grad, triple, weight, latents, middle_grad, scale, vectors, bias, block):
    rows, features = latents.shape
    whole = pl.BlockSpec(memory_space=pltpu.VMEM)
    return pl.pallas_call(
        close_kernel,
        in_specs=[ANY] * 5 + [whole, whole, ANY, whole],
        out_specs=[whole, ANY, ANY, ANY, ANY],
        out_shape=[
            jax.ShapeDtypeStruct((ROWS, 1152), F32),
            jax.ShapeDtypeStruct((4, rows // 4, features), BF16),
            jax.ShapeDtypeStruct((32,) + vectors.shape, BF16),
            jax.ShapeDtypeStruct(bias.shape, bias.dtype),
            jax.ShapeDtypeStruct((4, 40, 1152), F32),
        ],
        scratch_shapes=[
            pltpu.VMEM((4, 40, 1152), F32),
            pltpu.VMEM(triple.shape, BF16),
            pltpu.VMEM((3, features, features), BF16),
            pltpu.VMEM(latents.shape, BF16),
            pltpu.VMEM(latents.shape, F32),
            pltpu.VMEM((4, rows // 4, features), BF16),
            pltpu.VMEM(vectors.shape, F32),
            pltpu.VMEM(vectors.shape, BF16),
        ]
        + [pltpu.SemaphoreType.DMA((32,))] * 4
        + [pltpu.SemaphoreType.DMA((6,))] * 2
        + [pltpu.SemaphoreType.DMA((8,))]
        + list(Reduce.SCRATCH),
        compiler_params=pltpu.CompilerParams(
            collective_id=3, has_side_effects=True, vmem_limit_bytes=60 * 1024 * 1024
        ),
    )(grad, triple, weight, latents, middle_grad, scale, vectors, bias, block)


def swap_kernel(part_ref, block_ref, parts_ref, share_ref, pieces, sent, landed, more_sent, more_landed, local):
    here = Here()
    greet_all(here)
    shares = Shares(here, block_ref, pieces, share_ref, Wires(more_sent, more_landed), local.at[1])
    done = everyone(here, lambda place: part_ref.at[place // 4], parts_ref, sent, landed)
    own = pltpu.make_async_copy(part_ref.at[here.group], parts_ref.at[here.index], local.at[0])
    own.start()
    shares.start()
    shares.wait()
    own.wait()
    done()


def swap(parts, block):
    return pl.pallas_call(
        swap_kernel,
        in_specs=[ANY, pl.BlockSpec(memory_space=pltpu.VMEM)],
        out_specs=[ANY, ANY],
        out_shape=[
            jax.ShapeDtypeStruct((32,) + parts.shape[1:], parts.dtype),
            jax.ShapeDtypeStruct((4, 40, 1152), F32),
        ],
        scratch_shapes=[
            pltpu.VMEM((4, 40, 1152), F32),
            pltpu.SemaphoreType.DMA((32,)),
            pltpu.SemaphoreType.DMA((32,)),
            pltpu.SemaphoreType.DMA((3,)),
            pltpu.SemaphoreType.DMA((3,)),
            pltpu.SemaphoreType.DMA((2,)),
        ],
        compiler_params=pltpu.CompilerParams(collective_id=4, has_side_effects=True),
    )(parts, block)


def pad_lanes(values, width):
    return jnp.pad(values, ((0, 0), (0, width - values.shape[1])))


def on_device_fast(
    latents,
    condition,
    cotangent,
    modulate_weight,
    modulate_bias,
    triple_weight,
    triple_bias,
    output_weight,
    output_bias,
    expand_weight,
    expand_bias,
    shrink_weight,
    shrink_bias,
):
    micro, local, tokens, features = latents.shape
    devices = 32
    me = lax.axis_index("dp") * 4 + lax.axis_index("seq")
    hidden = expand_weight.shape[1]
    shard = jnp.stack([jnp.concatenate([triple_weight, output_weight], axis=1), expand_weight])
    shard = jnp.pad(shard, ((0, 0), (0, 12), (0, 0)))
    own_cond = lax.dynamic_index_in_dim(condition.reshape(4, features), lax.axis_index("seq"), axis=0, keepdims=False)
    biases = (modulate_bias, triple_bias, output_bias, expand_bias, shrink_bias)
    note = jnp.concatenate([own_cond, *biases]).astype(F32)
    note = jnp.pad(note, (0, 1664 - note.shape[0])).reshape(1, 1, 1664)
    notes, blocks, shrink_quad, shrink_column = introduce(note, shard, shrink_weight)
    notes = notes.reshape(32, 1664)
    cond_act = jax.nn.silu(notes[:, :features]).astype(BF16)
    cuts = []
    offset = features
    for bias in biases:
        cuts.append(notes[:, offset : offset + bias.shape[0]].reshape(-1))
        offset += bias.shape[0]
    modulate_offset, triple_offset, output_offset, expand_offset, shrink_offset = cuts
    owned = modulate_weight.shape[0]
    act_owned = lax.dynamic_slice_in_dim(cond_act, me * owned, owned, axis=1)
    parts = pad_lanes(dot_nn(act_owned, modulate_weight), 56 * LANES).reshape(4, 2, 4, 56, LANES)
    parts = jnp.swapaxes(parts, 0, 1).reshape(2, 16, 56, LANES)
    first_full, expand_column, shrink_full, parts, token_rows = open_up(
        blocks, shrink_quad, parts, latents.reshape(4, tokens, features)
    )
    first_full = first_full.reshape(4, features, features)
    modulation = jnp.sum(parts, axis=0).reshape(-1)[: 6 * features] + modulate_offset
    shift_one, scale_one, gate_one, shift_two, scale_two, gate_two = jnp.split(modulation[None, :], 6, axis=-1)

    token_rows = token_rows.reshape(4 * tokens, features)
    latent_float = token_rows.astype(F32)
    normed_one, inverse_one = norm_parts(latent_float)
    hidden_one = (normed_one * (1.0 + scale_one) + shift_one).astype(BF16)
    zero = jnp.zeros((features,), F32)
    first_bias = jnp.stack(
        [triple_offset[:features], zero, triple_offset[features:], output_offset]
    ).reshape(4, 1, features)
    output_full = first_full[3]
    (
        projected,
        mixed,
        log_total,
        branch_one,
        middle,
        hidden_two,
        pre_act,
        activated,
        expand_full,
        shrink_full,
        incoming,
    ) = forward(
        hidden_one,
        first_full,
        first_bias,
        token_rows,
        jnp.stack([gate_one, shift_two, scale_two]),
        expand_offset.reshape(4, 1, features),
        expand_column,
        shrink_full,
        shrink_column,
        cotangent.reshape(4, tokens, features),
    )
    expand_full = expand_full.reshape(4, features, features)
    shrink_full = shrink_full.reshape(hidden, features)
    output_rows, back_rows, shrink_grad, turn_sums = turn(
        activated, shrink_full, middle, incoming, gate_two, shrink_offset[None]
    )
    expand_grad, expand_offset_grad, middle_grad, mixed_grad, first_grad, back_sums, shrink_total, output = back(
        back_rows,
        hidden_two,
        pre_act,
        shrink_full,
        expand_full,
        middle,
        branch_one,
        incoming,
        mixed,
        first_full,
        jnp.stack([gate_one, scale_two]),
        shrink_grad.reshape(4, 2, 4, ROWS, features),
        output_rows,
    )
    expand_grad = expand_grad.reshape(4, 4, 2, ROWS, features)
    gate_two_grad, shrink_offset_grad = turn_sums[0], turn_sums[1]
    gate_one_grad, output_offset_grad = back_sums[0], back_sums[3]
    triple_rows, expand_block = attend_backward_reduce(projected, mixed_grad, log_total, expand_grad)
    first_grad, column_sums = triple_gradient(first_grad, hidden_one, triple_rows)
    first_grad = first_grad.reshape(4, 4, 2, ROWS, features)
    triple_offset_grad = jnp.concatenate([column_sums[0, 0], column_sums[2, 0]])
    vectors = jnp.concatenate(
        [
            jnp.zeros((2 * features,), F32),
            gate_one_grad,
            back_sums[1],
            back_sums[2],
            gate_two_grad,
            jnp.zeros((64 * LANES - 6 * features,), F32),
        ]
    ).reshape(64, LANES)
    bias_grads = jnp.concatenate(
        [
            values.reshape(devices, -1)
            for values in (triple_offset_grad, output_offset_grad, expand_offset_grad, shrink_offset_grad)
        ],
        axis=1,
    )
    bias_grads = pad_lanes(bias_grads, 1024).reshape(32, 8, LANES)
    first_block, token_grad, all_grads, bias_parts, expand_share = close_down(
        first_grad, triple_rows, first_full, token_rows, middle_grad, scale_one, vectors, bias_grads, expand_block
    )
    all_grads = all_grads.reshape(32, 8192)[:, : 6 * features]
    modulate_total = dot_tn(act_owned, all_grads)
    width = modulate_bias.shape[0]
    modulate_offset_total = jnp.sum(
        lax.dynamic_slice_in_dim(all_grads, me * width, width, axis=1).astype(F32), axis=0
    )
    cond_back = dot_nt(all_grads, modulate_weight)
    cond_back = jnp.pad(cond_back.reshape(8, 4, owned), ((0, 0), (0, 4), (0, LANES - owned)))
    cond_back, first_share = swap(cond_back, first_block)
    cond_back = cond_back[:, :4, :owned]
    cond_back = jnp.swapaxes(cond_back, 0, 1).reshape(condition.shape)
    cond_float = condition.astype(F32)
    sigmoid_cond = jax.nn.sigmoid(cond_float)
    condition_gradient = cond_back * (sigmoid_cond * (1.0 + cond_float * (1.0 - sigmoid_cond)))
    bias_total = jnp.sum(bias_parts.reshape(32, 1024), axis=0)
    bias_cuts = []
    offset = 0
    for bias in biases[1:]:
        bias_cuts.append(bias_total[offset : offset + bias.shape[0]])
        offset += bias.shape[0]
    first_share = first_share[:, :owned]
    expand_total = jnp.swapaxes(expand_share[:, :owned], 0, 1).reshape(expand_weight.shape)
    return (
        output.reshape(latents.shape),
        token_grad.reshape(latents.shape).astype(F32),
        condition_gradient,
        modulate_total,
        modulate_offset_total,
        jnp.concatenate([first_share[0], first_share[1], first_share[2]], axis=1),
        bias_cuts[0],
        first_share[3],
        bias_cuts[1],
        expand_total,
        bias_cuts[2],
        shrink_total,
        bias_cuts[3],
    )


def solution(mesh):
    tokens = P(None, "dp", "seq", None)
    conditions = P(None, "dp", None)
    weight = P(AXES, None)
    bias = P(AXES)
    parameters = (weight, bias) * 5
    fast = mesh.shape["dp"] == 8 and mesh.shape["seq"] == 4
    return jax.shard_map(
        on_device_fast if fast else on_device,
        mesh=mesh,
        in_specs=(tokens, conditions, tokens) + parameters,
        out_specs=(tokens, tokens, conditions) + parameters,
        check_vma=False,
    )
```

```python
import functools

import jax
import jax.numpy as jnp
from jax import lax
from jax.experimental import pallas as pl
from jax.experimental.pallas import tpu as pltpu
from jax.sharding import PartitionSpec as P

HEADS = 16
HD = 72
LANES = 128
WINDOW = 256
QUERY_BLOCK = 256

EPSILON = 1e-06
GELU_COEF = 0.7978845608028654
CUBIC = 0.044715
LOG2E = 1.4426950408889634
AXES = ("dp", "seq")
F32 = jnp.float32
BF16 = jnp.bfloat16


def gelu_parts(values):
    square = values * values
    tangent = jnp.tanh(GELU_COEF * values * (1.0 + CUBIC * square))
    half = 0.5 * (1.0 + tangent)
    slope = half + (0.5 * GELU_COEF) * values * (1.0 - tangent * tangent) * (1.0 + 3.0 * CUBIC * square)
    return (values * half, slope)


def norm_parts(values):
    centered = values - jnp.mean(values, axis=-1, keepdims=True)
    variance = jnp.mean(centered * centered, axis=-1, keepdims=True)
    inverse = lax.rsqrt(variance + EPSILON)
    return (centered * inverse, inverse)


def norm_back(incoming, normed, inverse, scaling):
    shift_grad = jnp.sum(incoming, axis=1)
    scale_grad = jnp.sum(incoming * normed, axis=1)
    normed_grad = incoming * (1.0 + scaling)
    mean_first = jnp.mean(normed_grad, axis=-1, keepdims=True)
    mean_second = jnp.mean(normed_grad * normed, axis=-1, keepdims=True)
    return (inverse * (normed_grad - mean_first - normed * mean_second), shift_grad, scale_grad)


def dot_nt(left, right):
    return lax.dot_general(left, right, (((1,), (1,)), ((), ())), preferred_element_type=F32)


def dot_tn(left, right):
    return lax.dot_general(left, right, (((0,), (0,)), ((), ())), preferred_element_type=F32)


def dot_nn(left, right):
    return jnp.dot(left, right, preferred_element_type=F32)


def head_window(features):
    head = pl.program_id(0)
    last = features // LANES - WINDOW // LANES
    tile = jnp.minimum(head * HD // LANES, last)
    start = pl.multiple_of(tile * LANES, LANES)
    first = head * HD - start
    lane = lax.broadcasted_iota(jnp.int32, (1, WINDOW), 1)
    return start, (lane >= first) & (lane < first + HD)


def attend_forward_kernel(query_ref, key_ref, value_ref, mixed_ref, log_ref):
    features = query_ref.shape[1]
    start, inside = head_window(features)
    window = pl.ds(start, WINDOW)
    keys = jnp.where(inside, key_ref[:, window], 0)
    values = jnp.where(inside, value_ref[:, window], 0)
    factor = HD**-0.5 * LOG2E
    for block in range(query_ref.shape[0] // QUERY_BLOCK):
        rows = pl.ds(block * QUERY_BLOCK, QUERY_BLOCK)
        scores = dot_nt(keys, query_ref[rows, window])
        peak = jnp.max(scores, axis=0, keepdims=True)
        powers = jnp.exp2((scores - peak) * factor)
        total = jnp.sum(powers, axis=0, keepdims=True)
        log_ref[0, :, rows] = peak * factor + jnp.log2(total)
        weights = (powers * (1.0 / total)).astype(BF16)
        mixed = dot_tn(values, weights).T.astype(BF16)
        mixed_ref[rows, window] = jnp.where(inside, mixed, mixed_ref[rows, window])


def attend_backward_kernel(
    query_ref, key_ref, value_ref, incoming_ref, log_ref, grad_ref, score_grads, weights
):
    features = query_ref.shape[1]
    start, inside = head_window(features)
    window = pl.ds(start, WINDOW)
    keys = jnp.where(inside, key_ref[:, window], 0)
    values = jnp.where(inside, value_ref[:, window], 0)
    scale = HD**-0.5
    factor = scale * LOG2E
    count = query_ref.shape[0] // QUERY_BLOCK
    turned = keys.T

    def begin(block):
        rows = pl.ds(block * QUERY_BLOCK, QUERY_BLOCK)
        return dot_nt(keys, query_ref[rows, window]), dot_nt(values, incoming_ref[rows, window])

    following = begin(0)
    for block in range(count):
        rows = pl.ds(block * QUERY_BLOCK, QUERY_BLOCK)
        scores, prob_grad = following
        if block + 1 < count:
            following = begin(block + 1)
        probs = jnp.exp2(scores * factor - log_ref[0, :, rows])
        centre = jnp.sum(probs * prob_grad, axis=0, keepdims=True)
        score_grads[:, rows] = (probs * (prob_grad - centre) * scale).astype(BF16)
        weights[:, rows] = probs.astype(BF16)
        query_grad = dot_nn(turned, score_grads[:, rows]).T.astype(grad_ref.dtype)
        grad_ref[rows, window] = jnp.where(inside, query_grad, grad_ref[rows, window])
    key_total = dot_nn(score_grads[...], query_ref[:, window])
    value_total = dot_nn(weights[...], incoming_ref[:, window])
    for part, total in ((1, key_total), (2, value_total)):
        place = pl.ds(pl.multiple_of(start + part * features, LANES), WINDOW)
        grad_ref[:, place] = jnp.where(inside, total.astype(grad_ref.dtype), grad_ref[:, place])


def whole_block(shape, column):
    return pl.BlockSpec(shape, lambda head: (0, column), pipeline_mode=pl.Buffered(1))


def attend_forward(projected, everyone):
    rows = projected.shape[0]
    features = projected.shape[1] // 3
    tokens = everyone.shape[0]
    return pl.pallas_call(
        attend_forward_kernel,
        grid=(HEADS,),
        in_specs=[
            whole_block((rows, features), 0),
            whole_block((tokens, features), 1),
            whole_block((tokens, features), 2),
        ],
        out_specs=[
            whole_block((rows, features), 0),
            pl.BlockSpec((1, 1, rows), lambda head: (head, 0, 0)),
        ],
        out_shape=[
            jax.ShapeDtypeStruct((rows, features), BF16),
            jax.ShapeDtypeStruct((HEADS, 1, rows), F32),
        ],
        compiler_params=pltpu.CompilerParams(vmem_limit_bytes=56 * 1024 * 1024),
        cost_estimate=pl.CostEstimate(
            flops=4 * rows * tokens * HEADS * WINDOW,
            bytes_accessed=2 * (rows * 2 + tokens * 2) * features,
            transcendentals=rows * tokens * HEADS,
        ),
    )(projected, everyone, everyone)


def attend_backward(projected, everyone, incoming, log_total):
    rows = projected.shape[0]
    features = projected.shape[1] // 3
    tokens = everyone.shape[0]
    kind = BF16 if rows == tokens else F32
    return pl.pallas_call(
        attend_backward_kernel,
        grid=(HEADS,),
        in_specs=[
            whole_block((rows, features), 0),
            whole_block((tokens, features), 1),
            whole_block((tokens, features), 2),
            whole_block((rows, features), 0),
            pl.BlockSpec((1, 1, rows), lambda head: (head, 0, 0)),
        ],
        out_specs=whole_block((tokens, 3 * features), 0),
        out_shape=jax.ShapeDtypeStruct((tokens, 3 * features), kind),
        scratch_shapes=[pltpu.VMEM((tokens, rows), BF16), pltpu.VMEM((tokens, rows), BF16)],
        compiler_params=pltpu.CompilerParams(vmem_limit_bytes=56 * 1024 * 1024),
        cost_estimate=pl.CostEstimate(
            flops=10 * rows * tokens * HEADS * WINDOW,
            bytes_accessed=2 * (rows * 2 + tokens * 5) * features,
            transcendentals=rows * tokens * HEADS,
        ),
    )(projected, everyone, everyone, incoming, log_total)


class Layout:
    def __init__(self, micro, local, tokens, seq):
        self.micro, self.local, self.tokens, self.seq = micro, local, tokens, seq
        self.latents = micro * local
        self.sharers = max(1, seq // self.latents)
        self.held = max(1, self.latents // seq)
        self.span = seq // self.sharers

    def gather(self, values):
        values = values.reshape(self.latents, self.tokens, values.shape[-1])
        if self.sharers > 1:
            values = jnp.repeat(values, self.sharers, axis=0)
        moved = lax.all_to_all(values, "seq", split_axis=0, concat_axis=1, tiled=True)
        if self.sharers > 1:
            part = lax.axis_index("seq") % self.sharers
            count = self.span * self.tokens
            moved = lax.dynamic_slice_in_dim(moved, part * count, count, axis=1)
        return moved

    def scatter(self, values):
        if self.sharers > 1:
            values = jnp.concatenate([values] * self.sharers, axis=1)
        moved = lax.all_to_all(values, "seq", split_axis=1, concat_axis=0, tiled=True)
        if self.sharers > 1:
            part = lax.axis_index("seq") // self.span
            moved = moved.reshape(self.latents, self.sharers, self.tokens, values.shape[-1])
            moved = lax.dynamic_index_in_dim(moved, part, axis=1, keepdims=False)
        return moved.reshape(self.micro, self.local, self.tokens, values.shape[-1])

    def own_group(self, values, axis):
        if self.sharers == self.seq:
            return values
        count = values.shape[axis] // self.seq * self.sharers
        return lax.dynamic_slice_in_dim(
            values, lax.axis_index("seq") // self.sharers * count, count, axis=axis
        )


def on_device(
    latents,
    condition,
    cotangent,
    modulate_weight,
    modulate_bias,
    triple_weight,
    triple_bias,
    output_weight,
    output_bias,
    expand_weight,
    expand_bias,
    shrink_weight,
    shrink_bias,
):
    micro, local, tokens, features = latents.shape
    hidden = expand_weight.shape[1]
    groups = lax.axis_size("dp")
    seq = lax.axis_size("seq")
    devices = groups * seq
    place = Layout(micro, local, tokens, seq)
    held = place.held
    me = lax.axis_index("dp") * seq + lax.axis_index("seq")

    everyone_cond = lax.all_gather(condition.reshape(micro * local, features), "dp", axis=0, tiled=True)
    bias_shard = jnp.concatenate([modulate_bias, triple_bias, output_bias, expand_bias, shrink_bias])
    biases = lax.all_gather(bias_shard, AXES, axis=0, tiled=False).astype(F32)
    cuts = []
    offset = 0
    for shard in (modulate_bias, triple_bias, output_bias, expand_bias, shrink_bias):
        cuts.append(biases[:, offset : offset + shard.shape[0]].reshape(-1))
        offset += shard.shape[0]
    modulate_offset, triple_offset, output_offset, expand_offset, shrink_offset = cuts

    latent_rows = place.gather(latents)
    first_shard = jnp.concatenate([triple_weight, output_weight], axis=1)
    first_full = lax.all_gather(first_shard, AXES, axis=0, tiled=True)
    triple_full = first_full[:, : 3 * features]
    output_full = first_full[:, 3 * features :]
    expand_full = lax.all_gather(expand_weight, AXES, axis=0, tiled=True)
    shrink_full = lax.all_gather(shrink_weight, AXES, axis=0, tiled=True)

    owned = modulate_weight.shape[0]
    cond_act = jax.nn.silu(everyone_cond.astype(F32)).astype(BF16)
    act_owned = lax.dynamic_slice_in_dim(cond_act, me * owned, owned, axis=1)
    modulation_part = dot_nn(act_owned, modulate_weight)
    if place.sharers > 1:
        modulation_part = jnp.repeat(modulation_part, place.sharers, axis=0)
    modulation_parts = lax.all_to_all(modulation_part, AXES, split_axis=0, concat_axis=0, tiled=True)
    modulation = jnp.sum(modulation_parts.reshape(devices, held, -1), axis=0) + modulate_offset
    shift_one, scale_one, gate_one, shift_two, scale_two, gate_two = jnp.split(
        modulation[:, None, :], 6, axis=-1
    )

    latent_float = latent_rows.astype(F32)
    normed_one, inverse_one = norm_parts(latent_float)
    hidden_one = (normed_one * (1.0 + scale_one) + shift_one).astype(BF16)
    rows = held * latent_rows.shape[1]

    def flat(values):
        return values.reshape(rows, values.shape[-1])

    def unflat(values):
        return values.reshape(held, rows // held, values.shape[-1])

    zero = jnp.zeros((features,), F32)
    full_bias = jnp.concatenate([triple_offset[:features], zero, triple_offset[features:]])
    projected = unflat((dot_nn(flat(hidden_one), triple_full) + full_bias).astype(BF16))
    if place.sharers > 1:
        everyone = place.own_group(lax.all_gather(projected, "seq", axis=1, tiled=True), 1)
    else:
        everyone = projected
    mixed_parts, log_parts = zip(
        *(attend_forward(projected[index], everyone[index]) for index in range(held))
    )
    mixed = jnp.stack(mixed_parts) if held > 1 else mixed_parts[0][None]
    branch_one = unflat(dot_nn(flat(mixed), output_full)) + output_offset
    middle = latent_float + gate_one * branch_one
    normed_two, inverse_two = norm_parts(middle)
    hidden_two = (normed_two * (1.0 + scale_two) + shift_two).astype(BF16)
    pre_act = dot_nn(flat(hidden_two), expand_full) + expand_offset
    activated = gelu_parts(pre_act)[0].astype(BF16)
    branch_two = unflat(dot_nn(activated, shrink_full)) + shrink_offset
    output = place.scatter((middle + gate_two * branch_two).astype(BF16))

    incoming = place.gather(cotangent).astype(F32)
    branch_two_grad = (gate_two * incoming).astype(BF16)
    gate_two_grad = jnp.sum(incoming * branch_two, axis=1)
    shrink_offset_grad = jnp.sum(branch_two_grad.astype(F32), axis=(0, 1))
    shrink_grad = dot_tn(activated, flat(branch_two_grad)).astype(BF16)
    shrink_total = lax.psum_scatter(shrink_grad, AXES, scatter_dimension=0, tiled=True).astype(F32)
    act_grad = dot_nt(flat(branch_two_grad), shrink_full)
    pre_grad = (act_grad * gelu_parts(pre_act)[1]).astype(BF16)
    expand_offset_grad = jnp.sum(pre_grad.astype(F32), axis=0)
    expand_grad = dot_tn(flat(hidden_two), pre_grad).astype(BF16)
    expand_total = scatter_rows(expand_grad, devices)
    hidden_two_grad = unflat(dot_nt(pre_grad, expand_full))
    norm_grad_two, shift_two_grad, scale_two_grad = norm_back(
        hidden_two_grad, normed_two, inverse_two, scale_two
    )
    middle_grad = incoming + norm_grad_two
    branch_one_grad = (gate_one * middle_grad).astype(BF16)
    gate_one_grad = jnp.sum(middle_grad * branch_one, axis=1)
    output_offset_grad = jnp.sum(branch_one_grad.astype(F32), axis=(0, 1))
    output_grad = dot_tn(flat(mixed), flat(branch_one_grad)).astype(BF16)
    mixed_grad = unflat(dot_nt(flat(branch_one_grad), output_full).astype(BF16))
    grads = []
    for index in range(held):
        grad = attend_backward(projected[index], everyone[index], mixed_grad[index], log_parts[index])
        if place.sharers > 1:
            key_value = grad[:, features:]
            key_value = lax.psum_scatter(
                own_slots(key_value, place), "seq", scatter_dimension=0, tiled=True
            ).astype(BF16)
            grad = jnp.concatenate([grad[: rows // held, :features].astype(BF16), key_value], axis=1)
        grads.append(grad)
    triple_rows = jnp.concatenate(grads) if held > 1 else grads[0]
    column_sums = jnp.sum(triple_rows.astype(F32), axis=0)
    triple_offset_grad = jnp.concatenate([column_sums[:features], column_sums[2 * features :]])
    triple_grad = dot_tn(flat(hidden_one), triple_rows).astype(BF16)
    first_grad = jnp.concatenate([triple_grad, output_grad], axis=1)
    first_total = scatter_rows(first_grad, devices)
    hidden_one_grad = unflat(dot_nt(triple_rows, triple_full))
    norm_grad_one, shift_one_grad, scale_one_grad = norm_back(
        hidden_one_grad, normed_one, inverse_one, scale_one
    )
    latents_gradient = place.scatter((middle_grad + norm_grad_one).astype(BF16)).astype(F32)

    modulation_grad = jnp.concatenate(
        [shift_one_grad, scale_one_grad, gate_one_grad, shift_two_grad, scale_two_grad, gate_two_grad],
        axis=-1,
    )
    if place.sharers > 1:
        parts = lax.all_gather(modulation_grad, "seq", axis=0, tiled=True)
        modulation_grad = jnp.sum(place.own_group(parts, 0), axis=0, keepdims=True)
    all_grads = lax.all_gather(modulation_grad.astype(BF16), AXES, axis=0, tiled=True)
    if place.sharers > 1:
        all_grads = all_grads[:: place.sharers]
    modulate_total = dot_tn(act_owned, all_grads)
    shard = modulate_bias.shape[0]
    modulate_offset_total = jnp.sum(
        lax.dynamic_slice_in_dim(all_grads, me * shard, shard, axis=1).astype(F32), axis=0
    )
    cond_back = dot_nt(all_grads, modulate_weight)
    everyone_back = lax.all_gather(cond_back, AXES, axis=1, tiled=True)
    group_back = lax.dynamic_slice_in_dim(
        everyone_back, lax.axis_index("dp") * micro * local, micro * local, axis=0
    ).reshape(condition.shape)
    cond_float = condition.astype(F32)
    sigmoid_cond = jax.nn.sigmoid(cond_float)
    condition_gradient = group_back * (sigmoid_cond * (1.0 + cond_float * (1.0 - sigmoid_cond)))

    bias_grads = jnp.concatenate(
        [
            values.reshape(devices, -1)
            for values in (triple_offset_grad, output_offset_grad, expand_offset_grad, shrink_offset_grad)
        ],
        axis=1,
    )
    bias_total = jnp.sum(
        lax.all_to_all(bias_grads, AXES, split_axis=0, concat_axis=0, tiled=True), axis=0
    )
    bias_cuts = []
    offset = 0
    for part in (triple_bias, output_bias, expand_bias, shrink_bias):
        bias_cuts.append(bias_total[offset : offset + part.shape[0]])
        offset += part.shape[0]
    return (
        output,
        latents_gradient,
        condition_gradient,
        modulate_total,
        modulate_offset_total,
        first_total[:, : 3 * features],
        bias_cuts[0],
        first_total[:, 3 * features :],
        bias_cuts[1],
        expand_total,
        bias_cuts[2],
        shrink_total,
        bias_cuts[3],
    )


def scatter_rows(values, devices):
    rows, columns = values.shape
    slots = values.reshape(rows * columns // 1152, 1152)
    total = lax.psum_scatter(slots, AXES, scatter_dimension=0, tiled=True)
    return total.reshape(rows // devices, columns).astype(F32)


def own_slots(values, place):
    group = lax.axis_index("seq") // place.sharers
    slots = jnp.zeros((place.seq // place.sharers,) + values.shape, values.dtype)
    slots = lax.dynamic_update_index_in_dim(slots, values, group, axis=0)
    return slots.reshape(-1, values.shape[-1])


MESH = pl.DeviceIdType.MESH
ANY = pl.BlockSpec(memory_space=pl.ANY)
ROWS = 144
MATMUL_ROWS = 1024
LOW, HIGH = pl.ds(0, 80), pl.ds(80, 64)


class Here:
    def __init__(self):
        dp, self.member = lax.axis_index("dp"), lax.axis_index("seq")
        self.group = dp
        self.z, self.core = dp // 2, dp % 2
        self.index = dp * 4 + self.member
        y, x = self.member // 2, self.member % 2
        self.across_x = y * 2 + (1 - x)
        self.across_y = (1 - y) * 2 + x
        self.across = (1 - y) * 2 + (1 - x)

    def at_x(self):
        return (self.group, self.across_x)

    def at_y(self):
        return (self.group, self.across_y)

    def at_core(self):
        return (self.z * 2 + (1 - self.core), self.member)

    def at_z(self, step):
        return (lax.rem(self.z + step, 4) * 2 + self.core, self.member)

    def at_member(self, step):
        return (self.group, lax.rem(self.member + step, 4))

    def at_index(self, step):
        place = lax.rem(self.index + step, 32)
        return (place // 4, lax.rem(place, 4))


def greet(partners):
    barrier = pltpu.get_barrier_semaphore()
    for partner in partners:
        pl.semaphore_signal(barrier, inc=1, device_id=partner, device_id_type=MESH)
    pl.semaphore_wait(barrier, len(partners))


def greet_all(here):
    barrier = pltpu.get_barrier_semaphore()

    def signal(step, carry):
        pl.semaphore_signal(barrier, inc=1, device_id=here.at_index(step), device_id_type=MESH)
        return carry

    lax.fori_loop(1, 32, signal, 0)
    pl.semaphore_wait(barrier, 31)


class Wires:
    def __init__(self, sent, landed):
        self.sent, self.landed = sent, landed

    def copy(self, number, source, target, partner):
        return pltpu.make_async_remote_copy(
            src_ref=source,
            dst_ref=target,
            send_sem=self.sent.at[number],
            recv_sem=self.landed.at[number],
            device_id=partner,
            device_id_type=MESH,
        )


def everyone(here, source_of, target, sent, landed):
    def copy_of(step):
        place = lax.rem(here.index + step, 32)
        return pltpu.make_async_remote_copy(
            src_ref=source_of(place),
            dst_ref=target.at[here.index],
            send_sem=sent.at[step],
            recv_sem=landed.at[step],
            device_id=here.at_index(step),
            device_id_type=MESH,
        )

    def start(step, carry):
        copy_of(step).start()
        return carry

    def wait(step, carry):
        copy_of(step).wait()
        return carry

    lax.fori_loop(1, 32, start, 0)
    return lambda: lax.fori_loop(1, 32, wait, 0)


def same_core(here, source, target, sent, landed):
    mine = here.z * 4 + here.member

    def copy_of(step):
        place = lax.rem(mine + step, 16)
        return pltpu.make_async_remote_copy(
            src_ref=source.at[place],
            dst_ref=target.at[mine],
            send_sem=sent.at[step],
            recv_sem=landed.at[step],
            device_id=(place // 4 * 2 + here.core, lax.rem(place, 4)),
            device_id_type=MESH,
        )

    def start(step, carry):
        copy_of(step).start()
        return carry

    def wait(step, carry):
        copy_of(step).wait()
        return carry

    lax.fori_loop(1, 16, start, 0)
    return lambda: lax.fori_loop(1, 16, wait, 0)


def introduce_kernel(
    note_ref, shard_ref, shrink_ref, notes_ref, blocks_ref, quad_ref, column_ref, landing, wide, buffer,
    note_sent, note_landed, sent, landed, local,
):
    here = Here()
    greet_all(here)
    wires = Wires(sent, landed)

    def columns(place):
        return shard_ref.at[:, :, pl.ds(pl.multiple_of(place * 1152, LANES), 1152)]

    quads = []
    for step in range(1, 4):
        place = lax.rem(here.member + step, 4)
        quads.append(wires.copy(step - 1, columns(place), landing.at[here.member], here.at_member(step)))
    highs = [
        wires.copy(2 + step, shrink_ref.at[HIGH], quad_ref.at[here.member], here.at_member(step))
        for step in range(1, 4)
    ]
    lows = [
        wires.copy(5 + step, shrink_ref.at[LOW], column_ref.at[here.z], here.at_z(step)) for step in range(1, 4)
    ]
    for copy in quads + lows:
        copy.start()
    keeps = [
        Bounce(shrink_ref.at[LOW], buffer.at[LOW], column_ref.at[here.z], local.at[2]),
        Bounce(shrink_ref.at[HIGH], buffer.at[HIGH], quad_ref.at[here.member], local.at[3]),
    ]
    for keep in keeps:
        keep.start()
    done = everyone(here, lambda place: note_ref.at[0], notes_ref, note_sent, note_landed)
    own = pltpu.make_async_copy(columns(here.member), landing.at[here.member], local.at[0])
    own.start()
    mine = pltpu.make_async_copy(note_ref.at[0], notes_ref.at[here.index], local.at[1])
    mine.start()
    for copy in highs:
        copy.start()
    own.wait()
    for keep in keeps:
        keep.go_on()
    for copy in quads:
        copy.wait_recv()
    for part in range(2):
        for member in range(4):
            wide[member * 36 : member * 36 + 36, :] = landing[member, part].astype(F32)[:36]
        blocks_ref[part] = wide[...].astype(BF16)
    for copy in quads:
        copy.wait_send()
    for copy in highs + lows + keeps:
        copy.wait()
    mine.wait()
    done()


def introduce(note, shard, shrink):
    return pl.pallas_call(
        introduce_kernel,
        in_specs=[ANY, ANY, ANY],
        out_specs=[ANY, pl.BlockSpec(memory_space=pltpu.VMEM), ANY, ANY],
        out_shape=[
            jax.ShapeDtypeStruct((32,) + note.shape[1:], note.dtype),
            jax.ShapeDtypeStruct((2, ROWS, 1152), BF16),
            jax.ShapeDtypeStruct((4, HIGH.size, 1152), BF16),
            jax.ShapeDtypeStruct((4, LOW.size, 1152), BF16),
        ],
        scratch_shapes=[
            pltpu.VMEM((4,) + shard.shape[:2] + (1152,), BF16),
            pltpu.VMEM((ROWS, 1152), F32),
            pltpu.VMEM((ROWS, 1152), BF16),
            pltpu.SemaphoreType.DMA((32,)),
            pltpu.SemaphoreType.DMA((32,)),
            pltpu.SemaphoreType.DMA((9,)),
            pltpu.SemaphoreType.DMA((9,)),
            pltpu.SemaphoreType.DMA((4,)),
        ],
        compiler_params=pltpu.CompilerParams(collective_id=1, has_side_effects=True),
    )(note, shard, shrink)


class Bounce:
    def __init__(self, source, buffer, target, semaphore):
        self.first = pltpu.make_async_copy(source, buffer, semaphore)
        self.second = pltpu.make_async_copy(buffer, target, semaphore)

    def start(self):
        self.first.start()

    def go_on(self):
        self.first.wait()
        self.second.start()

    def wait(self):
        self.second.wait()


ARRIVALS = (0, 1, 3, 2)


class Gather:
    COPIES = 31

    def __init__(self, here, place, own, sent, landed):
        self.here, self.place, self.own = here, place, own
        self.wires = Wires(sent, landed)

    def z_of(self, order):
        return lax.rem(self.here.z + 4 - ARRIVALS[order], 4)

    def along(self, step, block):
        here = self.here
        return self.wires.copy(step - 1, block, self.own(here.z), here.at_z(step))

    def begin(self, block):
        for step in (1, 3, 2):
            self.along(step, block).start()

    def sideways(self, kind, order):
        here = self.here
        z = self.z_of(order)
        partner = (here.at_x, here.at_y, here.at_core)[kind]()
        return self.wires.copy(
            3 + kind * 4 + order, self.own(z), self.place(here.member, z, here.core), partner
        )

    def passed(self, kind, order):
        here = self.here
        z = self.z_of(order)
        if kind == 3:
            member = here.across_x if order >= 2 else here.across_y
            partner = here.at_y() if order >= 2 else here.at_x()
        else:
            member = (here.across_x, here.across_y, here.across)[kind]
            partner = here.at_core()
        ref = self.place(member, z, here.core)
        return self.wires.copy(15 + kind * 4 + order, ref, ref, partner)

    def spread(self, order):
        for kind in range(3):
            self.sideways(kind, order).start()

    def relay(self, order):
        self.sideways(0, order).wait_recv()
        if order >= 2:
            self.passed(3, order).start()
        self.passed(0, order).start()
        self.sideways(1, order).wait_recv()
        if order < 2:
            self.passed(3, order).start()
        self.passed(1, order).start()

    def close(self, order):
        self.passed(3, order).wait_recv()
        self.passed(2, order).start()

    def end(self):
        for order in range(4):
            self.sideways(2, order).wait_recv()
            for kind in range(3):
                self.passed(kind, order).wait_recv()
        for order in range(4):
            for kind in range(3):
                self.sideways(kind, order).wait_send()
            for kind in range(4):
                self.passed(kind, order).wait_send()


class Column:
    COPIES = 13

    def __init__(self, here, full, quad, sent, landed):
        self.here, self.full, self.quad = here, full, quad
        self.wires = Wires(sent, landed)

    def pass_on(self, way, turn):
        here = self.here
        target = self.full.at[here.z - way * turn, here.core, :, HIGH]
        partner = ((here.z + way) * 2 + here.core, here.member)
        return self.wires.copy(turn + (3 if way < 0 else 0), self.quad if turn == 0 else target, target, partner)

    def came(self, way, turn):
        here = self.here
        return self.full.at[here.z - way * (turn + 1), here.core, :, HIGH]

    def arrival(self, way, turn):
        ref = self.came(way, turn)
        return self.wires.copy(turn + (3 if way < 0 else 0), ref, ref, self.here.at_core())

    def across(self, way, turn):
        ref = self.came(way, turn)
        return self.wires.copy(6 + turn + (3 if way < 0 else 0), ref, ref, self.here.at_core())

    def own_across(self):
        here = self.here
        return self.wires.copy(12, self.quad, self.full.at[here.z, here.core, :, HIGH], here.at_core())

    def sends(self, way, turn):
        z = self.here.z
        return (z < 3) & (z >= turn) if way > 0 else (z > 0) & (z <= 3 - turn)

    def comes(self, way, turn):
        z = self.here.z
        return z >= turn + 1 if way > 0 else z <= 2 - turn

    def each(self, test, turn, action):
        for way in (1, -1):
            pl.when(test(way, turn))(lambda way=way: action(way, turn))

    def begin(self):
        self.each(self.sends, 0, lambda way, turn: self.pass_on(way, turn).start())
        self.own_across().start()

    def end_first(self):
        self.each(self.comes, 0, lambda way, turn: self.arrival(way, turn).wait_recv())
        self.each(self.sends, 0, lambda way, turn: self.pass_on(way, turn).wait_send())
        self.own_across().wait()

    def step(self, turn):
        if turn > 1:
            self.each(self.comes, turn - 1, lambda way, turn: self.arrival(way, turn).wait_recv())
        if turn < 3:
            self.each(self.sends, turn, lambda way, turn: self.pass_on(way, turn).start())
        self.each(self.comes, turn - 1, lambda way, turn: self.across(way, turn).start())

    def end(self):
        for turn in range(3):
            self.each(self.comes, turn, lambda way, turn: self.across(way, turn).wait())
        for turn in range(1, 3):
            self.each(self.sends, turn, lambda way, turn: self.pass_on(way, turn).wait_send())


def open_kernel(
    block_ref, quad_ref, part_ref, token_ref, full_ref, expand_ref, shrink_ref, parts_ref, tokens_ref,
    part_mine, part_half, block_buffer, token_buffer, quad_buffer, part_sent, part_landed, sent, landed, more_sent, more_landed, local,
):
    here = Here()
    greet_all(here)
    more = Wires(more_sent, more_landed)
    half = more.copy(0, part_ref.at[1 - here.core], part_half, here.at_core())
    half.start()
    load = pltpu.make_async_copy(part_ref.at[here.core], part_mine, local.at[0])
    load.start()
    first = Gather(
        here,
        lambda member, z, core: full_ref.at[member, z, core],
        lambda z: full_ref.at[here.member, z, here.core],
        sent.at[0],
        landed.at[0],
    )
    second = Gather(here, None, lambda z: expand_ref.at[z], sent.at[1], landed.at[1])
    third = Column(here, shrink_ref, quad_ref, more_sent.at[pl.ds(4, 13)], more_landed.at[pl.ds(4, 13)])
    first.begin(block_ref.at[0])
    mine = here.z * 4 + here.member
    own = [
        Bounce(block_ref.at[0], block_buffer.at[0], first.own(here.z), local.at[1]),
        Bounce(block_ref.at[1], block_buffer.at[1], second.own(here.z), local.at[2]),
        Bounce(token_ref.at[here.member], token_buffer, tokens_ref.at[here.member], local.at[3]),
        Bounce(quad_ref, quad_buffer, shrink_ref.at[here.z, here.core, :, HIGH], local.at[5]),
    ]
    for copy in own:
        copy.start()
    moved = []
    for step in range(1, 4):
        place = lax.rem(here.member + step, 4)
        moved.append(more.copy(step, token_ref.at[place], tokens_ref.at[here.member], here.at_member(step)))
    for copy in moved:
        copy.start()
    for copy in own:
        copy.go_on()
    load.wait()
    half.wait()

    def add(place, carry):
        part_mine[place] += part_half[place]
        return carry

    lax.fori_loop(0, 16, add, 0)
    done = same_core(here, part_mine, parts_ref, part_sent, part_landed)
    keep = pltpu.make_async_copy(part_mine.at[mine], parts_ref.at[mine], local.at[4])
    keep.start()
    own[0].wait()
    first.spread(0)
    for order in range(1, 4):
        first.along(ARRIVALS[order], block_ref.at[0]).wait_recv()
        first.spread(order)
    second.begin(block_ref.at[1])
    third.begin()
    for order in range(4):
        first.relay(order)
    for order in range(4):
        first.close(order)
    first.end()
    third.end_first()
    for step in (1, 3, 2):
        first.along(step, block_ref.at[0]).wait_send()
        second.along(step, block_ref.at[1]).wait()
    for copy in moved:
        copy.wait()
    for copy in own[1:]:
        copy.wait()
    keep.wait()
    done()


def open_up(blocks, quad, parts, tokens):
    column = jax.ShapeDtypeStruct((4, ROWS, 1152), BF16)
    return pl.pallas_call(
        open_kernel,
        in_specs=[ANY] * 4,
        out_specs=[ANY] * 5,
        out_shape=[
            jax.ShapeDtypeStruct((4, 4, 2, ROWS, 1152), BF16),
            column,
            jax.ShapeDtypeStruct((4, 2, 4, ROWS, 1152), BF16),
            jax.ShapeDtypeStruct(parts.shape[1:], parts.dtype),
            jax.ShapeDtypeStruct(tokens.shape, tokens.dtype),
        ],
        scratch_shapes=[
            pltpu.VMEM(parts.shape[1:], F32),
            pltpu.VMEM(parts.shape[1:], F32),
            pltpu.VMEM((2, ROWS, 1152), BF16),
            pltpu.VMEM(tokens.shape[1:], BF16),
            pltpu.VMEM(quad.shape, BF16),
            pltpu.SemaphoreType.DMA((16,)),
            pltpu.SemaphoreType.DMA((16,)),
            pltpu.SemaphoreType.DMA((2, 31)),
            pltpu.SemaphoreType.DMA((2, 31)),
            pltpu.SemaphoreType.DMA((17,)),
            pltpu.SemaphoreType.DMA((17,)),
            pltpu.SemaphoreType.DMA((6,)),
        ],
        compiler_params=pltpu.CompilerParams(collective_id=2, has_side_effects=True),
    )(blocks, quad, parts, tokens)


MIX_AT = 19
EXPAND_AT = MIX_AT + 4
FORWARD_STEPS = EXPAND_AT + 4


def forward_kernel(
    hidden_ref, weight_ref, bias_ref, latent_ref, scaling_ref, expand_bias_ref, expand_column, shrink_given, shrink_column, incoming_ref,
    projected_ref, mixed_ref, log_ref, branch_ref, middle_ref, second_ref, pre_ref, active_ref,
    expand_full, shrink_full, incomings_ref,
    chunk, token_buffer, sent, landed, more_sent, more_landed, local, fetch,
):
    step = pl.program_id(0)
    here = Here()
    features = hidden_ref.shape[1]
    second = Gather(
        here,
        lambda member, z, core: expand_full.at[member, z, core],
        lambda z: expand_column.at[z],
        sent.at[0],
        landed.at[0],
    )
    fourth = Gather(
        here,
        lambda member, z, core: shrink_full.at[z, core, member, LOW],
        lambda z: shrink_column.at[z],
        sent.at[1],
        landed.at[1],
    )
    third = Column(here, shrink_full, None, more_sent.at[pl.ds(0, 13)], more_landed.at[pl.ds(0, 13)])
    more = Wires(more_sent, more_landed)
    own = (
        Bounce(expand_column, chunk.at[0, :, 0], expand_full.at[here.member, :, here.core], local.at[0]),
        Bounce(incoming_ref.at[here.member], token_buffer, incomings_ref.at[here.member], local.at[1]),
        Bounce(shrink_column, chunk.at[1, :, 0, LOW], shrink_full.at[:, here.core, here.member, LOW], local.at[2]),
    )

    def fetch_chunk(part):
        return pltpu.make_async_copy(expand_full.at[part], chunk.at[part % 2], fetch.at[part % 2])

    def move(number):
        place = lax.rem(here.member + number, 4)
        return more.copy(
            12 + number, incoming_ref.at[place], incomings_ref.at[here.member], here.at_member(number)
        )

    @pl.when(step == 0)
    def _():
        greet_near(here)
        for order in range(4):
            second.spread(order)
        third.step(1)
        for copy in own:
            copy.start()

    @pl.when(step == 1)
    def _():
        for copy in own:
            copy.go_on()

    def relay_expand():
        for order in range(4):
            second.relay(order)

    def spread_shrink():
        for order in range(4):
            fourth.spread(order)

    def relay_shrink():
        for order in range(4):
            fourth.relay(order)

    def start_moves():
        for number in (2, 1, 3):
            move(number).start()

    def close_expand():
        for order in range(4):
            second.close(order)

    def finish_expand():
        second.end()
        for copy in own:
            copy.wait()
        fetch_chunk(0).start()
        fetch_chunk(1).start()

    def finish():
        for order in range(4):
            fourth.close(order)
        third.end()
        fourth.end()
        for number in (1, 2, 3):
            move(number).wait()

    for turn, action in (
        (10, functools.partial(third.step, 2)),
        (13, relay_expand),
        (19, spread_shrink),
        (20, functools.partial(third.step, 3)),
        (21, close_expand),
        (1, start_moves),
        (EXPAND_AT + 2, relay_shrink),
        (EXPAND_AT - 1, finish_expand),
    ):
        pl.when(step == turn)(action)

    def row_blocks(body):
        def one(block, carry):
            body(pl.ds(pl.multiple_of(block * MATMUL_ROWS, MATMUL_ROWS), MATMUL_ROWS))
            return carry

        lax.fori_loop(0, hidden_ref.shape[0] // MATMUL_ROWS, one, 0)

    for part in range(3):

        @pl.when(step == part)
        def _():
            def project(rows):
                values = dot_nn(hidden_ref[rows, :], weight_ref[0]) + bias_ref[part]
                projected_ref[rows, part * features : (part + 1) * features] = values.astype(BF16)

            row_blocks(project)

    @pl.when((step >= 3) & (step < MIX_AT))
    def _():
        forward_head(step - 3, features, projected_ref, mixed_ref, log_ref)

    @pl.when((step >= MIX_AT) & (step < EXPAND_AT))
    def _():
        rows = pl.ds(pl.multiple_of((step - MIX_AT) * 256, 256), 256)
        branch = dot_nn(mixed_ref[rows, :], weight_ref[0]) + bias_ref[3]
        branch_ref[...] = branch
        middle = latent_ref[...].astype(F32) + scaling_ref[0] * branch
        middle_ref[...] = middle
        normed, _ = norm_parts(middle)
        second_ref[rows, :] = (normed * (1.0 + scaling_ref[2]) + scaling_ref[1]).astype(BF16)

    for part in range(4):

        @pl.when(step == EXPAND_AT + part)
        def _():
            fetch_chunk(part).wait()

            def expand(rows):
                weight = chunk[part % 2].reshape(features, features)
                values = dot_nn(second_ref[rows, :], weight) + expand_bias_ref[part]
                pre_ref[rows, :] = values
                active_ref[rows, :] = gelu_parts(values)[0].astype(BF16)

            row_blocks(expand)
            if part + 2 < 4:
                fetch_chunk(part + 2).start()

    pl.when(step == FORWARD_STEPS - 1)(finish)


def forward_head(head, features, projected_ref, mixed_ref, log_ref):
    last = features // LANES - WINDOW // LANES
    start = jnp.minimum(head * HD // LANES, last) * LANES
    first = head * HD - start
    lane = lax.broadcasted_iota(jnp.int32, (1, WINDOW), 1)
    inside = (lane >= first) & (lane < first + HD)

    def window(part):
        return pl.ds(pl.multiple_of(start + part * features, LANES), WINDOW)

    keys = jnp.where(inside, projected_ref[:, window(1)], 0)
    values = jnp.where(inside, projected_ref[:, window(2)], 0)
    turned = values.T
    factor = HD**-0.5 * LOG2E
    count = projected_ref.shape[0] // QUERY_BLOCK

    def score(block):
        return dot_nt(keys, projected_ref[pl.ds(block * QUERY_BLOCK, QUERY_BLOCK), window(0)])

    following = score(0)
    for block in range(count):
        rows = pl.ds(block * QUERY_BLOCK, QUERY_BLOCK)
        scores = following
        if block + 1 < count:
            following = score(block + 1)
        peak = jnp.max(scores, axis=0, keepdims=True)
        powers = jnp.exp2(scores * factor - peak * factor)
        total = jnp.sum(powers, axis=0, keepdims=True)
        log_ref[0, :, rows] = peak * factor + jnp.log2(total)
        weights = (powers * (1.0 / total)).astype(BF16)
        mixed = dot_nn(turned, weights).T.astype(BF16)
        mixed_ref[rows, window(0)] = jnp.where(inside, mixed, mixed_ref[rows, window(0)])


def greet_near(here):
    greet(
        [here.at_member(step) for step in range(1, 4)]
        + [here.at_z(step) for step in range(1, 4)]
        + [here.at_core()]
    )


def forward(hidden, weights, biases, latents, scalings, expand_bias, expand_column, shrink, shrink_column, incoming):
    rows, features = hidden.shape

    def clip(step, low, high):
        return jnp.minimum(jnp.maximum(step - low, 0), high)

    def everything(shape):
        return pl.BlockSpec(shape, lambda step: (0,) * len(shape), pipeline_mode=pl.Buffered(1))

    by_rows = pl.BlockSpec((256, features), lambda step: (clip(step, MIX_AT, 3), 0))
    by_part = pl.BlockSpec((rows, features), lambda step: (0, clip(step, EXPAND_AT, 3)))
    tokens = jax.ShapeDtypeStruct((rows, features), BF16)
    wide = jax.ShapeDtypeStruct((rows, features), F32)
    return pl.pallas_call(
        forward_kernel,
        grid=(FORWARD_STEPS,),
        input_output_aliases={7: 9},
        in_specs=[
            everything((rows, features)),
            pl.BlockSpec((1, features, features), lambda step: (jnp.minimum(step, 3), 0, 0)),
            everything((4, 1, features)),
            by_rows,
            everything((3, 1, features)),
            everything((4, 1, features)),
            ANY,
            ANY,
            ANY,
            ANY,
        ],
        out_specs=[
            everything((rows, 3 * features)),
            everything((rows, features)),
            pl.BlockSpec((1, 1, rows), lambda step: (clip(step, 3, HEADS - 1), 0, 0)),
            by_rows,
            by_rows,
            everything((rows, features)),
            by_part,
            by_part,
            ANY,
            ANY,
            ANY,
        ],
        out_shape=[
            jax.ShapeDtypeStruct((rows, 3 * features), BF16),
            tokens,
            jax.ShapeDtypeStruct((HEADS, 1, rows), F32),
            wide,
            wide,
            tokens,
            jax.ShapeDtypeStruct((rows, 4 * features), F32),
            jax.ShapeDtypeStruct((rows, 4 * features), BF16),
            jax.ShapeDtypeStruct((4, 4, 2, ROWS, 1152), BF16),
            jax.ShapeDtypeStruct((4, 2, 4, ROWS, 1152), BF16),
            jax.ShapeDtypeStruct(incoming.shape, BF16),
        ],
        scratch_shapes=[
            pltpu.VMEM((2, 4, 2, ROWS, 1152), BF16),
            pltpu.VMEM(incoming.shape[1:], BF16),
            pltpu.SemaphoreType.DMA((2, 31)),
            pltpu.SemaphoreType.DMA((2, 31)),
            pltpu.SemaphoreType.DMA((16,)),
            pltpu.SemaphoreType.DMA((16,)),
            pltpu.SemaphoreType.DMA((3,)),
            pltpu.SemaphoreType.DMA((2,)),
        ],
        compiler_params=pltpu.CompilerParams(
            collective_id=5, has_side_effects=True, vmem_limit_bytes=60 * 1024 * 1024
        ),
    )(hidden, weights, biases, latents, scalings, expand_bias, expand_column, shrink, shrink_column, incoming)


class Half:
    COPIES = 13

    def __init__(self, here, rows, source, total, kept, crossed, relayed, beside, along, sent, landed, local):
        self.here, self.rows, self.source, self.total, self.local = here, rows, source, total, local
        self.kept, self.crossed, self.relayed, self.beside, self.pieces = kept, crossed, relayed, beside, along
        self.wires = Wires(sent, landed)
        self.order = (here.across, here.across_x, here.across_y, here.member)

    def load(self, turn):
        return pltpu.make_async_copy(
            self.source(self.order[turn], self.here.core).at[:, self.rows],
            self.kept.at[turn, :, self.rows],
            self.local.at[turn],
        )

    def cross(self, turn):
        here = self.here
        return self.wires.copy(
            turn,
            self.source(self.order[turn], 1 - here.core).at[:, self.rows],
            self.crossed.at[turn, :, self.rows],
            here.at_core(),
        )

    def relay(self, way):
        partner = (self.here.at_x, self.here.at_y)[way]()
        half = pl.ds(2 - 2 * way, 2)
        return self.wires.copy(
            4 + way, self.kept.at[0, half, self.rows], self.relayed.at[way, :, self.rows], partner
        )

    def side(self, way, part):
        partner = (self.here.at_x, self.here.at_y)[way]()
        half = pl.ds(2 * part, 2)
        return self.wires.copy(
            6 + 2 * way + part,
            self.kept.at[1 + way, half, self.rows],
            self.beside.at[way, half, self.rows],
            partner,
        )

    def along(self, step):
        z = lax.rem(self.here.z + step, 4)
        return self.wires.copy(
            9 + step, self.kept.at[3, z, self.rows], self.pieces.at[step - 1, self.rows], self.here.at_z(step)
        )

    def begin(self):
        for turn in range(4):
            self.cross(turn).start()
            self.load(turn).start()

    def add_crossed(self, turn):
        self.load(turn).wait()
        self.cross(turn).wait_recv()

        def add(z, carry):
            mine = self.kept[turn, z, self.rows, :].astype(F32)
            self.kept[turn, z, self.rows, :] = (mine + self.crossed[turn, z, self.rows, :].astype(F32)).astype(BF16)
            return carry

        lax.fori_loop(0, 4, add, 0)

    def add_relayed(self, turn, way, first):
        def add(z, carry):
            mine = self.kept[turn, first + z, self.rows, :].astype(F32)
            self.kept[turn, first + z, self.rows, :] = (
                mine + self.relayed[way, z, self.rows, :].astype(F32)
            ).astype(BF16)
            return carry

        lax.fori_loop(0, 2, add, 0)

    def diagonal(self):
        self.add_crossed(0)
        self.relay(1).start()
        self.relay(0).start()

    def direct(self):
        self.add_crossed(1)
        self.side(0, 1).start()
        self.add_crossed(2)
        self.side(1, 0).start()
        self.add_crossed(3)

    def relays(self):
        self.relay(1).wait_recv()
        self.add_relayed(1, 1, 0)
        self.side(0, 0).start()
        self.relay(0).wait_recv()
        self.add_relayed(2, 0, 2)
        self.side(1, 1).start()

    def three(self, z):
        return (
            self.kept[3, z, self.rows, :].astype(F32)
            + self.beside[0, z, self.rows, :].astype(F32)
            + self.beside[1, z, self.rows, :].astype(F32)
        )

    def along_z(self):
        here = self.here
        for way in range(2):
            for part in range(2):
                self.side(way, part).wait_recv()
        for step in (2, 1, 3):
            z = lax.rem(here.z + step, 4)
            self.kept[3, z, self.rows, :] = self.three(z).astype(BF16)
            self.along(step).start()
        self.total[self.rows, :] = self.three(here.z)

    def finish(self):
        for step in (1, 3, 2):
            self.along(step).wait_recv()
        pieces = [self.pieces[step, self.rows, :].astype(F32) for step in range(3)]
        self.total[self.rows, :] += pieces[0] + pieces[1] + pieces[2]
        for turn in range(4):
            self.cross(turn).wait_send()
        for way in range(2):
            self.relay(way).wait_send()
            for part in range(2):
                self.side(way, part).wait_send()
        for step in range(1, 4):
            self.along(step).wait_send()


class Reduce:
    SCRATCH = (
        pltpu.VMEM((4, 4, ROWS, 1152), BF16),
        pltpu.VMEM((4, 4, ROWS, 1152), BF16),
        pltpu.VMEM((2, 2, ROWS, 1152), BF16),
        pltpu.VMEM((2, 4, ROWS, 1152), BF16),
        pltpu.VMEM((3, ROWS, 1152), BF16),
        pltpu.SemaphoreType.DMA((26,)),
        pltpu.SemaphoreType.DMA((26,)),
        pltpu.SemaphoreType.DMA((8,)),
    )

    def __init__(self, here, source, total, *scratch):
        buffers, (sent, landed, local) = scratch[:5], scratch[5:]
        self.halves = [
            Half(
                here,
                rows,
                source,
                total,
                *buffers,
                sent.at[pl.ds(13 * part, 13)],
                landed.at[pl.ds(13 * part, 13)],
                local.at[pl.ds(4 * part, 4)],
            )
            for part, rows in enumerate((pl.ds(0, 80), pl.ds(80, 64)))
        ]

    def begin(self):
        for half in self.halves:
            half.begin()

    def steps(self):
        first, second = self.halves
        return (
            (0.0, self.begin),
            (0.11, first.diagonal),
            (0.26, first.direct),
            (0.26, first.relays),
            (0.27, second.diagonal),
            (0.56, second.direct),
            (0.57, second.relays),
            (0.58, first.along_z),
            (0.84, second.along_z),
            (1.0, first.finish),
            (1.0, second.finish),
        )


def backward_reduce_kernel(
    query_ref, key_ref, value_ref, incoming_ref, log_ref, source_ref, grad_ref, total_ref,
    key_total, value_total, *scratch
):
    head = pl.program_id(0)
    here = Here()
    reduce = Reduce(here, lambda member, core: source_ref.at[member, :, core], total_ref, *scratch)

    @pl.when(head == 0)
    def _():
        greet((here.at_x(), here.at_y(), here.at_core(), here.at_z(1), here.at_z(2), here.at_z(3)))

    steps = reduce.steps()
    for share, action in steps[:-2]:
        pl.when(head == round(share * HEADS))(action)
    attend_backward_kernel(
        query_ref, key_ref, value_ref, incoming_ref, log_ref, grad_ref, key_total, value_total
    )
    for _, action in steps[-2:]:
        pl.when(head == HEADS - 1)(action)


def attend_backward_reduce(projected, incoming, log_total, source):
    rows = projected.shape[0]
    features = projected.shape[1] // 3
    return pl.pallas_call(
        backward_reduce_kernel,
        grid=(HEADS,),
        in_specs=[whole_block((rows, features), part) for part in (0, 1, 2, 0)]
        + [pl.BlockSpec((1, 1, rows), lambda head: (head, 0, 0)), ANY],
        out_specs=[whole_block((rows, 3 * features), 0), whole_block((ROWS, features), 0)],
        out_shape=[
            jax.ShapeDtypeStruct((rows, 3 * features), BF16),
            jax.ShapeDtypeStruct((ROWS, features), F32),
        ],
        scratch_shapes=[pltpu.VMEM((rows, rows), BF16), pltpu.VMEM((rows, rows), BF16), *Reduce.SCRATCH],
        compiler_params=pltpu.CompilerParams(
            collective_id=6, has_side_effects=True, vmem_limit_bytes=58 * 1024 * 1024
        ),
    )(projected, projected, projected, incoming, log_total, source)


def clipped(step, low, high):
    return jnp.minimum(jnp.maximum(step - low, 0), high)


def everything(shape):
    return pl.BlockSpec(shape, lambda step: (0,) * len(shape), pipeline_mode=pl.Buffered(1))


def turn_kernel(
    active_ref, shrink_ref, middle_ref, incoming_ref, gate_ref, bias_ref, token_ref, back_ref, grads_ref, sums_ref, total
):
    step = pl.program_id(0)

    @pl.when(step == 0)
    def _():
        sums_ref[...] = jnp.zeros_like(sums_ref)
        total[...] = dot_nn(active_ref[...], shrink_ref[...])

    @pl.when((step > 0) & (step < 4))
    def _():
        total[...] += dot_nn(active_ref[...], shrink_ref[...])

    @pl.when((step >= 4) & (step < 8))
    def _():
        rows = pl.ds(pl.multiple_of((step - 4) * 256, 256), 256)
        branch = total[rows, :] + bias_ref[...]
        incoming = incoming_ref[0].astype(F32)
        token_ref[0] = (middle_ref[...] + gate_ref[...] * branch).astype(BF16)
        back = (gate_ref[...] * incoming).astype(BF16)
        back_ref[rows, :] = back
        sums_ref[0:1, :] += jnp.sum(incoming * branch, axis=0, keepdims=True)
        sums_ref[1:2, :] += jnp.sum(back.astype(F32), axis=0, keepdims=True)

    @pl.when(step >= 8)
    def _():
        width = active_ref.shape[1] // 3
        for part in range(3):
            columns = slice(part * width, (part + 1) * width)
            grads_ref[0, columns, :] = dot_tn(active_ref[:, columns], back_ref[...]).astype(BF16)


def turn(active, shrink, middle, incoming, gate, bias):
    rows, features = middle.shape
    by_member = pl.BlockSpec((1, 256, features), lambda step: (clipped(step, 4, 3), 0, 0))
    return pl.pallas_call(
        turn_kernel,
        grid=(12,),
        in_specs=[
            pl.BlockSpec((rows, features), lambda step: (0, jnp.where(step < 8, jnp.minimum(step, 3), step - 8))),
            pl.BlockSpec((features, features), lambda step: (jnp.minimum(step, 3), 0)),
            pl.BlockSpec((256, features), lambda step: (clipped(step, 4, 3), 0)),
            by_member,
            everything((1, features)),
            everything((1, features)),
        ],
        out_specs=[
            by_member,
            everything((rows, features)),
            pl.BlockSpec((1, features, features), lambda step: (clipped(step, 8, 3), 0, 0)),
            everything((8, features)),
        ],
        out_shape=[
            jax.ShapeDtypeStruct(incoming.shape, BF16),
            jax.ShapeDtypeStruct((rows, features), BF16),
            jax.ShapeDtypeStruct((4, features, features), BF16),
            jax.ShapeDtypeStruct((8, features), F32),
        ],
        scratch_shapes=[pltpu.VMEM((rows, features), F32)],
        compiler_params=pltpu.CompilerParams(vmem_limit_bytes=56 * 1024 * 1024),
    )(active, shrink, middle, incoming, gate, bias)


NORM_AT = 12
BACK_STEPS = NORM_AT + 5
BACK_SHARE = 13


def back_kernel(
    back_ref, second_ref, pre_ref, shrink_ref, expand_ref, middle_ref, branch_ref, incoming_ref, mixed_ref, weight_ref,
    scaling_ref, source_ref, token_ref,
    expand_grad_ref, expand_sum_ref, middle_grad_ref, mixed_grad_ref, output_grad_ref, sums_ref, block_ref, tokens_ref,
    total, slope, branch_back, buffer, sent, landed, local, *scratch
):
    step = pl.program_id(0)
    here = Here()
    reduce = Reduce(here, lambda member, core: source_ref.at[:, core, member], block_ref, *scratch)

    wires = Wires(sent, landed)

    def move(number):
        place = lax.rem(here.member + number, 4)
        return wires.copy(number - 1, token_ref.at[place], tokens_ref.at[here.member], here.at_member(number))

    own = Bounce(token_ref.at[here.member], buffer, tokens_ref.at[here.member], local.at[0])

    @pl.when(step == 0)
    def _():
        greet_near(here)
        own.start()
        sums_ref[...] = jnp.zeros_like(sums_ref)

    @pl.when(step == 9)
    def _():
        own.go_on()
        for number in (2, 1, 3):
            move(number).start()

    @pl.when(step == 0)
    def _():
        total[...] = jnp.zeros_like(total)

    steps = reduce.steps()
    for share, action in steps[:-2]:
        pl.when(step == round(share * BACK_SHARE))(action)

    @pl.when(step < NORM_AT)
    def _():
        def one(block, carry):
            rows = pl.ds(pl.multiple_of(block * MATMUL_ROWS, MATMUL_ROWS), MATMUL_ROWS)
            active_grad = dot_nt(back_ref[rows, :], shrink_ref[...])
            grad = (active_grad * gelu_parts(pre_ref[rows, :])[1]).astype(BF16)
            slope[rows, :] = grad
            total[rows, :] += dot_nt(grad, expand_ref[0])
            return carry

        lax.fori_loop(0, total.shape[0] // MATMUL_ROWS, one, 0)
        expand_sum_ref[0] = jnp.sum(slope[...].astype(F32), axis=0, keepdims=True)
        expand_grad_ref[0] = dot_tn(second_ref[...], slope[...]).astype(BF16)

    @pl.when((step >= NORM_AT) & (step < NORM_AT + 4))
    def _():
        rows = pl.ds(pl.multiple_of((step - NORM_AT) * 256, 256), 256)
        grad = total[rows, :]
        normed, inverse = norm_parts(middle_ref[...])
        sums_ref[1:2, :] += jnp.sum(grad, axis=0, keepdims=True)
        sums_ref[2:3, :] += jnp.sum(grad * normed, axis=0, keepdims=True)
        normed_grad = grad * (1.0 + scaling_ref[1])
        mean_first = jnp.mean(normed_grad, axis=-1, keepdims=True)
        mean_second = jnp.mean(normed_grad * normed, axis=-1, keepdims=True)
        middle_grad = incoming_ref[0].astype(F32) + inverse * (normed_grad - mean_first - normed * mean_second)
        middle_grad_ref[...] = middle_grad
        sums_ref[0:1, :] += jnp.sum(middle_grad * branch_ref[...], axis=0, keepdims=True)
        branch_grad = (scaling_ref[0] * middle_grad).astype(BF16)
        branch_back[rows, :] = branch_grad
        sums_ref[3:4, :] += jnp.sum(branch_grad.astype(F32), axis=0, keepdims=True)
        mixed_grad_ref[...] = dot_nt(branch_grad, weight_ref[0]).astype(BF16)

    @pl.when(step == BACK_STEPS - 1)
    def _():
        width = mixed_ref.shape[1] // 3
        for part in range(3):
            columns = slice(part * width, (part + 1) * width)
            output_grad_ref[0, columns, :] = dot_tn(mixed_ref[:, columns], branch_back[...]).astype(BF16)

    for _, action in steps[-2:]:
        pl.when(step == BACK_STEPS - 1)(action)

    @pl.when(step == BACK_STEPS - 1)
    def _():
        for number in range(1, 4):
            move(number).wait()
        own.wait()


def back(back_rows, second, pre, shrink, expand, middle, branch, incoming, mixed, weights, scalings, source, token):
    rows, features = middle.shape
    third = features // 3
    by_rows = pl.BlockSpec((256, features), lambda step: (clipped(step, NORM_AT, 3), 0))

    def piece(step):
        return jnp.minimum(step, NORM_AT - 1)

    wide = jax.ShapeDtypeStruct((rows, features), F32)
    return pl.pallas_call(
        back_kernel,
        grid=(BACK_STEPS,),
        in_specs=[
            everything((rows, features)),
            everything((rows, features)),
            pl.BlockSpec((rows, third), lambda step: (0, piece(step))),
            pl.BlockSpec((third, features), lambda step: (piece(step), 0)),
            pl.BlockSpec((1, features, third), lambda step: (piece(step) // 3, 0, piece(step) % 3)),
            by_rows,
            by_rows,
            pl.BlockSpec((1, 256, features), lambda step: (clipped(step, NORM_AT, 3), 0, 0)),
            everything((rows, features)),
            pl.BlockSpec((1, features, features), lambda step: (3, 0, 0), pipeline_mode=pl.Buffered(1)),
            everything((2, 1, features)),
            ANY,
            ANY,
        ],
        out_specs=[
            pl.BlockSpec((1, features, third), lambda step: (piece(step) // 3, 0, piece(step) % 3)),
            pl.BlockSpec((1, 1, third), lambda step: (piece(step), 0, 0)),
            by_rows,
            by_rows,
            pl.BlockSpec((1, features, features), lambda step: (3, 0, 0), pipeline_mode=pl.Buffered(1)),
            everything((8, features)),
            everything((ROWS, features)),
            ANY,
        ],
        out_shape=[
            jax.ShapeDtypeStruct((4, features, features), BF16),
            jax.ShapeDtypeStruct((NORM_AT, 1, third), F32),
            wide,
            jax.ShapeDtypeStruct((rows, features), BF16),
            jax.ShapeDtypeStruct((4, features, features), BF16),
            jax.ShapeDtypeStruct((8, features), F32),
            jax.ShapeDtypeStruct((ROWS, features), F32),
            jax.ShapeDtypeStruct(token.shape, BF16),
        ],
        scratch_shapes=[
            pltpu.VMEM((rows, features), F32),
            pltpu.VMEM((rows, third), BF16),
            pltpu.VMEM((rows, features), BF16),
            pltpu.VMEM(token.shape[1:], BF16),
            pltpu.SemaphoreType.DMA((3,)),
            pltpu.SemaphoreType.DMA((3,)),
            pltpu.SemaphoreType.DMA((1,)),
            *Reduce.SCRATCH,
        ],
        compiler_params=pltpu.CompilerParams(
            collective_id=8, has_side_effects=True, vmem_limit_bytes=60 * 1024 * 1024
        ),
    )(back_rows, second, pre, shrink, expand, middle, branch, incoming, mixed, weights, scalings, source, token)


def triple_kernel(given_ref, hidden_ref, triple_ref, grad_ref, sums_ref):
    width = hidden_ref.shape[1] // 3
    for part in range(3):
        columns = slice(part * width, (part + 1) * width)
        grad_ref[0, columns, :] = dot_tn(hidden_ref[:, columns], triple_ref[...]).astype(BF16)
    sums_ref[0] = jnp.sum(triple_ref[...].astype(F32), axis=0, keepdims=True)


def triple_gradient(given, hidden, triple):
    rows, features = hidden.shape
    return pl.pallas_call(
        triple_kernel,
        grid=(3,),
        in_specs=[ANY, everything((rows, features)), pl.BlockSpec((rows, features), lambda step: (0, step))],
        out_specs=[
            pl.BlockSpec((1, features, features), lambda step: (step, 0, 0)),
            pl.BlockSpec((1, 1, features), lambda step: (step, 0, 0)),
        ],
        out_shape=[
            jax.ShapeDtypeStruct(given.shape, BF16),
            jax.ShapeDtypeStruct((3, 1, features), F32),
        ],
        input_output_aliases={0: 0},
        compiler_params=pltpu.CompilerParams(vmem_limit_bytes=56 * 1024 * 1024),
    )(given, hidden, triple)


class Shares:
    def __init__(self, here, block, pieces, target, wires, local):
        self.block, self.pieces = block, pieces
        self.copies = [
            wires.copy(
                step - 1,
                pieces.at[lax.rem(here.member + step, 4)],
                target.at[here.member],
                here.at_member(step),
            )
            for step in range(1, 4)
        ]
        self.copies.append(pltpu.make_async_copy(pieces.at[here.member], target.at[here.member], local))

    def start(self):
        for member in range(4):
            self.pieces[member, :36] = self.block[member * 36 : member * 36 + 36, :]
        for copy in self.copies:
            copy.start()

    def wait(self):
        for copy in self.copies:
            copy.wait()


def close_kernel(
    grad_ref, triple_ref, weight_ref, latent_ref, middle_ref, scale_ref, vector_ref, bias_ref, block_ref,
    total, tokens_ref, rows_ref, biases_ref, share_ref,
    pieces, triple, weight, latent, middle, token, wide, row, row_sent, row_landed, bias_sent, bias_landed,
    more_sent, more_landed, local, *scratch
):
    here = Here()
    features = latent_ref.shape[1]
    greet_all(here)
    reduce = Reduce(here, lambda member, core: grad_ref.at[member, :, core], total, *scratch)
    loads = [
        pltpu.make_async_copy(weight_ref.at[pl.ds(0, 3)], weight, local.at[0]),
        pltpu.make_async_copy(triple_ref, triple, local.at[1]),
        pltpu.make_async_copy(latent_ref, latent, local.at[2]),
        pltpu.make_async_copy(middle_ref, middle, local.at[3]),
    ]
    for copy in loads:
        copy.start()
    reduce.begin()
    bias_done = everyone(here, lambda place: bias_ref.at[place], biases_ref, bias_sent, bias_landed)
    own_bias = pltpu.make_async_copy(bias_ref.at[here.index], biases_ref.at[here.index], local.at[4])
    own_bias.start()
    wires = Wires(more_sent, more_landed)

    shares = Shares(here, block_ref, pieces, share_ref, Wires(more_sent.at[pl.ds(3, 3)], more_landed.at[pl.ds(3, 3)]), local.at[7])
    shares.start()

    def move(step):
        place = lax.rem(here.member + step, 4)
        return wires.copy(step - 1, token.at[place], tokens_ref.at[here.member], here.at_member(step))

    def compute(step):
        place = lax.rem(here.member + step, 4)
        rows = pl.ds(pl.multiple_of(place * 256, 256), 256)
        hidden_grad = dot_nt(triple[rows, :features], weight[0])
        hidden_grad += dot_nt(triple[rows, features : 2 * features], weight[1])
        hidden_grad += dot_nt(triple[rows, 2 * features :], weight[2])
        normed, inverse = norm_parts(latent[rows, :].astype(F32))
        shift = jnp.sum(hidden_grad, axis=0, keepdims=True)
        scale = jnp.sum(hidden_grad * normed, axis=0, keepdims=True)
        normed_grad = hidden_grad * (1.0 + scale_ref[...])
        mean_first = jnp.mean(normed_grad, axis=-1, keepdims=True)
        mean_second = jnp.mean(normed_grad * normed, axis=-1, keepdims=True)
        result = middle[rows, :] + inverse * (normed_grad - mean_first - normed * mean_second)
        token[place] = result.astype(BF16)
        return shift, scale

    for copy in loads:
        copy.wait()
    first, second = reduce.halves
    sums = [compute(2)]
    first.diagonal()
    sums.append(compute(1))
    first.direct()
    first.relays()
    second.diagonal()
    sums.append(compute(3))
    sums.append(compute(0))
    second.direct()
    second.relays()
    first.along_z()
    own = pltpu.make_async_copy(token.at[here.member], tokens_ref.at[here.member], local.at[5])
    own.start()
    wide[...] = vector_ref[...]
    for part in range(2):
        vector = sums[0][part] + sums[1][part] + sums[2][part] + sums[3][part]
        for tile in range(features // LANES):
            place = part * (features // LANES) + tile
            wide[place : place + 1, :] = vector[:, tile * LANES : (tile + 1) * LANES]
    row[...] = wide[...].astype(BF16)
    rows_done = everyone(here, lambda place: row, rows_ref, row_sent, row_landed)
    own_row = pltpu.make_async_copy(row, rows_ref.at[here.index], local.at[6])
    own_row.start()
    second.along_z()
    for step in (2, 1, 3):
        move(step).start()
    first.finish()
    second.finish()
    shares.wait()
    for step in range(1, 4):
        move(step).wait()
    own.wait()
    own_bias.wait()
    own_row.wait()
    rows_done()
    bias_done()


def close_down(grad, triple, weight, latents, middle_grad, scale, vectors, bias, block):
    rows, features = latents.shape
    whole = pl.BlockSpec(memory_space=pltpu.VMEM)
    return pl.pallas_call(
        close_kernel,
        in_specs=[ANY] * 5 + [whole, whole, ANY, whole],
        out_specs=[whole, ANY, ANY, ANY, ANY],
        out_shape=[
            jax.ShapeDtypeStruct((ROWS, 1152), F32),
            jax.ShapeDtypeStruct((4, rows // 4, features), BF16),
            jax.ShapeDtypeStruct((32,) + vectors.shape, BF16),
            jax.ShapeDtypeStruct(bias.shape, bias.dtype),
            jax.ShapeDtypeStruct((4, 40, 1152), F32),
        ],
        scratch_shapes=[
            pltpu.VMEM((4, 40, 1152), F32),
            pltpu.VMEM(triple.shape, BF16),
            pltpu.VMEM((3, features, features), BF16),
            pltpu.VMEM(latents.shape, BF16),
            pltpu.VMEM(latents.shape, F32),
            pltpu.VMEM((4, rows // 4, features), BF16),
            pltpu.VMEM(vectors.shape, F32),
            pltpu.VMEM(vectors.shape, BF16),
        ]
        + [pltpu.SemaphoreType.DMA((32,))] * 4
        + [pltpu.SemaphoreType.DMA((6,))] * 2
        + [pltpu.SemaphoreType.DMA((8,))]
        + list(Reduce.SCRATCH),
        compiler_params=pltpu.CompilerParams(
            collective_id=3, has_side_effects=True, vmem_limit_bytes=60 * 1024 * 1024
        ),
    )(grad, triple, weight, latents, middle_grad, scale, vectors, bias, block)


def swap_kernel(part_ref, block_ref, parts_ref, share_ref, pieces, sent, landed, more_sent, more_landed, local):
    here = Here()
    greet_all(here)
    shares = Shares(here, block_ref, pieces, share_ref, Wires(more_sent, more_landed), local.at[1])
    done = everyone(here, lambda place: part_ref.at[place // 4], parts_ref, sent, landed)
    own = pltpu.make_async_copy(part_ref.at[here.group], parts_ref.at[here.index], local.at[0])
    own.start()
    shares.start()
    shares.wait()
    own.wait()
    done()


def swap(parts, block):
    return pl.pallas_call(
        swap_kernel,
        in_specs=[ANY, pl.BlockSpec(memory_space=pltpu.VMEM)],
        out_specs=[ANY, ANY],
        out_shape=[
            jax.ShapeDtypeStruct((32,) + parts.shape[1:], parts.dtype),
            jax.ShapeDtypeStruct((4, 40, 1152), F32),
        ],
        scratch_shapes=[
            pltpu.VMEM((4, 40, 1152), F32),
            pltpu.SemaphoreType.DMA((32,)),
            pltpu.SemaphoreType.DMA((32,)),
            pltpu.SemaphoreType.DMA((3,)),
            pltpu.SemaphoreType.DMA((3,)),
            pltpu.SemaphoreType.DMA((2,)),
        ],
        compiler_params=pltpu.CompilerParams(collective_id=4, has_side_effects=True),
    )(parts, block)


def pad_lanes(values, width):
    return jnp.pad(values, ((0, 0), (0, width - values.shape[1])))


def on_device_fast(
    latents,
    condition,
    cotangent,
    modulate_weight,
    modulate_bias,
    triple_weight,
    triple_bias,
    output_weight,
    output_bias,
    expand_weight,
    expand_bias,
    shrink_weight,
    shrink_bias,
):
    micro, local, tokens, features = latents.shape
    devices = 32
    me = lax.axis_index("dp") * 4 + lax.axis_index("seq")
    hidden = expand_weight.shape[1]
    shard = jnp.stack([jnp.concatenate([triple_weight, output_weight], axis=1), expand_weight])
    shard = jnp.pad(shard, ((0, 0), (0, 12), (0, 0)))
    own_cond = lax.dynamic_index_in_dim(condition.reshape(4, features), lax.axis_index("seq"), axis=0, keepdims=False)
    biases = (modulate_bias, triple_bias, output_bias, expand_bias, shrink_bias)
    note = jnp.concatenate([own_cond, *biases]).astype(F32)
    note = jnp.pad(note, (0, 1664 - note.shape[0])).reshape(1, 1, 1664)
    notes, blocks, shrink_quad, shrink_column = introduce(note, shard, shrink_weight)
    notes = notes.reshape(32, 1664)
    cond_act = jax.nn.silu(notes[:, :features]).astype(BF16)
    cuts = []
    offset = features
    for bias in biases:
        cuts.append(notes[:, offset : offset + bias.shape[0]].reshape(-1))
        offset += bias.shape[0]
    modulate_offset, triple_offset, output_offset, expand_offset, shrink_offset = cuts
    owned = modulate_weight.shape[0]
    act_owned = lax.dynamic_slice_in_dim(cond_act, me * owned, owned, axis=1)
    parts = pad_lanes(dot_nn(act_owned, modulate_weight), 56 * LANES).reshape(4, 2, 4, 56, LANES)
    parts = jnp.swapaxes(parts, 0, 1).reshape(2, 16, 56, LANES)
    first_full, expand_column, shrink_full, parts, token_rows = open_up(
        blocks, shrink_quad, parts, latents.reshape(4, tokens, features)
    )
    first_full = first_full.reshape(4, features, features)
    modulation = jnp.sum(parts, axis=0).reshape(-1)[: 6 * features] + modulate_offset
    shift_one, scale_one, gate_one, shift_two, scale_two, gate_two = jnp.split(modulation[None, :], 6, axis=-1)

    token_rows = token_rows.reshape(4 * tokens, features)
    latent_float = token_rows.astype(F32)
    normed_one, inverse_one = norm_parts(latent_float)
    hidden_one = (normed_one * (1.0 + scale_one) + shift_one).astype(BF16)
    zero = jnp.zeros((features,), F32)
    first_bias = jnp.stack(
        [triple_offset[:features], zero, triple_offset[features:], output_offset]
    ).reshape(4, 1, features)
    output_full = first_full[3]
    (
        projected,
        mixed,
        log_total,
        branch_one,
        middle,
        hidden_two,
        pre_act,
        activated,
        expand_full,
        shrink_full,
        incoming,
    ) = forward(
        hidden_one,
        first_full,
        first_bias,
        token_rows,
        jnp.stack([gate_one, shift_two, scale_two]),
        expand_offset.reshape(4, 1, features),
        expand_column,
        shrink_full,
        shrink_column,
        cotangent.reshape(4, tokens, features),
    )
    expand_full = expand_full.reshape(4, features, features)
    shrink_full = shrink_full.reshape(hidden, features)
    output_rows, back_rows, shrink_grad, turn_sums = turn(
        activated, shrink_full, middle, incoming, gate_two, shrink_offset[None]
    )
    expand_grad, expand_offset_grad, middle_grad, mixed_grad, first_grad, back_sums, shrink_total, output = back(
        back_rows,
        hidden_two,
        pre_act,
        shrink_full,
        expand_full,
        middle,
        branch_one,
        incoming,
        mixed,
        first_full,
        jnp.stack([gate_one, scale_two]),
        shrink_grad.reshape(4, 2, 4, ROWS, features),
        output_rows,
    )
    expand_grad = expand_grad.reshape(4, 4, 2, ROWS, features)
    gate_two_grad, shrink_offset_grad = turn_sums[0], turn_sums[1]
    gate_one_grad, output_offset_grad = back_sums[0], back_sums[3]
    triple_rows, expand_block = attend_backward_reduce(projected, mixed_grad, log_total, expand_grad)
    first_grad, column_sums = triple_gradient(first_grad, hidden_one, triple_rows)
    first_grad = first_grad.reshape(4, 4, 2, ROWS, features)
    triple_offset_grad = jnp.concatenate([column_sums[0, 0], column_sums[2, 0]])
    vectors = jnp.concatenate(
        [
            jnp.zeros((2 * features,), F32),
            gate_one_grad,
            back_sums[1],
            back_sums[2],
            gate_two_grad,
            jnp.zeros((64 * LANES - 6 * features,), F32),
        ]
    ).reshape(64, LANES)
    bias_grads = jnp.concatenate(
        [
            values.reshape(devices, -1)
            for values in (triple_offset_grad, output_offset_grad, expand_offset_grad, shrink_offset_grad)
        ],
        axis=1,
    )
    bias_grads = pad_lanes(bias_grads, 1024).reshape(32, 8, LANES)
    first_block, token_grad, all_grads, bias_parts, expand_share = close_down(
        first_grad, triple_rows, first_full, token_rows, middle_grad, scale_one, vectors, bias_grads, expand_block
    )
    all_grads = all_grads.reshape(32, 8192)[:, : 6 * features]
    modulate_total = dot_tn(act_owned, all_grads)
    width = modulate_bias.shape[0]
    modulate_offset_total = jnp.sum(
        lax.dynamic_slice_in_dim(all_grads, me * width, width, axis=1).astype(F32), axis=0
    )
    cond_back = dot_nt(all_grads, modulate_weight)
    cond_back = jnp.pad(cond_back.reshape(8, 4, owned), ((0, 0), (0, 4), (0, LANES - owned)))
    cond_back, first_share = swap(cond_back, first_block)
    cond_back = cond_back[:, :4, :owned]
    cond_back = jnp.swapaxes(cond_back, 0, 1).reshape(condition.shape)
    cond_float = condition.astype(F32)
    sigmoid_cond = jax.nn.sigmoid(cond_float)
    condition_gradient = cond_back * (sigmoid_cond * (1.0 + cond_float * (1.0 - sigmoid_cond)))
    bias_total = jnp.sum(bias_parts.reshape(32, 1024), axis=0)
    bias_cuts = []
    offset = 0
    for bias in biases[1:]:
        bias_cuts.append(bias_total[offset : offset + bias.shape[0]])
        offset += bias.shape[0]
    first_share = first_share[:, :owned]
    expand_total = jnp.swapaxes(expand_share[:, :owned], 0, 1).reshape(expand_weight.shape)
    return (
        output.reshape(latents.shape),
        token_grad.reshape(latents.shape).astype(F32),
        condition_gradient,
        modulate_total,
        modulate_offset_total,
        jnp.concatenate([first_share[0], first_share[1], first_share[2]], axis=1),
        bias_cuts[0],
        first_share[3],
        bias_cuts[1],
        expand_total,
        bias_cuts[2],
        shrink_total,
        bias_cuts[3],
    )


def solution(mesh):
    tokens = P(None, "dp", "seq", None)
    conditions = P(None, "dp", None)
    weight = P(AXES, None)
    bias = P(AXES)
    parameters = (weight, bias) * 5
    fast = mesh.shape["dp"] == 8 and mesh.shape["seq"] == 4
    return jax.shard_map(
        on_device_fast if fast else on_device,
        mesh=mesh,
        in_specs=(tokens, conditions, tokens) + parameters,
        out_specs=(tokens, tokens, conditions) + parameters,
        check_vma=False,
    )
```
